32 devices in a mesh: seq: 8 (over z, x), head: 4 (over y, core).
Axes of the slice: x: 2, y: 2, z: 4, core: 2. Of those that a mesh axis runs over, the one named last changes fastest.
Arguments:
- image_input_rows: bfloat16 [1024, 3072], P(('seq', 'head')), may hold values from -6 to 6
- adapter_down_weight: bfloat16 [3072, 64], replicated, may hold values from -0.109375 to 0.109375
- adapter_up_weight: bfloat16 [64, 1536], replicated, may hold values from -0.75 to 0.75
- image_query_rows: bfloat16 [1024, 1536], P(('seq', 'head')), may hold values from -72 to 72
- image_key_rows: bfloat16 [1024, 1536], P(('seq', 'head')), may hold values from -4 to 4
- image_value_codes: int32 [1024, 1536], P(('seq', 'head')), may hold values from -127 to 127
- value_fraction: bfloat16 [1024, 1536], P(('seq', 'head')), may hold values from -0.5 to 0.5
- value_step_sizes: float32 [8, 12], replicated, may hold values from 0.004 to 0.03
- timestep_group: int32 [1000], replicated, may hold values from 0 to 7
- timestep: int32 [1], replicated, may hold values from 0 to 999
- image_output_grad: bfloat16 [1024, 1536], P(('seq', 'head')), may hold values from -1960 to 1960
- text_query_rows: bfloat16 [512, 1536], P(None, 'head'), may hold values from -4 to 4
- text_key_rows: bfloat16 [512, 1536], P(None, 'head'), may hold values from -4 to 4
- text_value_rows: bfloat16 [512, 1536], P(None, 'head'), may hold values from -4 to 4
- text_output_grad: bfloat16 [512, 1536], P(None, 'head'), may hold values from -512 to 512
Outputs:
- dq_img: bfloat16 [1024, 1536], P(('seq', 'head'))
- dk_img: bfloat16 [1024, 1536], P(('seq', 'head'))
- image_value_grad: bfloat16 [1024, 1536], P(('seq', 'head'))
- dq_txt: bfloat16 [512, 1536], P('seq', 'head')
- dk_txt: bfloat16 [512, 1536], P('seq', 'head')
- dv_txt: bfloat16 [512, 1536], P('seq', 'head')
- grad_down: float32 [3072, 64], replicated
- grad_up: float32 [64, 1536], replicated
- grad_steps: float32 [8, 12], replicated
The draws below stay inside these ranges and needn't reach their ends.
All inputs are finite; a program needn't handle non-finite values.
Results may differ from the reference program's by a relative error of at most 0.013.
Values may be sent and summed in bfloat16 or wider, within the bound.
A program may use at most 128 MiB of HBM per device.

```python
import math
import jax
import jax.numpy as jnp
from jax import lax

MODEL_WIDTH = 3072
HEAD_SIZE = 128
HEAD_TOTAL = 12
ADAPTER_RANK = 64
TXT = 512
QMAX = 127
SLOTS = 8
TSTEPS = 1000
IMG = 1024


def shared_keys(key):
    return jax.random.truncated_normal(key, -3.0, 3.0, (IMG, HEAD_TOTAL * HEAD_SIZE), jnp.float32)


def draw_image_key_rows(key, part):
    shared = shared_keys(key)
    return shared.astype(jnp.bfloat16)


def draw_image_query_rows(key, part):
    key = jax.random.fold_in(key, 23)
    first_key = jax.random.fold_in(key, 0)
    drawn = jnp.clip(jax.random.normal(first_key, (IMG, HEAD_TOTAL * HEAD_SIZE), jnp.float32), -4.0, 4.0)
    return drawn.astype(jnp.bfloat16)


def draw_image_output_grad(key, part):
    key = jax.random.fold_in(key, 37)
    rising = jnp.arange(IMG, dtype=jnp.float32)[:, None] / IMG
    drawn = jnp.clip(jax.random.normal(key, (IMG, HEAD_TOTAL * HEAD_SIZE), jnp.float32), -4.0, 4.0)
    return (128.0 * (1.0 + 2.0 * rising) * drawn).astype(jnp.bfloat16)


def with_ends(entries, rng, low, largest):
    place = [jax.random.randint(jax.random.fold_in(rng, axis), (), 0, length) for axis, length in enumerate(entries.shape)]
    longest = entries.shape.index(max(entries.shape))
    next_to = place[:longest] + [(place[longest] + 1) % entries.shape[longest]] + place[longest + 1:]
    return entries.at[tuple(place)].set(low).at[tuple(next_to)].set(largest)


def shard_levels(key, extent, cuts, smallest, top_value):
    loudness, own = 1.0, jax.random.fold_in(key, 6)
    for dim, blocks in cuts:
        heights = jnp.exp(jax.random.uniform(jax.random.fold_in(own, dim), (blocks,), jnp.float32, smallest / len(cuts), top_value / len(cuts)))
        loudness = loudness * jnp.repeat(heights, extent[dim] // blocks).reshape([-1 if axis == dim else 1 for axis in range(len(extent))])
    return loudness


def bell_draw(rng, dims, spread, limit, shards=(), kind=jnp.bfloat16):
    level = shard_levels(rng, dims, shards, -0.22, 0.18) if shards else 1.0
    values = jax.random.normal(rng, dims, jnp.float32) * spread * level
    return jnp.minimum(jnp.maximum(values, -limit), limit).astype(kind)


def setup_inputs(seed: int = 0) -> dict:
    splits = jax.random.split(jax.random.key(seed), 16)
    return {
        "image_input_rows": bell_draw(splits[0], (IMG, MODEL_WIDTH), 1.0, 6.0, ((0, 32),)),
        "adapter_down_weight": bell_draw(splits[1], (MODEL_WIDTH, ADAPTER_RANK), MODEL_WIDTH ** -0.5, 0.109375),
        "adapter_up_weight": bell_draw(splits[2], (ADAPTER_RANK, HEAD_TOTAL * HEAD_SIZE), ADAPTER_RANK ** -0.5, 0.75),
        "image_query_rows": draw_image_query_rows(jax.random.fold_in(splits[15], 71), 0),
        "image_key_rows": draw_image_key_rows(jax.random.fold_in(splits[15], 71), 0),
        "image_value_codes": with_ends(jax.random.randint(splits[5], (IMG, HEAD_TOTAL * HEAD_SIZE), -QMAX, QMAX + 1), jax.random.fold_in(splits[5], 1), -QMAX, QMAX).astype(jnp.int32),
        "value_fraction": jnp.clip(jax.random.uniform(splits[6], (IMG, HEAD_TOTAL * HEAD_SIZE), jnp.float32, -0.5, 0.5) * shard_levels(splits[6], (IMG, HEAD_TOTAL * HEAD_SIZE), ((0, 32),), -0.4, 0.0), -0.5, 0.5).astype(jnp.bfloat16),
        "value_step_sizes": jnp.clip(jnp.exp(jax.random.uniform(splits[7], (SLOTS, HEAD_TOTAL), jnp.float32, math.log(0.004), math.log(0.03))), 0.004, 0.03),
        "timestep_group": with_ends(jax.random.randint(splits[8], (TSTEPS,), 0, SLOTS), jax.random.fold_in(splits[8], 1), 0, SLOTS - 1).astype(jnp.int32),
        "timestep": jax.random.randint(splits[9], (1,), 0, TSTEPS).astype(jnp.int32),
        "image_output_grad": draw_image_output_grad(jax.random.fold_in(splits[15], 71), 0),
        "text_query_rows": bell_draw(splits[11], (TXT, HEAD_TOTAL * HEAD_SIZE), 1.0, 4.0, ((1, 4),)),
        "text_key_rows": bell_draw(splits[12], (TXT, HEAD_TOTAL * HEAD_SIZE), 1.0, 4.0, ((1, 4),)),
        "text_value_rows": bell_draw(splits[13], (TXT, HEAD_TOTAL * HEAD_SIZE), 1.0, 4.0, ((1, 4),)),
        "text_output_grad": bell_draw(splits[14], (TXT, HEAD_TOTAL * HEAD_SIZE), 128.0, 512.0, ((1, 4),)),
    }


unscale = 0.0078125


def head_major(rows):
    return rows.reshape(rows.shape[0], HEAD_TOTAL, HEAD_SIZE).transpose(1, 0, 2)


def token_major(heads):
    return heads.transpose(1, 0, 2).reshape(heads.shape[1], HEAD_TOTAL * HEAD_SIZE)


def reference(image_input_rows, adapter_down_weight, adapter_up_weight, image_query_rows, image_key_rows, image_value_codes, value_fraction, value_step_sizes, timestep_group, timestep, image_output_grad, text_query_rows, text_key_rows, text_value_rows, text_output_grad):
    slot_index = timestep_group[timestep[0]]
    step_row = value_step_sizes[slot_index]
    code_values = image_value_codes.astype(jnp.float32)
    v_img = (code_values * jnp.repeat(step_row, HEAD_SIZE)[None, :]).astype(jnp.bfloat16)
    queries = head_major(jnp.concatenate([image_query_rows, text_query_rows], axis=0))
    key_rows = head_major(jnp.concatenate([image_key_rows, text_key_rows], axis=0))
    value_rows = head_major(jnp.concatenate([v_img, text_value_rows], axis=0))
    out_grads = head_major(jnp.concatenate([image_output_grad, text_output_grad], axis=0))
    total_rows = IMG + TXT
    block_rows = math.gcd(total_rows, 512)
    scale = HEAD_SIZE ** -0.5

    def one_head(operands):
        query_head, key_head, value_head, grad_head = operands
        query_blocks = query_head.reshape(total_rows // block_rows, block_rows, HEAD_SIZE)
        grad_blocks = grad_head.reshape(total_rows // block_rows, block_rows, HEAD_SIZE)

        def one_block(carried, blocks):
            key_grad, value_grad = carried
            query_block, grad_block = blocks
            scores = jnp.dot(query_block, key_head.T, preferred_element_type=jnp.float32) * scale
            row_max = jnp.max(scores, axis=1, keepdims=True)
            log_sums = row_max + jnp.log(jnp.sum(jnp.exp(scores - row_max), axis=1, keepdims=True))
            probs = jnp.exp(scores - log_sums)
            dprobs = jnp.dot(grad_block, value_head.T, preferred_element_type=jnp.float32)
            deltas = jnp.sum(probs * dprobs, axis=1, keepdims=True)
            dscores = (probs * (dprobs - deltas)).astype(jnp.bfloat16)
            query_grad = jnp.dot(dscores, key_head, preferred_element_type=jnp.float32) * scale
            key_grad = key_grad + jnp.dot(dscores.T, query_block, preferred_element_type=jnp.float32) * scale
            value_grad = value_grad + jnp.dot(probs.astype(jnp.bfloat16).T, grad_block, preferred_element_type=jnp.float32)
            return (key_grad, value_grad), query_grad

        empty = jnp.zeros((total_rows, HEAD_SIZE), jnp.float32)
        (key_grad, value_grad), query_grad = lax.scan(one_block, (empty, empty), (query_blocks, grad_blocks))
        return query_grad.reshape(total_rows, HEAD_SIZE), key_grad, value_grad

    query_grad, key_grad, value_grad = lax.map(one_head, (queries, key_rows, value_rows, out_grads))
    query_grad = token_major(query_grad).astype(jnp.bfloat16)
    key_grad = token_major(key_grad).astype(jnp.bfloat16)
    value_grad = token_major(value_grad).astype(jnp.bfloat16)
    dv_quant = value_grad[:IMG]
    inside = jnp.abs(image_value_codes) < QMAX
    lsq_term = jnp.where(inside, -value_fraction.astype(jnp.float32), code_values)
    image_value_grad = jnp.where(inside, dv_quant, jnp.zeros_like(dv_quant))
    head_sums = jnp.sum((dv_quant.astype(jnp.float32) * lsq_term).reshape(IMG, HEAD_TOTAL, HEAD_SIZE), axis=(0, 2))
    slot_rows = jnp.arange(SLOTS, dtype=jnp.int32) == slot_index
    grad_steps = jnp.where(slot_rows[:, None], head_sums[None, :], 0.0) * (QMAX ** -0.5 * unscale)
    lowrank_gradient = jnp.dot(image_value_grad, adapter_up_weight.T, preferred_element_type=jnp.float32).astype(jnp.bfloat16)
    grad_down = jnp.dot(image_input_rows.T, lowrank_gradient, preferred_element_type=jnp.float32) * unscale
    lowrank_input = jnp.dot(image_input_rows, adapter_down_weight, preferred_element_type=jnp.float32).astype(jnp.bfloat16)
    grad_up = jnp.dot(lowrank_input.T, image_value_grad, preferred_element_type=jnp.float32) * unscale
    return (query_grad[:IMG], key_grad[:IMG], image_value_grad, query_grad[IMG:], key_grad[IMG:], value_grad[IMG:], grad_down, grad_up, grad_steps)
```

```python
import functools
import math

import jax
import jax.numpy as jnp
from jax import lax
from jax.experimental import pallas as pl
from jax.experimental.pallas import tpu as pltpu
from jax.sharding import PartitionSpec as P

HEAD_SIZE = 128
QMAX = 127


unscale = 0.0078125


def split_heads(rows):
    return rows.reshape(rows.shape[0], rows.shape[1] // HEAD_SIZE, HEAD_SIZE)


def join_heads(heads):
    return heads.reshape(heads.shape[0], heads.shape[1] * heads.shape[2])


def head_scores(queries, key_rows):
    return jnp.einsum(
        "qhd,khd->hqk", queries, key_rows, preferred_element_type=jnp.float32
    ) * HEAD_SIZE ** (-0.5)


def over_keys(step_fn, initial, key_rows, value_rows):
    block_rows = math.gcd(key_rows.shape[0], 2048)

    def over_one_turn(turn_index, carried):
        key_block = lax.dynamic_slice_in_dim(key_rows, turn_index * block_rows, block_rows, 0)
        value_block = lax.dynamic_slice_in_dim(value_rows, turn_index * block_rows, block_rows, 0)
        return step_fn(carried, key_block, value_block)

    return lax.fori_loop(0, key_rows.shape[0] // block_rows, over_one_turn, initial)


def key_terms(carried, queries, grads, log_rows, delta_rows, own_keys, own_values):
    key_grad, value_grad = carried
    probs = jnp.exp(head_scores(queries, own_keys) - log_rows.T[:, :, None])
    dprobs = jnp.einsum("qhd,khd->hqk", grads, own_values, preferred_element_type=jnp.float32)
    dscores = (probs * (dprobs - delta_rows.T[:, :, None])).astype(jnp.bfloat16)
    value_grad = value_grad + jnp.einsum(
        "hqk,qhd->khd", probs.astype(jnp.bfloat16), grads, preferred_element_type=jnp.float32
    )
    key_grad = key_grad + jnp.einsum(
        "hqk,qhd->khd", dscores, queries, preferred_element_type=jnp.float32
    ) * HEAD_SIZE ** (-0.5)
    return (key_grad, value_grad)


def on_device(
    image_input_rows,
    adapter_down_weight,
    adapter_up_weight,
    image_query_rows,
    image_key_rows,
    image_value_codes,
    value_fraction,
    value_step_sizes,
    timestep_group,
    timestep,
    image_output_grad,
    text_query_rows,
    text_key_rows,
    text_value_rows,
    text_output_grad,
):
    slot_index = jnp.sum(
        jnp.where(
            jnp.arange(timestep_group.shape[0], dtype=jnp.int32) == timestep[0], timestep_group, 0
        )
    )
    slot_rows = jnp.arange(value_step_sizes.shape[0], dtype=jnp.int32) == slot_index
    step_row = jnp.sum(jnp.where(slot_rows[:, None], value_step_sizes, 0.0), axis=0)
    code_values = image_value_codes.astype(jnp.float32)
    v_dequant = (code_values * jnp.repeat(step_row, HEAD_SIZE)[None, :]).astype(jnp.bfloat16)
    inside = jnp.abs(image_value_codes) < QMAX
    lsq_term = jnp.where(inside, -value_fraction.astype(jnp.float32), code_values)
    query_img, key_img, value_img, grad_img = (
        lax.all_to_all(image_query_rows, "head", split_axis=1, concat_axis=0, tiled=True),
        lax.all_to_all(image_key_rows, "head", split_axis=1, concat_axis=0, tiled=True),
        lax.all_to_all(v_dequant, "head", split_axis=1, concat_axis=0, tiled=True),
        lax.all_to_all(image_output_grad, "head", split_axis=1, concat_axis=0, tiled=True),
    )
    share_rows = text_query_rows.shape[0] // lax.axis_size("seq")
    first_row = lax.axis_index("seq") * share_rows

    def own_rows(table):
        return lax.dynamic_slice_in_dim(table, first_row, share_rows, 0)

    image_rows = query_img.shape[0]
    query_local = jnp.concatenate([query_img, own_rows(text_query_rows)], axis=0)
    grad_local = jnp.concatenate([grad_img, own_rows(text_output_grad)], axis=0)
    query_split = split_heads(query_local)
    grad_split = split_heads(grad_local)
    local_count = query_split.shape[0]
    head_count = query_split.shape[1]
    key_image, value_image = (
        lax.all_gather(key_img, "seq", axis=0, tiled=True),
        lax.all_gather(value_img, "seq", axis=0, tiled=True),
    )
    text_keys = split_heads(text_key_rows)
    text_values = split_heads(text_value_rows)
    key_sets = ((split_heads(key_image), split_heads(value_image)), (text_keys, text_values))

    def stat_turn(carried, key_block, value_block):
        row_max, running, weighted = carried
        scores = head_scores(query_split, key_block)
        dprobs = jnp.einsum(
            "qhd,khd->hqk", grad_split, value_block, preferred_element_type=jnp.float32
        )
        new_max = jnp.maximum(row_max, jnp.max(scores, axis=2, keepdims=True))
        factor = jnp.exp(row_max - new_max)
        expo = jnp.exp(scores - new_max)
        running = running * factor + jnp.sum(expo, axis=2, keepdims=True)
        weighted = weighted * factor + jnp.sum(expo * dprobs, axis=2, keepdims=True)
        return (new_max, running, weighted)

    row_stats = (
        jnp.full((head_count, local_count, 1), -jnp.inf, jnp.float32),
        jnp.zeros((head_count, local_count, 1), jnp.float32),
        jnp.zeros((head_count, local_count, 1), jnp.float32),
    )
    for key_rows, value_rows in key_sets:
        row_stats = over_keys(stat_turn, row_stats, key_rows, value_rows)
    log_sums = row_stats[0] + jnp.log(row_stats[1])
    deltas = row_stats[2] / row_stats[1]

    def query_turn(running, key_block, value_block):
        probs = jnp.exp(head_scores(query_split, key_block) - log_sums)
        dprobs = jnp.einsum(
            "qhd,khd->hqk", grad_split, value_block, preferred_element_type=jnp.float32
        )
        dscores = (probs * (dprobs - deltas)).astype(jnp.bfloat16)
        return running + jnp.einsum(
            "hqk,khd->qhd", dscores, key_block, preferred_element_type=jnp.float32
        ) * HEAD_SIZE ** (-0.5)

    query_grad = jnp.zeros((local_count, head_count, HEAD_SIZE), jnp.float32)
    for key_rows, value_rows in key_sets:
        query_grad = over_keys(query_turn, query_grad, key_rows, value_rows)
    query_grad = join_heads(query_grad).astype(jnp.bfloat16)
    log_rows = log_sums[:, :, 0].T
    delta_rows = deltas[:, :, 0].T
    own_keys = split_heads(key_img)
    own_values = split_heads(value_img)
    empty = jnp.zeros(own_keys.shape, jnp.float32)
    query_rows = lax.all_gather(query_local.astype(jnp.float32), "seq", axis=0, tiled=True).astype(
        jnp.bfloat16
    )
    grad_rows = lax.all_gather(grad_local.astype(jnp.float32), "seq", axis=0, tiled=True).astype(
        jnp.bfloat16
    )
    log_part = lax.all_gather(log_rows, "seq", axis=0, tiled=True)
    delta_part = lax.all_gather(delta_rows, "seq", axis=0, tiled=True)
    piece_rows = query_rows.shape[0]
    block_rows = piece_rows if piece_rows <= 2048 else math.gcd(piece_rows, 2048)

    def fold_one_turn(turn_index, running):

        def rows_of(table):
            return lax.dynamic_slice_in_dim(table, turn_index * block_rows, block_rows, 0)

        return key_terms(
            running,
            split_heads(rows_of(query_rows)),
            split_heads(rows_of(grad_rows)),
            rows_of(log_part),
            rows_of(delta_part),
            own_keys,
            own_values,
        )

    key_grad, value_grad = lax.fori_loop(0, piece_rows // block_rows, fold_one_turn, (empty, empty))
    key_grad = join_heads(key_grad).astype(jnp.bfloat16)
    value_grad = join_heads(value_grad).astype(jnp.bfloat16)
    text_empty = jnp.zeros(text_keys.shape, jnp.float32)
    text_key, text_value = key_terms(
        (text_empty, text_empty),
        query_split,
        grad_split,
        log_rows,
        delta_rows,
        text_keys,
        text_values,
    )
    text_key, text_value = (
        lax.psum_scatter(join_heads(text_key), "seq", scatter_dimension=0, tiled=True),
        lax.psum_scatter(join_heads(text_value), "seq", scatter_dimension=0, tiled=True),
    )
    dk_txt = text_key.astype(jnp.bfloat16)
    dv_txt = text_value.astype(jnp.bfloat16)
    dq_txt = query_grad[image_rows:]
    dq_heads = query_grad[:image_rows]
    dq_img, dk_img, dv_quant = (
        lax.all_to_all(dq_heads, "head", split_axis=0, concat_axis=1, tiled=True),
        lax.all_to_all(key_grad, "head", split_axis=0, concat_axis=1, tiled=True),
        lax.all_to_all(value_grad, "head", split_axis=0, concat_axis=1, tiled=True),
    )
    image_value_grad = jnp.where(inside, dv_quant, jnp.zeros_like(dv_quant))
    lowrank_gradient = jnp.einsum(
        "vg,zg->vz", image_value_grad, adapter_up_weight, preferred_element_type=jnp.float32
    ).astype(jnp.bfloat16)
    part_down = jnp.einsum(
        "td,tr->dr", image_input_rows, lowrank_gradient, preferred_element_type=jnp.float32
    )
    lowrank_input = jnp.dot(
        image_input_rows, adapter_down_weight, preferred_element_type=jnp.float32
    ).astype(jnp.bfloat16)
    part_up = jnp.einsum(
        "tr,tw->rw", lowrank_input, image_value_grad, preferred_element_type=jnp.float32
    )
    token_rows = dv_quant.shape[0]
    token_terms = (dv_quant.astype(jnp.float32) * lsq_term).reshape(
        token_rows, value_step_sizes.shape[1], HEAD_SIZE
    )
    total_down, total_up, step_sums = lax.psum(
        (part_down, part_up, jnp.sum(token_terms, axis=(0, 2))), ("seq", "head")
    )
    grad_steps = jnp.where(slot_rows[:, None], step_sums[None, :], 0.0) * (QMAX ** (-0.5) * unscale)
    return (
        dq_img,
        dk_img,
        image_value_grad,
        dq_txt,
        dk_txt,
        dv_txt,
        total_down * unscale,
        total_up * unscale,
        grad_steps,
    )


MESH = pl.DeviceIdType.MESH
BF = jnp.bfloat16
F32 = jnp.float32
NT = (((1,), (1,)), ((), ()))
NN = (((1,), (0,)), ((), ()))


def dot(left, right, dims=NN):
    return lax.dot_general(left, right, dims, preferred_element_type=F32)


def attention_kernel(
    seq,
    head,
    q_ref,
    k_ref,
    code_ref,
    do_ref,
    tq_ref,
    tk_ref,
    tv_ref,
    tdo_ref,
    step_ref,
    dq_ref,
    dk_ref,
    dv_ref,
    dqt_ref,
    dkt_ref,
    dvt_ref,
    stage,
    recv,
    kv2,
    tkv,
    tqd,
    kall,
    ktr,
    vall,
    qall,
    doall,
    dqall,
    dkacc,
    dvacc,
    xo,
    xi,
    to,
    ti,
    ost,
    ret,
    tfin,
    rett,
    s1,
    r1,
    s2,
    r2,
    st,
    rt,
    s3,
    r3,
    s4,
    r4,
    s5,
    r5,
):
    rows = q_ref.shape[0]
    heads = q_ref.shape[1] // HEAD_SIZE
    text = tq_ref.shape[0]
    half = text // 2
    planes = head // 2
    peers = seq * planes
    group = tq_ref.shape[1] // HEAD_SIZE
    pair = 2 * group
    first = (seq - pair) // 2
    image = peers * rows
    share = text // seq
    scale = HEAD_SIZE ** (-0.5)

    s = lax.axis_index("seq")
    g = lax.axis_index("head")
    c = lax.rem(g, 2)
    y = g // 2
    me = s * planes + y
    partner = (s, g + 1 - 2 * c)
    slot = s - first
    is_head = jnp.logical_and(slot >= 0, slot < pair)
    mine = y * pair + slot
    holds_text = jnp.logical_and(is_head, slot // group == c)
    takes_text = jnp.logical_and(is_head, slot // group != c)
    lane_block = lax.rem(slot, group)

    def peer(p):
        return (p // planes, (p % planes) * 2 + c)

    def home(h):
        return (first + h % pair, (h // pair) * 2 + c)

    def home_peer(h):
        return (first + h % pair) * planes + h // pair

    def send(src, dst, ssem, rsem, to_id):
        return pltpu.make_async_remote_copy(
            src_ref=src, dst_ref=dst, send_sem=ssem, recv_sem=rsem, device_id=to_id, device_id_type=MESH
        )

    barrier = pltpu.get_barrier_semaphore()
    for p in range(peers):

        @pl.when(me != p)
        def _():
            pl.semaphore_signal(barrier, inc=1, device_id=peer(p), device_id_type=MESH)

    pl.semaphore_signal(barrier, inc=1, device_id=partner, device_id_type=MESH)

    for h in range(heads):
        cols = slice(h * HEAD_SIZE, (h + 1) * HEAD_SIZE)
        stage[h, 0:rows] = k_ref[:, cols]
        stage[h, rows : 2 * rows] = code_ref[:, cols].astype(F32).astype(BF)
        stage[h, 2 * rows : 3 * rows] = q_ref[:, cols]
        stage[h, 3 * rows : 4 * rows] = do_ref[:, cols]

    pl.semaphore_wait(barrier, peers)

    def first_send(h):
        return send(stage.at[h], recv.at[me], s1.at[h], r1.at[me], home(h))

    def first_recv(p):
        return send(stage.at[0], recv.at[p], s1.at[0], r1.at[p], partner)

    for h in range(heads):

        @pl.when(me != home_peer(h))
        def _():
            first_send(h).start()

    def text_copies():
        cols = pl.ds(pl.multiple_of(lane_block * HEAD_SIZE, HEAD_SIZE), HEAD_SIZE)
        low = pl.ds(half, half)
        return (
            send(tk_ref.at[:, cols], tkv.at[0], st.at[0], rt.at[0], partner),
            send(tv_ref.at[:, cols], tkv.at[1], st.at[1], rt.at[1], partner),
            send(tq_ref.at[low, cols], tqd.at[0], st.at[2], rt.at[2], partner),
            send(tdo_ref.at[low, cols], tqd.at[1], st.at[3], rt.at[3], partner),
        )

    @pl.when(holds_text)
    def _():
        for copy in text_copies():
            copy.start()
        cols = pl.ds(pl.multiple_of(lane_block * HEAD_SIZE, HEAD_SIZE), HEAD_SIZE)
        kall[2 * image : 2 * image + text] = tk_ref[:, cols]
        vall[2 * image : 2 * image + text] = tv_ref[:, cols]
        qall[image : image + half] = tq_ref[0:half, cols]
        doall[image : image + half] = tdo_ref[0:half, cols]

    @pl.when(is_head)
    def _():
        recv[pl.ds(me, 1)] = stage[pl.ds(mine, 1)]
        for p in range(peers):

            @pl.when(me != p)
            def _():
                first_recv(p).wait_recv()

        swap = send(recv.at[:, pl.ds(0, 2 * rows)], kv2, s2.at[0], r2.at[0], partner)
        swap.start()
        step = step_ref[:, pl.ds(pl.multiple_of(mine * HEAD_SIZE, HEAD_SIZE), HEAD_SIZE)]

        def dequant(codes):
            return (codes.reshape(image, HEAD_SIZE).astype(F32) * step).astype(BF)

        kall[0:image] = recv[:, 0:rows].reshape(image, HEAD_SIZE)
        vall[0:image] = dequant(recv[:, rows : 2 * rows])
        qall[0:image] = recv[:, 2 * rows : 3 * rows].reshape(image, HEAD_SIZE)
        doall[0:image] = recv[:, 3 * rows : 4 * rows].reshape(image, HEAD_SIZE)

        @pl.when(takes_text)
        def _():
            for copy in text_copies():
                copy.wait_recv()
            kall[2 * image : 2 * image + text] = tkv[0]
            vall[2 * image : 2 * image + text] = tkv[1]
            qall[image : image + half] = tqd[0]
            doall[image : image + half] = tqd[1]

        swap.wait_recv()
        kall[image : 2 * image] = kv2[:, 0:rows].reshape(image, HEAD_SIZE)
        vall[image : 2 * image] = dequant(kv2[:, rows : 2 * rows])
        ktr[...] = kall[...].T
        dkacc[...] = jnp.zeros_like(dkacc)
        dvacc[...] = jnp.zeros_like(dvacc)

        def query_block(index, carried):
            at = pl.ds(pl.multiple_of(index * half, half), half)
            queries, grads = qall[at], doall[at]
            scores = dot(kall[...], queries, NT) * scale
            expo = jnp.exp(scores - jnp.max(scores, axis=0, keepdims=True))
            probs = expo * (1.0 / jnp.sum(expo, axis=0, keepdims=True))
            dvacc[...] += dot(probs.astype(BF), grads)
            dprobs = dot(vall[...], grads, NT)
            deltas = jnp.sum(probs * dprobs, axis=0, keepdims=True)
            dscores = (probs * (dprobs - deltas)).astype(BF)
            dkacc[...] += dot(dscores, queries)
            dqall[at] = (dot(ktr[...], dscores).T * scale).astype(BF)
            return carried

        lax.fori_loop(0, (image + half) // half, query_block, 0)
        xo[0] = (dkacc[image : 2 * image] * scale).astype(BF)
        xo[1] = dvacc[image : 2 * image].astype(BF)
        trade = send(xo, xi, s3.at[0], r3.at[0], partner)
        trade.start()
        text_trade = send(to, ti, s3.at[1], r3.at[1], partner)

        @pl.when(takes_text)
        def _():
            to[0:text] = (dkacc[2 * image : 2 * image + text] * scale).astype(BF)
            to[text : 2 * text] = dvacc[2 * image : 2 * image + text].astype(BF)
            to[2 * text : 2 * text + half] = dqall[image : image + half]
            text_trade.start()

        ost[:, 0:rows] = dqall[0:image].reshape(peers, rows, HEAD_SIZE)
        trade.wait_recv()
        ost[:, rows : 2 * rows] = (
            (dkacc[0:image] * scale + xi[0].astype(F32)).astype(BF).reshape(peers, rows, HEAD_SIZE)
        )
        ost[:, 2 * rows : 3 * rows] = (
            (dvacc[0:image] + xi[1].astype(F32)).astype(BF).reshape(peers, rows, HEAD_SIZE)
        )
        for p in range(peers):

            @pl.when(me != p)
            def _():
                send(ost.at[p], ret.at[mine], s4.at[p], r4.at[mine], peer(p)).start()

        ret[pl.ds(mine, 1)] = ost[pl.ds(me, 1)]

        @pl.when(holds_text)
        def _():
            text_trade.wait_recv()
            full = (seq, share, HEAD_SIZE)
            tfin[0 : seq // 2, 0] = dqall[image : image + half].reshape(seq // 2, share, HEAD_SIZE)
            tfin[seq // 2 : seq, 0] = ti[2 * text : 2 * text + half].reshape(seq // 2, share, HEAD_SIZE)
            tfin[:, 1] = (
                (dkacc[2 * image : 2 * image + text] * scale + ti[0:text].astype(F32)).astype(BF).reshape(full)
            )
            tfin[:, 2] = (
                (dvacc[2 * image : 2 * image + text] + ti[text : 2 * text].astype(F32)).astype(BF).reshape(full)
            )
            for other in range(seq):

                @pl.when(s != other)
                def _():
                    send(
                        tfin.at[other], rett.at[lane_block], s5.at[other], r5.at[lane_block], (other, g)
                    ).start()

            rett[pl.ds(lane_block, 1)] = tfin[pl.ds(s, 1)]

    for j in range(group):

        @pl.when(s != first + c * group + j)
        def _():
            send(tfin.at[0], rett.at[j], s5.at[0], r5.at[j], partner).wait_recv()

        cols = slice(j * HEAD_SIZE, (j + 1) * HEAD_SIZE)
        dqt_ref[:, cols] = rett[j, 0]
        dkt_ref[:, cols] = rett[j, 1]
        dvt_ref[:, cols] = rett[j, 2]

    for h in range(heads):

        @pl.when(me != home_peer(h))
        def _():
            send(ost.at[0], ret.at[h], s4.at[0], r4.at[h], partner).wait_recv()

        cols = slice(h * HEAD_SIZE, (h + 1) * HEAD_SIZE)
        dq_ref[:, cols] = ret[h, 0:rows]
        dk_ref[:, cols] = ret[h, rows : 2 * rows]
        dv_ref[:, cols] = ret[h, 2 * rows : 3 * rows]

    for h in range(heads):

        @pl.when(me != home_peer(h))
        def _():
            first_send(h).wait_send()

    @pl.when(is_head)
    def _():
        send(recv.at[:, pl.ds(0, 2 * rows)], kv2, s2.at[0], r2.at[0], partner).wait_send()
        send(xo, xi, s3.at[0], r3.at[0], partner).wait_send()
        for p in range(peers):

            @pl.when(me != p)
            def _():
                send(ost.at[p], ret.at[mine], s4.at[p], r4.at[mine], peer(p)).wait_send()

    @pl.when(takes_text)
    def _():
        send(to, ti, s3.at[1], r3.at[1], partner).wait_send()

    @pl.when(holds_text)
    def _():
        for copy in text_copies():
            copy.wait_send()
        for other in range(seq):

            @pl.when(s != other)
            def _():
                send(
                    tfin.at[other], rett.at[lane_block], s5.at[other], r5.at[lane_block], (other, g)
                ).wait_send()


def whole_heads(
    seq,
    head,
    image_input_rows,
    adapter_down_weight,
    adapter_up_weight,
    image_query_rows,
    image_key_rows,
    image_value_codes,
    value_fraction,
    value_step_sizes,
    timestep_group,
    timestep,
    image_output_grad,
    text_query_rows,
    text_key_rows,
    text_value_rows,
    text_output_grad,
):
    rows, width = image_query_rows.shape
    text, text_width = text_query_rows.shape
    heads, group = width // HEAD_SIZE, text_width // HEAD_SIZE
    peers = seq * head // 2
    image, share = peers * rows, text // seq
    keys = 2 * image + text
    slot_index = jnp.sum(
        jnp.where(
            jnp.arange(timestep_group.shape[0], dtype=jnp.int32) == timestep[0], timestep_group, 0
        )
    )
    slot_rows = jnp.arange(value_step_sizes.shape[0], dtype=jnp.int32) == slot_index
    step_row = jnp.sum(jnp.where(slot_rows[:, None], value_step_sizes, 0.0), axis=0)
    step_lanes = jnp.repeat(step_row, HEAD_SIZE)[None, :]
    vmem = pl.BlockSpec(memory_space=pltpu.VMEM)
    sems = pltpu.SemaphoreType.DMA
    dq_img, dk_img, dv_quant, dq_txt, dk_txt, dv_txt = pl.pallas_call(
        functools.partial(attention_kernel, seq, head),
        out_shape=[jax.ShapeDtypeStruct((rows, width), BF)] * 3
        + [jax.ShapeDtypeStruct((share, text_width), BF)] * 3,
        in_specs=[vmem] * 9,
        out_specs=[vmem] * 6,
        scratch_shapes=[
            pltpu.VMEM((heads, 4 * rows, HEAD_SIZE), BF),
            pltpu.VMEM((peers, 4 * rows, HEAD_SIZE), BF),
            pltpu.VMEM((peers, 2 * rows, HEAD_SIZE), BF),
            pltpu.VMEM((2, text, HEAD_SIZE), BF),
            pltpu.VMEM((2, text // 2, HEAD_SIZE), BF),
            pltpu.VMEM((keys, HEAD_SIZE), BF),
            pltpu.VMEM((HEAD_SIZE, keys), BF),
            pltpu.VMEM((keys, HEAD_SIZE), BF),
            pltpu.VMEM((image + text // 2, HEAD_SIZE), BF),
            pltpu.VMEM((image + text // 2, HEAD_SIZE), BF),
            pltpu.VMEM((image + text // 2, HEAD_SIZE), BF),
            pltpu.VMEM((keys, HEAD_SIZE), F32),
            pltpu.VMEM((keys, HEAD_SIZE), F32),
            pltpu.VMEM((2, image, HEAD_SIZE), BF),
            pltpu.VMEM((2, image, HEAD_SIZE), BF),
            pltpu.VMEM((2 * text + text // 2, HEAD_SIZE), BF),
            pltpu.VMEM((2 * text + text // 2, HEAD_SIZE), BF),
            pltpu.VMEM((peers, 3 * rows, HEAD_SIZE), BF),
            pltpu.VMEM((heads, 3 * rows, HEAD_SIZE), BF),
            pltpu.VMEM((seq, 3, share, HEAD_SIZE), BF),
            pltpu.VMEM((group, 3, share, HEAD_SIZE), BF),
            sems((heads,)),
            sems((peers,)),
            sems((1,)),
            sems((1,)),
            sems((4,)),
            sems((4,)),
            sems((2,)),
            sems((2,)),
            sems((peers,)),
            sems((heads,)),
            sems((seq,)),
            sems((group,)),
        ],
        compiler_params=pltpu.CompilerParams(
            collective_id=0, has_side_effects=True, vmem_limit_bytes=48 * 1024 * 1024
        ),
        name="whole_heads",
    )(
        image_query_rows,
        image_key_rows,
        image_value_codes,
        image_output_grad,
        text_query_rows,
        text_key_rows,
        text_value_rows,
        text_output_grad,
        step_lanes,
    )
    inside = jnp.abs(image_value_codes) < QMAX
    lsq_term = jnp.where(
        inside, -value_fraction.astype(jnp.float32), image_value_codes.astype(jnp.float32)
    )
    image_value_grad = jnp.where(inside, dv_quant, jnp.zeros_like(dv_quant))
    lowrank_gradient = dot(image_value_grad, adapter_up_weight, NT).astype(BF)
    part_down = jnp.einsum(
        "td,tr->dr", image_input_rows, lowrank_gradient, preferred_element_type=jnp.float32
    )
    lowrank_input = dot(image_input_rows, adapter_down_weight).astype(BF)
    part_up = jnp.einsum(
        "tr,tw->rw", lowrank_input, image_value_grad, preferred_element_type=jnp.float32
    )
    token_terms = (dv_quant.astype(jnp.float32) * lsq_term).reshape(rows, heads, HEAD_SIZE)
    total_down, total_up, step_sums = lax.psum(
        (part_down, part_up, jnp.sum(token_terms, axis=(0, 2))), ("seq", "head")
    )
    grad_steps = jnp.where(slot_rows[:, None], step_sums[None, :], 0.0) * (QMAX ** (-0.5) * unscale)
    return (
        dq_img,
        dk_img,
        image_value_grad,
        dq_txt,
        dk_txt,
        dv_txt,
        total_down * unscale,
        total_up * unscale,
        grad_steps,
    )


def pick(mesh):
    seq, head = mesh.shape["seq"], mesh.shape["head"]

    def chosen(*arguments):
        rows, width = arguments[3].shape
        text, text_width = arguments[11].shape
        pair = 2 * text_width // HEAD_SIZE
        fits = (
            head % 2 == 0
            and seq % 2 == 0
            and seq >= pair
            and rows % 16 == 0
            and text % (seq * 16) == 0
            and (seq * head // 2 * rows) % (text // 2) == 0
            and (seq * head * rows + text) * HEAD_SIZE <= 1 << 18
        )
        if fits:
            return whole_heads(seq, head, *arguments)
        return on_device(*arguments)

    return chosen


def solution(mesh):
    placed = (
        P(("seq", "head"), None),
        P(),
        P(),
        P(("seq", "head"), None),
        P(("seq", "head"), None),
        P(("seq", "head"), None),
        P(("seq", "head"), None),
        P(),
        P(),
        P(),
        P(("seq", "head"), None),
        P(None, "head"),
        P(None, "head"),
        P(None, "head"),
        P(None, "head"),
    )
    return jax.shard_map(
        pick(mesh),
        mesh=mesh,
        in_specs=placed,
        out_specs=(
            P(("seq", "head"), None),
            P(("seq", "head"), None),
            P(("seq", "head"), None),
            P("seq", "head"),
            P("seq", "head"),
            P("seq", "head"),
            P(),
            P(),
            P(),
        ),
        check_vma=False,
    )
```

```python
import functools
import math

import jax
import jax.numpy as jnp
from jax import lax
from jax.experimental import pallas as pl
from jax.experimental.pallas import tpu as pltpu
from jax.sharding import PartitionSpec as P

HEAD_SIZE = 128
QMAX = 127


unscale = 0.0078125


def split_heads(rows):
    return rows.reshape(rows.shape[0], rows.shape[1] // HEAD_SIZE, HEAD_SIZE)


def join_heads(heads):
    return heads.reshape(heads.shape[0], heads.shape[1] * heads.shape[2])


def head_scores(queries, key_rows):
    return jnp.einsum(
        "qhd,khd->hqk", queries, key_rows, preferred_element_type=jnp.float32
    ) * HEAD_SIZE ** (-0.5)


def over_keys(step_fn, initial, key_rows, value_rows):
    block_rows = math.gcd(key_rows.shape[0], 2048)

    def over_one_turn(turn_index, carried):
        key_block = lax.dynamic_slice_in_dim(key_rows, turn_index * block_rows, block_rows, 0)
        value_block = lax.dynamic_slice_in_dim(value_rows, turn_index * block_rows, block_rows, 0)
        return step_fn(carried, key_block, value_block)

    return lax.fori_loop(0, key_rows.shape[0] // block_rows, over_one_turn, initial)


def key_terms(carried, queries, grads, log_rows, delta_rows, own_keys, own_values):
    key_grad, value_grad = carried
    probs = jnp.exp(head_scores(queries, own_keys) - log_rows.T[:, :, None])
    dprobs = jnp.einsum("qhd,khd->hqk", grads, own_values, preferred_element_type=jnp.float32)
    dscores = (probs * (dprobs - delta_rows.T[:, :, None])).astype(jnp.bfloat16)
    value_grad = value_grad + jnp.einsum(
        "hqk,qhd->khd", probs.astype(jnp.bfloat16), grads, preferred_element_type=jnp.float32
    )
    key_grad = key_grad + jnp.einsum(
        "hqk,qhd->khd", dscores, queries, preferred_element_type=jnp.float32
    ) * HEAD_SIZE ** (-0.5)
    return (key_grad, value_grad)


def on_device(
    image_input_rows,
    adapter_down_weight,
    adapter_up_weight,
    image_query_rows,
    image_key_rows,
    image_value_codes,
    value_fraction,
    value_step_sizes,
    timestep_group,
    timestep,
    image_output_grad,
    text_query_rows,
    text_key_rows,
    text_value_rows,
    text_output_grad,
):
    slot_index = jnp.sum(
        jnp.where(
            jnp.arange(timestep_group.shape[0], dtype=jnp.int32) == timestep[0], timestep_group, 0
        )
    )
    slot_rows = jnp.arange(value_step_sizes.shape[0], dtype=jnp.int32) == slot_index
    step_row = jnp.sum(jnp.where(slot_rows[:, None], value_step_sizes, 0.0), axis=0)
    code_values = image_value_codes.astype(jnp.float32)
    v_dequant = (code_values * jnp.repeat(step_row, HEAD_SIZE)[None, :]).astype(jnp.bfloat16)
    inside = jnp.abs(image_value_codes) < QMAX
    lsq_term = jnp.where(inside, -value_fraction.astype(jnp.float32), code_values)
    query_img, key_img, value_img, grad_img = (
        lax.all_to_all(image_query_rows, "head", split_axis=1, concat_axis=0, tiled=True),
        lax.all_to_all(image_key_rows, "head", split_axis=1, concat_axis=0, tiled=True),
        lax.all_to_all(v_dequant, "head", split_axis=1, concat_axis=0, tiled=True),
        lax.all_to_all(image_output_grad, "head", split_axis=1, concat_axis=0, tiled=True),
    )
    share_rows = text_query_rows.shape[0] // lax.axis_size("seq")
    first_row = lax.axis_index("seq") * share_rows

    def own_rows(table):
        return lax.dynamic_slice_in_dim(table, first_row, share_rows, 0)

    image_rows = query_img.shape[0]
    query_local = jnp.concatenate([query_img, own_rows(text_query_rows)], axis=0)
    grad_local = jnp.concatenate([grad_img, own_rows(text_output_grad)], axis=0)
    query_split = split_heads(query_local)
    grad_split = split_heads(grad_local)
    local_count = query_split.shape[0]
    head_count = query_split.shape[1]
    key_image, value_image = (
        lax.all_gather(key_img, "seq", axis=0, tiled=True),
        lax.all_gather(value_img, "seq", axis=0, tiled=True),
    )
    text_keys = split_heads(text_key_rows)
    text_values = split_heads(text_value_rows)
    key_sets = ((split_heads(key_image), split_heads(value_image)), (text_keys, text_values))

    def stat_turn(carried, key_block, value_block):
        row_max, running, weighted = carried
        scores = head_scores(query_split, key_block)
        dprobs = jnp.einsum(
            "qhd,khd->hqk", grad_split, value_block, preferred_element_type=jnp.float32
        )
        new_max = jnp.maximum(row_max, jnp.max(scores, axis=2, keepdims=True))
        factor = jnp.exp(row_max - new_max)
        expo = jnp.exp(scores - new_max)
        running = running * factor + jnp.sum(expo, axis=2, keepdims=True)
        weighted = weighted * factor + jnp.sum(expo * dprobs, axis=2, keepdims=True)
        return (new_max, running, weighted)

    row_stats = (
        jnp.full((head_count, local_count, 1), -jnp.inf, jnp.float32),
        jnp.zeros((head_count, local_count, 1), jnp.float32),
        jnp.zeros((head_count, local_count, 1), jnp.float32),
    )
    for key_rows, value_rows in key_sets:
        row_stats = over_keys(stat_turn, row_stats, key_rows, value_rows)
    log_sums = row_stats[0] + jnp.log(row_stats[1])
    deltas = row_stats[2] / row_stats[1]

    def query_turn(running, key_block, value_block):
        probs = jnp.exp(head_scores(query_split, key_block) - log_sums)
        dprobs = jnp.einsum(
            "qhd,khd->hqk", grad_split, value_block, preferred_element_type=jnp.float32
        )
        dscores = (probs * (dprobs - deltas)).astype(jnp.bfloat16)
        return running + jnp.einsum(
            "hqk,khd->qhd", dscores, key_block, preferred_element_type=jnp.float32
        ) * HEAD_SIZE ** (-0.5)

    query_grad = jnp.zeros((local_count, head_count, HEAD_SIZE), jnp.float32)
    for key_rows, value_rows in key_sets:
        query_grad = over_keys(query_turn, query_grad, key_rows, value_rows)
    query_grad = join_heads(query_grad).astype(jnp.bfloat16)
    log_rows = log_sums[:, :, 0].T
    delta_rows = deltas[:, :, 0].T
    own_keys = split_heads(key_img)
    own_values = split_heads(value_img)
    empty = jnp.zeros(own_keys.shape, jnp.float32)
    query_rows = lax.all_gather(query_local.astype(jnp.float32), "seq", axis=0, tiled=True).astype(
        jnp.bfloat16
    )
    grad_rows = lax.all_gather(grad_local.astype(jnp.float32), "seq", axis=0, tiled=True).astype(
        jnp.bfloat16
    )
    log_part = lax.all_gather(log_rows, "seq", axis=0, tiled=True)
    delta_part = lax.all_gather(delta_rows, "seq", axis=0, tiled=True)
    piece_rows = query_rows.shape[0]
    block_rows = piece_rows if piece_rows <= 2048 else math.gcd(piece_rows, 2048)

    def fold_one_turn(turn_index, running):

        def rows_of(table):
            return lax.dynamic_slice_in_dim(table, turn_index * block_rows, block_rows, 0)

        return key_terms(
            running,
            split_heads(rows_of(query_rows)),
            split_heads(rows_of(grad_rows)),
            rows_of(log_part),
            rows_of(delta_part),
            own_keys,
            own_values,
        )

    key_grad, value_grad = lax.fori_loop(0, piece_rows // block_rows, fold_one_turn, (empty, empty))
    key_grad = join_heads(key_grad).astype(jnp.bfloat16)
    value_grad = join_heads(value_grad).astype(jnp.bfloat16)
    text_empty = jnp.zeros(text_keys.shape, jnp.float32)
    text_key, text_value = key_terms(
        (text_empty, text_empty),
        query_split,
        grad_split,
        log_rows,
        delta_rows,
        text_keys,
        text_values,
    )
    text_key, text_value = (
        lax.psum_scatter(join_heads(text_key), "seq", scatter_dimension=0, tiled=True),
        lax.psum_scatter(join_heads(text_value), "seq", scatter_dimension=0, tiled=True),
    )
    dk_txt = text_key.astype(jnp.bfloat16)
    dv_txt = text_value.astype(jnp.bfloat16)
    dq_txt = query_grad[image_rows:]
    dq_heads = query_grad[:image_rows]
    dq_img, dk_img, dv_quant = (
        lax.all_to_all(dq_heads, "head", split_axis=0, concat_axis=1, tiled=True),
        lax.all_to_all(key_grad, "head", split_axis=0, concat_axis=1, tiled=True),
        lax.all_to_all(value_grad, "head", split_axis=0, concat_axis=1, tiled=True),
    )
    image_value_grad = jnp.where(inside, dv_quant, jnp.zeros_like(dv_quant))
    lowrank_gradient = jnp.einsum(
        "vg,zg->vz", image_value_grad, adapter_up_weight, preferred_element_type=jnp.float32
    ).astype(jnp.bfloat16)
    part_down = jnp.einsum(
        "td,tr->dr", image_input_rows, lowrank_gradient, preferred_element_type=jnp.float32
    )
    lowrank_input = jnp.dot(
        image_input_rows, adapter_down_weight, preferred_element_type=jnp.float32
    ).astype(jnp.bfloat16)
    part_up = jnp.einsum(
        "tr,tw->rw", lowrank_input, image_value_grad, preferred_element_type=jnp.float32
    )
    token_rows = dv_quant.shape[0]
    token_terms = (dv_quant.astype(jnp.float32) * lsq_term).reshape(
        token_rows, value_step_sizes.shape[1], HEAD_SIZE
    )
    total_down, total_up, step_sums = lax.psum(
        (part_down, part_up, jnp.sum(token_terms, axis=(0, 2))), ("seq", "head")
    )
    grad_steps = jnp.where(slot_rows[:, None], step_sums[None, :], 0.0) * (QMAX ** (-0.5) * unscale)
    return (
        dq_img,
        dk_img,
        image_value_grad,
        dq_txt,
        dk_txt,
        dv_txt,
        total_down * unscale,
        total_up * unscale,
        grad_steps,
    )


MESH = pl.DeviceIdType.MESH
BF = jnp.bfloat16
F32 = jnp.float32
NT = (((1,), (1,)), ((), ()))
NN = (((1,), (0,)), ((), ()))


def dot(left, right, dims=NN):
    return lax.dot_general(left, right, dims, preferred_element_type=F32)


def attention_kernel(
    seq,
    head,
    q_in,
    k_in,
    code_in,
    do_in,
    tq_in,
    tk_in,
    tv_in,
    tdo_in,
    x_in,
    frac_in,
    up_in,
    down_in,
    step_ref,
    group_ref,
    time_ref,
    dq_ref,
    dk_ref,
    dv_ref,
    dqt_ref,
    dkt_ref,
    dvt_ref,
    down_ref,
    up_ref,
    steps_ref,
    q_ref,
    k_ref,
    code_ref,
    do_ref,
    x_ref,
    frac_ref,
    upw_ref,
    downw_ref,
    stage,
    recv,
    kv2,
    tkv,
    tqd,
    kall,
    ktr,
    vall,
    qall,
    doall,
    dqall,
    dkacc,
    dvacc,
    xo,
    xi,
    to,
    ti,
    ost,
    ret,
    tfin,
    rett,
    xlow_out,
    xlow_in,
    xst,
    xcol,
    up_out,
    up_in2,
    up_all,
    low_out,
    low_in,
    red_out,
    red_in,
    gath,
    li,
    s1,
    r1,
    s2,
    r2,
    st,
    rt,
    s3,
    r3,
    s4,
    r4,
    s5,
    r5,
    s6,
    r6,
    s7,
    r7,
    s8,
    r8,
    s9,
    r9,
    s10,
    r10,
    s11,
    r11,
    s12,
    r12,
):
    rows = q_ref.shape[0]
    heads = q_ref.shape[1] // HEAD_SIZE
    text = tq_in.shape[0]
    half = text // 2
    planes = head // 2
    peers = seq * planes
    group = tq_in.shape[1] // HEAD_SIZE
    pair = 2 * group
    first = (seq - pair) // 2
    image = peers * rows
    share = text // seq
    scale = HEAD_SIZE ** (-0.5)
    rank = upw_ref.shape[0]
    wide = x_ref.shape[1] // seq
    part = rank // head
    hrank = rank // 2
    hrows = rows // 2

    s = lax.axis_index("seq")
    g = lax.axis_index("head")
    c = lax.rem(g, 2)
    y = g // 2
    me = s * planes + y
    partner = (s, g + 1 - 2 * c)
    slot = s - first
    is_head = jnp.logical_and(slot >= 0, slot < pair)
    mine = y * pair + slot
    holds_text = jnp.logical_and(is_head, slot // group == c)
    takes_text = jnp.logical_and(is_head, slot // group != c)
    lane_block = lax.rem(slot, group)

    def peer(p):
        return (p // planes, lax.rem(p, planes) * 2 + c)

    def home(h):
        return (first + lax.rem(h, pair), (h // pair) * 2 + c)

    def home_peer(h):
        return (first + lax.rem(h, pair)) * planes + h // pair

    def send(src, dst, ssem, rsem, to_id):
        return pltpu.make_async_remote_copy(
            src_ref=src, dst_ref=dst, send_sem=ssem, recv_sem=rsem, device_id=to_id, device_id_type=MESH
        )

    loads = [
        pltpu.make_async_copy(src, dst, li.at[i])
        for i, (src, dst) in enumerate(
            (
                (k_in, k_ref),
                (code_in, code_ref),
                (q_in, q_ref),
                (do_in, do_ref),
                (x_in, x_ref),
                (down_in, downw_ref),
                (up_in, upw_ref),
                (frac_in, frac_ref),
            )
        )
    ]
    for load in loads:
        load.start()

    barrier = pltpu.get_barrier_semaphore()
    for i in range(1, peers):
        pl.semaphore_signal(
            barrier, inc=1, device_id=peer(lax.rem(me + i, peers)), device_id_type=MESH
        )
    for other in range(planes):
        pl.semaphore_signal(
            barrier, inc=1, device_id=(s, other * 2 + 1 - c), device_id_type=MESH
        )

    for load in loads[:4]:
        load.wait()
    for h in range(heads):
        cols = slice(h * HEAD_SIZE, (h + 1) * HEAD_SIZE)
        stage[h, 0:rows] = k_ref[:, cols]
        stage[h, rows : 2 * rows] = code_ref[:, cols].astype(F32).astype(BF)
        stage[h, 2 * rows : 3 * rows] = q_ref[:, cols]
        stage[h, 3 * rows : 4 * rows] = do_ref[:, cols]

    pl.semaphore_wait(barrier, peers - 1 + planes)

    def first_send(h):
        return send(stage.at[h], recv.at[me], s1.at[h], r1.at[me], home(h))

    def first_recv(p):
        return send(stage.at[0], recv.at[p], s1.at[0], r1.at[p], partner)

    for i in range(heads):
        h = lax.rem(me + i, heads)

        @pl.when(me != home_peer(h))
        def _():
            first_send(h).start()

    def text_sources():
        cols = pl.ds(pl.multiple_of(lane_block * HEAD_SIZE, HEAD_SIZE), HEAD_SIZE)
        return cols, pl.ds(0, half), pl.ds(half, half)

    def text_copies():
        cols, _, low = text_sources()
        return (
            send(tk_in.at[:, cols], tkv.at[0], st.at[0], rt.at[0], partner),
            send(tv_in.at[:, cols], tkv.at[1], st.at[1], rt.at[1], partner),
            send(tq_in.at[low, cols], tqd.at[0], st.at[2], rt.at[2], partner),
            send(tdo_in.at[low, cols], tqd.at[1], st.at[3], rt.at[3], partner),
        )

    def text_loads():
        cols, high, _ = text_sources()
        return (
            pltpu.make_async_copy(tk_in.at[:, cols], tkv.at[0], li.at[8]),
            pltpu.make_async_copy(tv_in.at[:, cols], tkv.at[1], li.at[9]),
            pltpu.make_async_copy(tq_in.at[high, cols], tqd.at[0], li.at[10]),
            pltpu.make_async_copy(tdo_in.at[high, cols], tqd.at[1], li.at[11]),
        )

    @pl.when(holds_text)
    def _():
        for copy in text_copies() + text_loads():
            copy.start()

    for load in loads[4:6]:
        load.wait()
    for t in range(seq):
        xst[t] = x_ref[:, t * wide : (t + 1) * wide]

    def column_send(t):
        return send(xst.at[t], xcol.at[s], s6.at[t], r6.at[s], (t, g))

    for i in range(1, seq):
        column_send(lax.rem(s + i, seq)).start()
    xcol[pl.ds(s, 1)] = xst[pl.ds(s, 1)]

    xlow = dot(x_ref[...], downw_ref[...])
    xlow_out[...] = jnp.concatenate([xlow[0:hrows], xlow[hrows:rows]], axis=1).astype(BF)

    def low_send(h):
        return send(xlow_out, xlow_in.at[me], s7.at[h], r7.at[me], home(h))

    for i in range(heads):
        h = lax.rem(me + i, heads)

        @pl.when(me != home_peer(h))
        def _():
            low_send(h).start()

    for load in loads[6:8]:
        load.wait()

    def up_send(p):
        return send(
            up_out.at[c], up_all.at[mine, c], s9.at[p], r9.at[mine], peer(p)
        )

    @pl.when(is_head)
    def _():
        recv[pl.ds(me, 1)] = stage[pl.ds(mine, 1)]
        xlow_in[pl.ds(me, 1)] = xlow_out[...].reshape(1, hrows, HEAD_SIZE)
        for p in range(peers):

            @pl.when(me != p)
            def _():
                first_recv(p).wait_recv()

        swap = send(recv.at[:, pl.ds(0, 2 * rows)], kv2, s2.at[0], r2.at[0], partner)
        swap.start()
        step = step_ref[group_ref[time_ref[0]], mine]

        def dequant(codes):
            return (codes.reshape(image, HEAD_SIZE).astype(F32) * step).astype(BF)

        kall[0:image] = recv[:, 0:rows].reshape(image, HEAD_SIZE)
        vall[0:image] = dequant(recv[:, rows : 2 * rows])
        qall[0:image] = recv[:, 2 * rows : 3 * rows].reshape(image, HEAD_SIZE)
        doall[0:image] = recv[:, 3 * rows : 4 * rows].reshape(image, HEAD_SIZE)

        @pl.when(takes_text)
        def _():
            for copy in text_copies():
                copy.wait_recv()

        @pl.when(holds_text)
        def _():
            for copy in text_loads():
                copy.wait()

        kall[2 * image : 2 * image + text] = tkv[0]
        vall[2 * image : 2 * image + text] = tkv[1]
        qall[image : image + half] = tqd[0]
        doall[image : image + half] = tqd[1]
        swap.wait_recv()
        kall[image : 2 * image] = kv2[:, 0:rows].reshape(image, HEAD_SIZE)
        vall[image : 2 * image] = dequant(kv2[:, rows : 2 * rows])
        ktr[...] = kall[...].T
        dkacc[...] = jnp.zeros_like(dkacc)
        dvacc[...] = jnp.zeros_like(dvacc)

        def query_block(index, carried):
            at = pl.ds(pl.multiple_of(index * half, half), half)
            queries, grads = qall[at], doall[at]
            scores = dot(kall[...], queries, NT) * scale
            expo = jnp.exp(scores - jnp.max(scores, axis=0, keepdims=True))
            probs = expo * (1.0 / jnp.sum(expo, axis=0, keepdims=True))
            dvacc[...] += dot(probs.astype(BF), grads)
            dprobs = dot(vall[...], grads, NT)
            deltas = jnp.sum(probs * dprobs, axis=0, keepdims=True)
            dscores = (probs * (dprobs - deltas)).astype(BF)
            dkacc[...] += dot(dscores, queries)
            dqall[at] = (dot(ktr[...], dscores).T * scale).astype(BF)
            return carried

        lax.fori_loop(0, (image + half) // half, query_block, 0)
        xo[0] = (dkacc[image : 2 * image] * scale).astype(BF)
        xo[1] = dvacc[image : 2 * image].astype(BF)
        trade = send(xo, xi, s3.at[0], r3.at[0], partner)
        trade.start()
        text_trade = send(to, ti, s3.at[1], r3.at[1], partner)

        @pl.when(takes_text)
        def _():
            to[0:text] = (dkacc[2 * image : 2 * image + text] * scale).astype(BF)
            to[text : 2 * text] = dvacc[2 * image : 2 * image + text].astype(BF)
            to[2 * text : 2 * text + half] = dqall[image : image + half]
            text_trade.start()

        ost[:, 0:rows] = dqall[0:image].reshape(peers, rows, HEAD_SIZE)
        trade.wait_recv()
        ost[:, rows : 2 * rows] = (
            (dkacc[0:image] * scale + xi[0].astype(F32)).astype(BF).reshape(peers, rows, HEAD_SIZE)
        )
        ost[:, 2 * rows : 3 * rows] = (
            (dvacc[0:image] + xi[1].astype(F32)).astype(BF).reshape(peers, rows, HEAD_SIZE)
        )
        for i in range(1, peers):
            p = lax.rem(me + i, peers)
            send(ost.at[p], ret.at[mine], s4.at[p], r4.at[mine], peer(p)).start()

        ret[pl.ds(mine, 1)] = ost[pl.ds(me, 1)]

        for p in range(peers):

            @pl.when(me != p)
            def _():
                send(xlow_out, xlow_in.at[p], s7.at[0], r7.at[p], partner).wait_recv()

        codes = recv[:, rows : 2 * rows]
        kept = jnp.where(jnp.abs(codes.astype(F32)) < QMAX, ost[:, 2 * rows : 3 * rows].astype(F32), 0.0)
        kept = kept.astype(BF)
        low_rows = xlow_in[...].reshape(peers * hrows, HEAD_SIZE).T
        early = dot(low_rows, kept[:, 0:hrows].reshape(peers * hrows, HEAD_SIZE))
        late = dot(low_rows, kept[:, hrows:rows].reshape(peers * hrows, HEAD_SIZE))
        part_up = (early[0:rank] + late[rank : 2 * rank]).reshape(2, hrank, HEAD_SIZE)
        up_out32 = up_in2.at[0]
        up_out32[...] = part_up
        up_trade = send(up_in2.at[0, 1 - c], up_in2.at[1, 0], s8.at[0], r8.at[0], partner)
        up_trade.start()

        @pl.when(holds_text)
        def _():
            text_trade.wait_recv()
            full = (seq, share, HEAD_SIZE)
            tfin[0 : seq // 2, 0] = dqall[image : image + half].reshape(seq // 2, share, HEAD_SIZE)
            tfin[seq // 2 : seq, 0] = ti[2 * text : 2 * text + half].reshape(seq // 2, share, HEAD_SIZE)
            tfin[:, 1] = (
                (dkacc[2 * image : 2 * image + text] * scale + ti[0:text].astype(F32)).astype(BF).reshape(full)
            )
            tfin[:, 2] = (
                (dvacc[2 * image : 2 * image + text] + ti[text : 2 * text].astype(F32)).astype(BF).reshape(full)
            )
            for i in range(1, seq):
                other = lax.rem(s + i, seq)
                send(
                    tfin.at[other], rett.at[lane_block], s5.at[other], r5.at[lane_block], (other, g)
                ).start()

            rett[pl.ds(lane_block, 1)] = tfin[pl.ds(s, 1)]

        up_trade.wait_recv()
        up_out[pl.ds(c, 1)] = (
            (up_in2[pl.ds(0, 1), pl.ds(c, 1)] + up_in2[pl.ds(1, 1), pl.ds(0, 1)]) * unscale
        ).astype(BF).reshape(1, hrank, HEAD_SIZE)
        for i in range(1, peers):
            up_send(lax.rem(me + i, peers)).start()
        up_all[pl.ds(mine, 1), pl.ds(c, 1)] = up_out[pl.ds(c, 1)].reshape(1, 1, hrank, HEAD_SIZE)

    low = jnp.zeros((rows, rank), F32)
    lane = lax.broadcasted_iota(jnp.int32, (1, HEAD_SIZE), 1)
    step_terms = jnp.zeros((1, HEAD_SIZE), F32)
    for h in range(heads):

        @pl.when(me != home_peer(h))
        def _():
            send(ost.at[0], ret.at[h], s4.at[0], r4.at[h], partner).wait_recv()

        cols = slice(h * HEAD_SIZE, (h + 1) * HEAD_SIZE)
        codes = code_ref[:, cols]
        inside = jnp.abs(codes) < QMAX
        value_grad = ret[h, 2 * rows : 3 * rows].astype(F32)
        kept = jnp.where(inside, value_grad, 0.0).astype(BF)
        lsq_term = jnp.where(inside, -frac_ref[:, cols].astype(F32), codes.astype(F32))
        total = jnp.sum(value_grad * lsq_term)
        step_terms = step_terms + jnp.where(lane == h, total, 0.0)
        low = low + dot(kept, upw_ref[:, cols], NT)
        dq_ref[:, cols] = ret[h, 0:rows]
        dk_ref[:, cols] = ret[h, rows : 2 * rows]
        dv_ref[:, cols] = kept

    step_high = step_terms.astype(BF).astype(F32)
    step_low = step_terms - step_high
    row_at = lax.broadcasted_iota(jnp.int32, (rows, rank), 0)
    beside = jnp.where(
        row_at == 0, step_high[:, 0:rank], jnp.where(row_at == 1, step_low[:, 0:rank], 0.0)
    )
    low_out[...] = jnp.concatenate([low, beside], axis=1).astype(BF)

    def tile_send(t):
        return send(low_out, low_in.at[s], s10.at[t], r10.at[s], (t, g))

    for i in range(1, seq):
        tile_send(lax.rem(s + i, seq)).start()
    low_in[pl.ds(s, 1)] = low_out[...].reshape(1, rows, HEAD_SIZE)

    for j in range(group):

        @pl.when(s != first + c * group + j)
        def _():
            send(tfin.at[0], rett.at[j], s5.at[0], r5.at[j], partner).wait_recv()

        cols = slice(j * HEAD_SIZE, (j + 1) * HEAD_SIZE)
        dqt_ref[:, cols] = rett[j, 0]
        dkt_ref[:, cols] = rett[j, 1]
        dvt_ref[:, cols] = rett[j, 2]

    for t in range(seq):

        @pl.when(s != t)
        def _():
            send(xst.at[0], xcol.at[t], s6.at[0], r6.at[t], partner).wait_recv()
            send(low_out, low_in.at[t], s10.at[0], r10.at[t], partner).wait_recv()

    tiles = low_in[...]
    flat = tiles.reshape(seq * rows, HEAD_SIZE).T
    block = dot(flat, xcol[...].reshape(seq * rows, wide))[0:rank]
    step_group = jnp.sum(
        jnp.sum(tiles[:, 0:2].astype(F32), axis=0), axis=0, keepdims=True
    )
    for other in range(head):
        red_out[other, 0:part] = block[other * part : (other + 1) * part]
        red_out[other, part : part + 8, 0:HEAD_SIZE] = jnp.broadcast_to(step_group, (8, HEAD_SIZE))
        red_out[other, part : part + 8, HEAD_SIZE:wide] = jnp.zeros((8, wide - HEAD_SIZE), F32)

    def reduce_send(other):
        return send(red_out.at[other], red_in.at[g], s11.at[other], r11.at[g], (s, other))

    for i in range(1, head):
        reduce_send(lax.rem(g + i, head)).start()
    red_in[pl.ds(g, 1)] = red_out[pl.ds(g, 1)]
    for other in range(head):

        @pl.when(g != other)
        def _():
            send(red_out.at[0], red_in.at[other], s11.at[0], r11.at[other], partner).wait_recv()

    summed = jnp.sum(red_in[...], axis=0)
    gath[pl.ds(y, 1), pl.ds(c, 1), pl.ds(s, 1)] = (
        (summed[0:part] * unscale).astype(BF).reshape(1, 1, 1, part, wide)
    )

    def row_send(t):
        return send(
            gath.at[y, c, s], gath.at[y, c, s], s12.at[t], r12.at[s], (t, g)
        )

    def plane_send(i):
        to_plane = lax.rem(y + i, planes)
        return send(
            gath.at[y, c], gath.at[y, c], s12.at[seq + i], r12.at[seq + y], (s, to_plane * 2 + c)
        )

    def core_send():
        return send(gath.at[:, c], gath.at[:, c], s12.at[seq], r12.at[seq + planes], partner)

    def core_up_send():
        return send(up_all.at[:, c], up_all.at[:, c], s8.at[1], r8.at[1], partner)

    for i in range(1, seq):
        row_send(lax.rem(s + i, seq)).start()

    slot_index = group_ref[time_ref[0]]
    step_row = summed[part : part + 1, HEAD_SIZE // 2 : HEAD_SIZE // 2 + heads] * (QMAX ** (-0.5) * unscale)
    slots = steps_ref.shape[0]
    slot_at = lax.broadcasted_iota(jnp.int32, (slots, heads), 0)
    steps_ref[...] = jnp.where(slot_at == slot_index, jnp.broadcast_to(step_row, (slots, heads)), 0.0)

    for h in range(heads):

        @pl.when(me != home_peer(h))
        def _():
            send(up_out.at[0], up_all.at[h, c], s9.at[0], r9.at[h], partner).wait_recv()

    core_up_send().start()

    for t in range(seq):

        @pl.when(s != t)
        def _():
            send(gath.at[y, c, t], gath.at[y, c, t], s12.at[0], r12.at[t], partner).wait_recv()

    for i in range(1, planes):
        plane_send(i).start()
    for i in range(1, planes):
        from_plane = lax.rem(y + i, planes)
        send(
            gath.at[from_plane, c], gath.at[from_plane, c], s12.at[seq + i], r12.at[seq + from_plane], partner
        ).wait_recv()
    core_send().start()
    send(up_all.at[:, 1 - c], up_all.at[:, 1 - c], s8.at[1], r8.at[1], partner).wait_recv()
    for h in range(heads):
        cols = slice(h * HEAD_SIZE, (h + 1) * HEAD_SIZE)
        up_ref[:, cols] = up_all[h].reshape(rank, HEAD_SIZE).astype(F32)
    send(gath.at[:, 1 - c], gath.at[:, 1 - c], s12.at[seq], r12.at[seq + planes], partner).wait_recv()
    for t in range(seq):
        down_ref[t * wide : (t + 1) * wide] = gath[:, :, t].reshape(rank, wide).astype(F32).T

    for h in range(heads):

        @pl.when(me != home_peer(h))
        def _():
            first_send(h).wait_send()
            low_send(h).wait_send()

    for i in range(1, seq):
        t = lax.rem(s + i, seq)
        column_send(t).wait_send()
        tile_send(t).wait_send()
        row_send(t).wait_send()
    for i in range(1, head):
        reduce_send(lax.rem(g + i, head)).wait_send()
    for i in range(1, planes):
        plane_send(i).wait_send()
    core_send().wait_send()
    core_up_send().wait_send()

    @pl.when(is_head)
    def _():
        send(recv.at[:, pl.ds(0, 2 * rows)], kv2, s2.at[0], r2.at[0], partner).wait_send()
        send(xo, xi, s3.at[0], r3.at[0], partner).wait_send()
        send(up_in2.at[0, 1 - c], up_in2.at[1, 0], s8.at[0], r8.at[0], partner).wait_send()
        for i in range(1, peers):
            p = lax.rem(me + i, peers)
            send(ost.at[p], ret.at[mine], s4.at[p], r4.at[mine], peer(p)).wait_send()
            up_send(p).wait_send()

    @pl.when(takes_text)
    def _():
        send(to, ti, s3.at[1], r3.at[1], partner).wait_send()

    @pl.when(holds_text)
    def _():
        for copy in text_copies():
            copy.wait_send()
        for i in range(1, seq):
            other = lax.rem(s + i, seq)
            send(
                tfin.at[other], rett.at[lane_block], s5.at[other], r5.at[lane_block], (other, g)
            ).wait_send()


def whole_heads(
    seq,
    head,
    image_input_rows,
    adapter_down_weight,
    adapter_up_weight,
    image_query_rows,
    image_key_rows,
    image_value_codes,
    value_fraction,
    value_step_sizes,
    timestep_group,
    timestep,
    image_output_grad,
    text_query_rows,
    text_key_rows,
    text_value_rows,
    text_output_grad,
):
    rows, width = image_query_rows.shape
    text, text_width = text_query_rows.shape
    heads, group = width // HEAD_SIZE, text_width // HEAD_SIZE
    peers = seq * head // 2
    image, share = peers * rows, text // seq
    keys = 2 * image + text
    rank, wide = adapter_up_weight.shape[0], image_input_rows.shape[1] // seq
    planes = head // 2
    vmem = pl.BlockSpec(memory_space=pltpu.VMEM)
    sems = pltpu.SemaphoreType.DMA
    hbm = pl.BlockSpec(memory_space=pl.ANY)
    smem = pl.BlockSpec(memory_space=pltpu.SMEM)
    return tuple(pl.pallas_call(
        functools.partial(attention_kernel, seq, head),
        out_shape=[jax.ShapeDtypeStruct((rows, width), BF)] * 3
        + [jax.ShapeDtypeStruct((share, text_width), BF)] * 3
        + [
            jax.ShapeDtypeStruct(adapter_down_weight.shape, F32),
            jax.ShapeDtypeStruct(adapter_up_weight.shape, F32),
            jax.ShapeDtypeStruct(value_step_sizes.shape, F32),
        ],
        in_specs=[hbm] * 12 + [smem] * 3,
        out_specs=[vmem] * 9,
        scratch_shapes=[
            pltpu.VMEM((rows, width), BF),
            pltpu.VMEM((rows, width), BF),
            pltpu.VMEM((rows, width), jnp.int32),
            pltpu.VMEM((rows, width), BF),
            pltpu.VMEM(image_input_rows.shape, BF),
            pltpu.VMEM((rows, width), BF),
            pltpu.VMEM(adapter_up_weight.shape, BF),
            pltpu.VMEM(adapter_down_weight.shape, BF),
            pltpu.VMEM((heads, 4 * rows, HEAD_SIZE), BF),
            pltpu.VMEM((peers, 4 * rows, HEAD_SIZE), BF),
            pltpu.VMEM((peers, 2 * rows, HEAD_SIZE), BF),
            pltpu.VMEM((2, text, HEAD_SIZE), BF),
            pltpu.VMEM((2, text // 2, HEAD_SIZE), BF),
            pltpu.VMEM((keys, HEAD_SIZE), BF),
            pltpu.VMEM((HEAD_SIZE, keys), BF),
            pltpu.VMEM((keys, HEAD_SIZE), BF),
            pltpu.VMEM((image + text // 2, HEAD_SIZE), BF),
            pltpu.VMEM((image + text // 2, HEAD_SIZE), BF),
            pltpu.VMEM((image + text // 2, HEAD_SIZE), BF),
            pltpu.VMEM((keys, HEAD_SIZE), F32),
            pltpu.VMEM((keys, HEAD_SIZE), F32),
            pltpu.VMEM((2, image, HEAD_SIZE), BF),
            pltpu.VMEM((2, image, HEAD_SIZE), BF),
            pltpu.VMEM((2 * text + text // 2, HEAD_SIZE), BF),
            pltpu.VMEM((2 * text + text // 2, HEAD_SIZE), BF),
            pltpu.VMEM((peers, 3 * rows, HEAD_SIZE), BF),
            pltpu.VMEM((heads, 3 * rows, HEAD_SIZE), BF),
            pltpu.VMEM((seq, 3, share, HEAD_SIZE), BF),
            pltpu.VMEM((group, 3, share, HEAD_SIZE), BF),
            pltpu.VMEM((rows // 2, HEAD_SIZE), BF),
            pltpu.VMEM((peers, rows // 2, HEAD_SIZE), BF),
            pltpu.VMEM((seq, rows, wide), BF),
            pltpu.VMEM((seq, rows, wide), BF),
            pltpu.VMEM((2, rank // 2, HEAD_SIZE), BF),
            pltpu.VMEM((2, 2, rank // 2, HEAD_SIZE), F32),
            pltpu.VMEM((heads, 2, rank // 2, HEAD_SIZE), BF),
            pltpu.VMEM((rows, HEAD_SIZE), BF),
            pltpu.VMEM((seq, rows, HEAD_SIZE), BF),
            pltpu.VMEM((head, rank // head + 8, wide), F32),
            pltpu.VMEM((head, rank // head + 8, wide), F32),
            pltpu.VMEM((planes, 2, seq, rank // head, wide), BF),
            sems((12,)),
            sems((heads,)),
            sems((peers,)),
            sems((1,)),
            sems((1,)),
            sems((4,)),
            sems((4,)),
            sems((2,)),
            sems((2,)),
            sems((peers,)),
            sems((heads,)),
            sems((seq,)),
            sems((group,)),
            sems((seq,)),
            sems((seq,)),
            sems((heads,)),
            sems((peers,)),
            sems((2,)),
            sems((2,)),
            sems((peers,)),
            sems((heads,)),
            sems((seq,)),
            sems((seq,)),
            sems((head,)),
            sems((head,)),
            sems((seq + planes,)),
            sems((seq + planes + 1,)),
        ],
        compiler_params=pltpu.CompilerParams(
            collective_id=0, has_side_effects=True, vmem_limit_bytes=56 * 1024 * 1024
        ),
        name="whole_heads",
    )(
        image_query_rows,
        image_key_rows,
        image_value_codes,
        image_output_grad,
        text_query_rows,
        text_key_rows,
        text_value_rows,
        text_output_grad,
        image_input_rows,
        value_fraction,
        adapter_up_weight,
        adapter_down_weight,
        value_step_sizes,
        timestep_group,
        timestep,
    ))


def pick(mesh):
    seq, head = mesh.shape["seq"], mesh.shape["head"]

    def chosen(*arguments):
        rows, width = arguments[3].shape
        text, text_width = arguments[11].shape
        pair = 2 * text_width // HEAD_SIZE
        fits = (
            head % 2 == 0
            and seq % 2 == 0
            and seq >= pair
            and rows % 32 == 0
            and 2 * arguments[2].shape[0] == HEAD_SIZE
            and width // HEAD_SIZE <= arguments[2].shape[0]
            and arguments[2].shape[0] % (16 * head) == 0
            and arguments[0].shape[1] % (seq * HEAD_SIZE) == 0
            and text % (seq * 16) == 0
            and (seq * head // 2 * rows) % (text // 2) == 0
            and (seq * head * rows + text) * HEAD_SIZE <= 1 << 18
        )
        if fits:
            return whole_heads(seq, head, *arguments)
        return on_device(*arguments)

    return chosen


def solution(mesh):
    placed = (
        P(("seq", "head"), None),
        P(),
        P(),
        P(("seq", "head"), None),
        P(("seq", "head"), None),
        P(("seq", "head"), None),
        P(("seq", "head"), None),
        P(),
        P(),
        P(),
        P(("seq", "head"), None),
        P(None, "head"),
        P(None, "head"),
        P(None, "head"),
        P(None, "head"),
    )
    return jax.shard_map(
        pick(mesh),
        mesh=mesh,
        in_specs=placed,
        out_specs=(
            P(("seq", "head"), None),
            P(("seq", "head"), None),
            P(("seq", "head"), None),
            P("seq", "head"),
            P("seq", "head"),
            P("seq", "head"),
            P(),
            P(),
            P(),
        ),
        check_vma=False,
    )
```

```python
import functools
import math

import jax
import jax.numpy as jnp
from jax import lax
from jax.experimental import pallas as pl
from jax.experimental.pallas import tpu as pltpu
from jax.sharding import PartitionSpec as P

HEAD_SIZE = 128
QMAX = 127


unscale = 0.0078125


def split_heads(rows):
    return rows.reshape(rows.shape[0], rows.shape[1] // HEAD_SIZE, HEAD_SIZE)


def join_heads(heads):
    return heads.reshape(heads.shape[0], heads.shape[1] * heads.shape[2])


def head_scores(queries, key_rows):
    return jnp.einsum(
        "qhd,khd->hqk", queries, key_rows, preferred_element_type=jnp.float32
    ) * HEAD_SIZE ** (-0.5)


def over_keys(step_fn, initial, key_rows, value_rows):
    block_rows = math.gcd(key_rows.shape[0], 2048)

    def over_one_turn(turn_index, carried):
        key_block = lax.dynamic_slice_in_dim(key_rows, turn_index * block_rows, block_rows, 0)
        value_block = lax.dynamic_slice_in_dim(value_rows, turn_index * block_rows, block_rows, 0)
        return step_fn(carried, key_block, value_block)

    return lax.fori_loop(0, key_rows.shape[0] // block_rows, over_one_turn, initial)


def key_terms(carried, queries, grads, log_rows, delta_rows, own_keys, own_values):
    key_grad, value_grad = carried
    probs = jnp.exp(head_scores(queries, own_keys) - log_rows.T[:, :, None])
    dprobs = jnp.einsum("qhd,khd->hqk", grads, own_values, preferred_element_type=jnp.float32)
    dscores = (probs * (dprobs - delta_rows.T[:, :, None])).astype(jnp.bfloat16)
    value_grad = value_grad + jnp.einsum(
        "hqk,qhd->khd", probs.astype(jnp.bfloat16), grads, preferred_element_type=jnp.float32
    )
    key_grad = key_grad + jnp.einsum(
        "hqk,qhd->khd", dscores, queries, preferred_element_type=jnp.float32
    ) * HEAD_SIZE ** (-0.5)
    return (key_grad, value_grad)


def on_device(
    image_input_rows,
    adapter_down_weight,
    adapter_up_weight,
    image_query_rows,
    image_key_rows,
    image_value_codes,
    value_fraction,
    value_step_sizes,
    timestep_group,
    timestep,
    image_output_grad,
    text_query_rows,
    text_key_rows,
    text_value_rows,
    text_output_grad,
):
    slot_index = jnp.sum(
        jnp.where(
            jnp.arange(timestep_group.shape[0], dtype=jnp.int32) == timestep[0], timestep_group, 0
        )
    )
    slot_rows = jnp.arange(value_step_sizes.shape[0], dtype=jnp.int32) == slot_index
    step_row = jnp.sum(jnp.where(slot_rows[:, None], value_step_sizes, 0.0), axis=0)
    code_values = image_value_codes.astype(jnp.float32)
    v_dequant = (code_values * jnp.repeat(step_row, HEAD_SIZE)[None, :]).astype(jnp.bfloat16)
    inside = jnp.abs(image_value_codes) < QMAX
    lsq_term = jnp.where(inside, -value_fraction.astype(jnp.float32), code_values)
    query_img, key_img, value_img, grad_img = (
        lax.all_to_all(image_query_rows, "head", split_axis=1, concat_axis=0, tiled=True),
        lax.all_to_all(image_key_rows, "head", split_axis=1, concat_axis=0, tiled=True),
        lax.all_to_all(v_dequant, "head", split_axis=1, concat_axis=0, tiled=True),
        lax.all_to_all(image_output_grad, "head", split_axis=1, concat_axis=0, tiled=True),
    )
    share_rows = text_query_rows.shape[0] // lax.axis_size("seq")
    first_row = lax.axis_index("seq") * share_rows

    def own_rows(table):
        return lax.dynamic_slice_in_dim(table, first_row, share_rows, 0)

    image_rows = query_img.shape[0]
    query_local = jnp.concatenate([query_img, own_rows(text_query_rows)], axis=0)
    grad_local = jnp.concatenate([grad_img, own_rows(text_output_grad)], axis=0)
    query_split = split_heads(query_local)
    grad_split = split_heads(grad_local)
    local_count = query_split.shape[0]
    head_count = query_split.shape[1]
    key_image, value_image = (
        lax.all_gather(key_img, "seq", axis=0, tiled=True),
        lax.all_gather(value_img, "seq", axis=0, tiled=True),
    )
    text_keys = split_heads(text_key_rows)
    text_values = split_heads(text_value_rows)
    key_sets = ((split_heads(key_image), split_heads(value_image)), (text_keys, text_values))

    def stat_turn(carried, key_block, value_block):
        row_max, running, weighted = carried
        scores = head_scores(query_split, key_block)
        dprobs = jnp.einsum(
            "qhd,khd->hqk", grad_split, value_block, preferred_element_type=jnp.float32
        )
        new_max = jnp.maximum(row_max, jnp.max(scores, axis=2, keepdims=True))
        factor = jnp.exp(row_max - new_max)
        expo = jnp.exp(scores - new_max)
        running = running * factor + jnp.sum(expo, axis=2, keepdims=True)
        weighted = weighted * factor + jnp.sum(expo * dprobs, axis=2, keepdims=True)
        return (new_max, running, weighted)

    row_stats = (
        jnp.full((head_count, local_count, 1), -jnp.inf, jnp.float32),
        jnp.zeros((head_count, local_count, 1), jnp.float32),
        jnp.zeros((head_count, local_count, 1), jnp.float32),
    )
    for key_rows, value_rows in key_sets:
        row_stats = over_keys(stat_turn, row_stats, key_rows, value_rows)
    log_sums = row_stats[0] + jnp.log(row_stats[1])
    deltas = row_stats[2] / row_stats[1]

    def query_turn(running, key_block, value_block):
        probs = jnp.exp(head_scores(query_split, key_block) - log_sums)
        dprobs = jnp.einsum(
            "qhd,khd->hqk", grad_split, value_block, preferred_element_type=jnp.float32
        )
        dscores = (probs * (dprobs - deltas)).astype(jnp.bfloat16)
        return running + jnp.einsum(
            "hqk,khd->qhd", dscores, key_block, preferred_element_type=jnp.float32
        ) * HEAD_SIZE ** (-0.5)

    query_grad = jnp.zeros((local_count, head_count, HEAD_SIZE), jnp.float32)
    for key_rows, value_rows in key_sets:
        query_grad = over_keys(query_turn, query_grad, key_rows, value_rows)
    query_grad = join_heads(query_grad).astype(jnp.bfloat16)
    log_rows = log_sums[:, :, 0].T
    delta_rows = deltas[:, :, 0].T
    own_keys = split_heads(key_img)
    own_values = split_heads(value_img)
    empty = jnp.zeros(own_keys.shape, jnp.float32)
    query_rows = lax.all_gather(query_local.astype(jnp.float32), "seq", axis=0, tiled=True).astype(
        jnp.bfloat16
    )
    grad_rows = lax.all_gather(grad_local.astype(jnp.float32), "seq", axis=0, tiled=True).astype(
        jnp.bfloat16
    )
    log_part = lax.all_gather(log_rows, "seq", axis=0, tiled=True)
    delta_part = lax.all_gather(delta_rows, "seq", axis=0, tiled=True)
    piece_rows = query_rows.shape[0]
    block_rows = piece_rows if piece_rows <= 2048 else math.gcd(piece_rows, 2048)

    def fold_one_turn(turn_index, running):

        def rows_of(table):
            return lax.dynamic_slice_in_dim(table, turn_index * block_rows, block_rows, 0)

        return key_terms(
            running,
            split_heads(rows_of(query_rows)),
            split_heads(rows_of(grad_rows)),
            rows_of(log_part),
            rows_of(delta_part),
            own_keys,
            own_values,
        )

    key_grad, value_grad = lax.fori_loop(0, piece_rows // block_rows, fold_one_turn, (empty, empty))
    key_grad = join_heads(key_grad).astype(jnp.bfloat16)
    value_grad = join_heads(value_grad).astype(jnp.bfloat16)
    text_empty = jnp.zeros(text_keys.shape, jnp.float32)
    text_key, text_value = key_terms(
        (text_empty, text_empty),
        query_split,
        grad_split,
        log_rows,
        delta_rows,
        text_keys,
        text_values,
    )
    text_key, text_value = (
        lax.psum_scatter(join_heads(text_key), "seq", scatter_dimension=0, tiled=True),
        lax.psum_scatter(join_heads(text_value), "seq", scatter_dimension=0, tiled=True),
    )
    dk_txt = text_key.astype(jnp.bfloat16)
    dv_txt = text_value.astype(jnp.bfloat16)
    dq_txt = query_grad[image_rows:]
    dq_heads = query_grad[:image_rows]
    dq_img, dk_img, dv_quant = (
        lax.all_to_all(dq_heads, "head", split_axis=0, concat_axis=1, tiled=True),
        lax.all_to_all(key_grad, "head", split_axis=0, concat_axis=1, tiled=True),
        lax.all_to_all(value_grad, "head", split_axis=0, concat_axis=1, tiled=True),
    )
    image_value_grad = jnp.where(inside, dv_quant, jnp.zeros_like(dv_quant))
    lowrank_gradient = jnp.einsum(
        "vg,zg->vz", image_value_grad, adapter_up_weight, preferred_element_type=jnp.float32
    ).astype(jnp.bfloat16)
    part_down = jnp.einsum(
        "td,tr->dr", image_input_rows, lowrank_gradient, preferred_element_type=jnp.float32
    )
    lowrank_input = jnp.dot(
        image_input_rows, adapter_down_weight, preferred_element_type=jnp.float32
    ).astype(jnp.bfloat16)
    part_up = jnp.einsum(
        "tr,tw->rw", lowrank_input, image_value_grad, preferred_element_type=jnp.float32
    )
    token_rows = dv_quant.shape[0]
    token_terms = (dv_quant.astype(jnp.float32) * lsq_term).reshape(
        token_rows, value_step_sizes.shape[1], HEAD_SIZE
    )
    total_down, total_up, step_sums = lax.psum(
        (part_down, part_up, jnp.sum(token_terms, axis=(0, 2))), ("seq", "head")
    )
    grad_steps = jnp.where(slot_rows[:, None], step_sums[None, :], 0.0) * (QMAX ** (-0.5) * unscale)
    return (
        dq_img,
        dk_img,
        image_value_grad,
        dq_txt,
        dk_txt,
        dv_txt,
        total_down * unscale,
        total_up * unscale,
        grad_steps,
    )


MESH = pl.DeviceIdType.MESH
BF = jnp.bfloat16
F32 = jnp.float32
NT = (((1,), (1,)), ((), ()))
NN = (((1,), (0,)), ((), ()))


def dot(left, right, dims=NN):
    return lax.dot_general(left, right, dims, preferred_element_type=F32)


def attention_kernel(
    seq,
    head,
    q_in,
    k_in,
    code_in,
    do_in,
    tq_in,
    tk_in,
    tv_in,
    tdo_in,
    x_in,
    frac_in,
    up_in,
    down_in,
    step_ref,
    group_ref,
    time_ref,
    dq_ref,
    dk_ref,
    dv_ref,
    dqt_ref,
    dkt_ref,
    dvt_ref,
    down_ref,
    up_ref,
    steps_ref,
    q_ref,
    k_ref,
    code_ref,
    do_ref,
    x_ref,
    frac_ref,
    upw_ref,
    downw_ref,
    stage,
    recv,
    kv2,
    tkv,
    tqd,
    kall,
    ktr,
    vall,
    qall,
    doall,
    dqall,
    dkacc,
    dvacc,
    xo,
    xi,
    to,
    ti,
    ost,
    ret,
    tfin,
    rett,
    xlow_out,
    xlow_in,
    xst,
    xcol,
    up_out,
    up_in2,
    up_all,
    low_out,
    low_in,
    red_out,
    red_in,
    gath,
    li,
    s1,
    r1,
    s2,
    r2,
    st,
    rt,
    s3,
    r3,
    s4,
    r4,
    s5,
    r5,
    s6,
    r6,
    s7,
    r7,
    s8,
    r8,
    s9,
    r9,
    s10,
    r10,
    s11,
    r11,
    s12,
    r12,
):
    rows = q_ref.shape[0]
    heads = q_ref.shape[1] // HEAD_SIZE
    text = tq_in.shape[0]
    half = text // 2
    planes = head // 2
    peers = seq * planes
    group = tq_in.shape[1] // HEAD_SIZE
    pair = 2 * group
    first = (seq - pair) // 2
    image = peers * rows
    share = text // seq
    scale = HEAD_SIZE ** (-0.5)
    rank = upw_ref.shape[0]
    wide = x_ref.shape[1] // seq
    part = rank // head
    hrank = rank // 2
    hrows = rows // 2

    s = lax.axis_index("seq")
    g = lax.axis_index("head")
    c = lax.rem(g, 2)
    y = g // 2
    me = s * planes + y
    partner = (s, g + 1 - 2 * c)
    slot = s - first
    is_head = jnp.logical_and(slot >= 0, slot < pair)
    mine = y * pair + slot
    holds_text = jnp.logical_and(is_head, slot // group == c)
    takes_text = jnp.logical_and(is_head, slot // group != c)
    lane_block = lax.rem(slot, group)

    def peer(p):
        return (p // planes, lax.rem(p, planes) * 2 + c)

    def home(h):
        return (first + lax.rem(h, pair), (h // pair) * 2 + c)

    def home_peer(h):
        return (first + lax.rem(h, pair)) * planes + h // pair

    def send(src, dst, ssem, rsem, to_id):
        return pltpu.make_async_remote_copy(
            src_ref=src, dst_ref=dst, send_sem=ssem, recv_sem=rsem, device_id=to_id, device_id_type=MESH
        )

    loads = [
        pltpu.make_async_copy(src, dst, li.at[i])
        for i, (src, dst) in enumerate(
            (
                (k_in, k_ref),
                (code_in, code_ref),
                (q_in, q_ref),
                (do_in, do_ref),
                (x_in, x_ref),
                (down_in, downw_ref),
                (up_in, upw_ref),
                (frac_in, frac_ref),
            )
        )
    ]
    for load in loads:
        load.start()

    barrier = pltpu.get_barrier_semaphore()
    for i in range(1, peers):
        pl.semaphore_signal(
            barrier, inc=1, device_id=peer(lax.rem(me + i, peers)), device_id_type=MESH
        )
    for other in range(planes):
        pl.semaphore_signal(
            barrier, inc=1, device_id=(s, other * 2 + 1 - c), device_id_type=MESH
        )

    for load in loads[:4]:
        load.wait()
    for h in range(heads):
        cols = slice(h * HEAD_SIZE, (h + 1) * HEAD_SIZE)
        stage[h, 0:rows] = k_ref[:, cols]
        stage[h, rows : 2 * rows] = code_ref[:, cols].astype(F32).astype(BF)
        stage[h, 2 * rows : 3 * rows] = q_ref[:, cols]
        stage[h, 3 * rows : 4 * rows] = do_ref[:, cols]

    pl.semaphore_wait(barrier, peers - 1 + planes)

    def first_send(h, k):
        at = pl.ds(k * 2 * rows, 2 * rows)
        return send(stage.at[h, at], recv.at[me, at], s1.at[k, h], r1.at[k, me], home(h))

    def first_recv(p, k):
        at = pl.ds(k * 2 * rows, 2 * rows)
        return send(stage.at[0, at], recv.at[p, at], s1.at[k, 0], r1.at[k, p], partner)

    for k in range(2):
        for i in range(heads):
            h = lax.rem(me + i, heads)

            @pl.when(me != home_peer(h))
            def _():
                first_send(h, k).start()

    def text_sources():
        cols = pl.ds(pl.multiple_of(lane_block * HEAD_SIZE, HEAD_SIZE), HEAD_SIZE)
        return cols, pl.ds(0, half), pl.ds(half, half)

    def text_copies():
        cols, _, low = text_sources()
        return (
            send(tk_in.at[:, cols], tkv.at[0], st.at[0], rt.at[0], partner),
            send(tv_in.at[:, cols], tkv.at[1], st.at[1], rt.at[1], partner),
            send(tq_in.at[low, cols], tqd.at[0], st.at[2], rt.at[2], partner),
            send(tdo_in.at[low, cols], tqd.at[1], st.at[3], rt.at[3], partner),
        )

    def text_loads():
        cols, high, _ = text_sources()
        return (
            pltpu.make_async_copy(tk_in.at[:, cols], tkv.at[0], li.at[8]),
            pltpu.make_async_copy(tv_in.at[:, cols], tkv.at[1], li.at[9]),
            pltpu.make_async_copy(tq_in.at[high, cols], tqd.at[0], li.at[10]),
            pltpu.make_async_copy(tdo_in.at[high, cols], tqd.at[1], li.at[11]),
        )

    @pl.when(holds_text)
    def _():
        for copy in text_copies() + text_loads():
            copy.start()

    for load in loads[4:6]:
        load.wait()
    for t in range(seq):
        xst[t] = x_ref[:, t * wide : (t + 1) * wide]

    def column_send(t):
        return send(xst.at[t], xcol.at[s], s6.at[t], r6.at[s], (t, g))

    xlow = dot(x_ref[...], downw_ref[...], NT)
    xlow_out[...] = jnp.concatenate([xlow[0:hrows], xlow[hrows:rows]], axis=1).astype(BF)

    def low_send(h):
        return send(xlow_out, xlow_in.at[me], s7.at[h], r7.at[me], home(h))

    for i in range(heads):
        h = lax.rem(me + i, heads)

        @pl.when(me != home_peer(h))
        def _():
            low_send(h).start()

    for load in loads[6:8]:
        load.wait()

    def up_send(p):
        return send(
            up_out.at[c], up_all.at[mine, c], s9.at[p], r9.at[mine], peer(p)
        )

    def column_sends():
        for i in range(1, seq):
            column_send(lax.rem(s + i, seq)).start()
        xcol[pl.ds(s, 1)] = xst[pl.ds(s, 1)]

    @pl.when(jnp.logical_not(is_head))
    def _():
        column_sends()

    def up_trade():
        return send(up_in2.at[0, 1 - c], up_in2.at[1, 0], s8.at[0], r8.at[0], partner)

    def text_trade():
        return send(to, ti, s3.at[2], r3.at[2], partner)

    def back_query(p):
        return send(
            dqall.at[pl.ds(pl.multiple_of(p * rows, rows), rows)], ret.at[mine, pl.ds(0, rows)],
            s4.at[0, p], r4.at[0, mine], peer(p)
        )

    def back_send(k, p):
        at = pl.ds(k * rows, rows)
        return send(ost.at[p, at], ret.at[mine, at], s4.at[k, p], r4.at[k, mine], peer(p))

    def back_recv(k, h):
        at = pl.ds(k * rows, rows)
        return send(ost.at[0, at], ret.at[h, at], s4.at[k, 0], r4.at[k, h], partner)

    def trade(k):
        return send(xo.at[k], xi.at[k], s3.at[k], r3.at[k], partner)

    @pl.when(is_head)
    def _():
        recv[pl.ds(me, 1)] = stage[pl.ds(mine, 1)]
        xlow_in[pl.ds(me, 1)] = xlow_out[...].reshape(1, hrows, HEAD_SIZE)
        for p in range(peers):

            @pl.when(me != p)
            def _():
                first_recv(p, 0).wait_recv()

        swap = send(recv.at[:, pl.ds(0, 2 * rows)], kv2, s2.at[0], r2.at[0], partner)
        swap.start()
        step = step_ref[group_ref[time_ref[0]], mine]

        def dequant(codes):
            return (codes.reshape(image, HEAD_SIZE).astype(F32) * step).astype(BF)

        kall[0:image] = recv[:, 0:rows].reshape(image, HEAD_SIZE)
        vall[0:image] = dequant(recv[:, rows : 2 * rows])
        for p in range(peers):

            @pl.when(me != p)
            def _():
                first_recv(p, 1).wait_recv()

        column_sends()
        qall[0:image] = recv[:, 2 * rows : 3 * rows].reshape(image, HEAD_SIZE)
        doall[0:image] = recv[:, 3 * rows : 4 * rows].reshape(image, HEAD_SIZE)

        @pl.when(takes_text)
        def _():
            for copy in text_copies():
                copy.wait_recv()

        @pl.when(holds_text)
        def _():
            for copy in text_loads():
                copy.wait()

        kall[2 * image : 2 * image + text] = tkv[0]
        vall[2 * image : 2 * image + text] = tkv[1]
        qall[image : image + half] = tqd[0]
        doall[image : image + half] = tqd[1]
        swap.wait_recv()
        kall[image : 2 * image] = kv2[:, 0:rows].reshape(image, HEAD_SIZE)
        vall[image : 2 * image] = dequant(kv2[:, rows : 2 * rows])
        ktr[...] = kall[...].T
        dkacc[...] = jnp.zeros_like(dkacc)
        dvacc[...] = jnp.zeros_like(dvacc)

        def query_block(index, carried):
            at = pl.ds(pl.multiple_of(index * half, half), half)
            queries, grads = qall[at], doall[at]
            scores = dot(kall[...], queries, NT)
            top = jnp.max(scores, axis=0, keepdims=True) * (scale * math.log2(math.e))
            expo = jnp.exp2(scores * (scale * math.log2(math.e)) - top)
            probs = expo * (1.0 / jnp.sum(expo, axis=0, keepdims=True))
            dvacc[...] += dot(probs.astype(BF), grads)
            dprobs = dot(vall[...], grads, NT)
            deltas = jnp.sum(probs * dprobs, axis=0, keepdims=True)
            dscores = (probs * (dprobs - deltas)).astype(BF)
            dkacc[...] += dot(dscores, queries)
            dqall[at] = (dot(ktr[...], dscores).T * scale).astype(BF)

            @pl.when(index < image // half)
            def _():
                for i in range(half // rows):
                    p = index * (half // rows) + i

                    @pl.when(p != me)
                    def _():
                        back_query(p).start()

            return carried

        lax.fori_loop(0, (image + half) // half, query_block, 0)
        xo[1] = dvacc[image : 2 * image].astype(BF)
        trade(1).start()
        xo[0] = (dkacc[image : 2 * image] * scale).astype(BF)
        trade(0).start()
        trade(1).wait_recv()
        ost[:, 2 * rows : 3 * rows] = (
            (dvacc[0:image] + xi[1].astype(F32)).astype(BF).reshape(peers, rows, HEAD_SIZE)
        )
        for i in range(1, peers):
            back_send(2, lax.rem(me + i, peers)).start()
        trade(0).wait_recv()
        ost[:, rows : 2 * rows] = (
            (dkacc[0:image] * scale + xi[0].astype(F32)).astype(BF).reshape(peers, rows, HEAD_SIZE)
        )
        for i in range(1, peers):
            back_send(1, lax.rem(me + i, peers)).start()
        ret[pl.ds(mine, 1), rows : 3 * rows] = ost[pl.ds(me, 1), rows : 3 * rows]
        ret[pl.ds(mine, 1), 0:rows] = dqall[pl.ds(pl.multiple_of(me * rows, rows), rows)].reshape(
            1, rows, HEAD_SIZE
        )

        @pl.when(takes_text)
        def _():
            to[0:text] = (dkacc[2 * image : 2 * image + text] * scale).astype(BF)
            to[text : 2 * text] = dvacc[2 * image : 2 * image + text].astype(BF)
            to[2 * text : 2 * text + half] = dqall[image : image + half]
            text_trade().start()

        for p in range(peers):

            @pl.when(me != p)
            def _():
                send(xlow_out, xlow_in.at[p], s7.at[0], r7.at[p], partner).wait_recv()

        codes = recv[:, rows : 2 * rows]
        kept = jnp.where(jnp.abs(codes.astype(F32)) < QMAX, ost[:, 2 * rows : 3 * rows].astype(F32), 0.0)
        kept = kept.astype(BF)
        low_rows = xlow_in[...].reshape(peers * hrows, HEAD_SIZE).T
        early = dot(low_rows, kept[:, 0:hrows].reshape(peers * hrows, HEAD_SIZE))
        late = dot(low_rows, kept[:, hrows:rows].reshape(peers * hrows, HEAD_SIZE))
        part_up = (early[0:rank] + late[rank : 2 * rank]).reshape(2, hrank, HEAD_SIZE)
        up_in2[0] = part_up
        up_trade().start()

    low = jnp.zeros((rows, rank), F32)
    sums = []
    for h in range(heads):

        @pl.when(me != home_peer(h))
        def _():
            back_recv(2, h).wait_recv()

        cols = slice(h * HEAD_SIZE, (h + 1) * HEAD_SIZE)
        codes = code_ref[:, cols]
        inside = jnp.abs(codes) < QMAX
        value_grad = ret[h, 2 * rows : 3 * rows].astype(F32)
        kept = jnp.where(inside, value_grad, 0.0).astype(BF)
        lsq_term = jnp.where(inside, -frac_ref[:, cols].astype(F32), codes.astype(F32))
        sums.append(jnp.sum(value_grad * lsq_term, axis=0, keepdims=True))
        low = low + dot(kept, upw_ref[:, cols], NT)
        dv_ref[:, cols] = kept

    sums.append(jnp.zeros((rows - heads, HEAD_SIZE), F32))
    step_terms = jnp.sum(jnp.concatenate(sums, axis=0), axis=1, keepdims=True)
    step_high = step_terms.astype(BF).astype(F32)
    lane_at = lax.broadcasted_iota(jnp.int32, (rows, rank), 1)
    beside = jnp.where(lane_at == 0, step_high, jnp.where(lane_at == 1, step_terms - step_high, 0.0))
    low_out[...] = jnp.concatenate([low, beside], axis=1).astype(BF)

    def tile_send(t):
        return send(low_out, low_in.at[s], s10.at[t], r10.at[s], (t, g))

    for i in range(1, seq):
        tile_send(lax.rem(s + i, seq)).start()
    low_in[pl.ds(s, 1)] = low_out[...].reshape(1, rows, HEAD_SIZE)

    @pl.when(is_head)
    def _():
        @pl.when(holds_text)
        def _():
            text_trade().wait_recv()
            full = (seq, share, HEAD_SIZE)
            tfin[0 : seq // 2, 0] = dqall[image : image + half].reshape(seq // 2, share, HEAD_SIZE)
            tfin[seq // 2 : seq, 0] = ti[2 * text : 2 * text + half].reshape(seq // 2, share, HEAD_SIZE)
            tfin[:, 1] = (
                (dkacc[2 * image : 2 * image + text] * scale + ti[0:text].astype(F32)).astype(BF).reshape(full)
            )
            tfin[:, 2] = (
                (dvacc[2 * image : 2 * image + text] + ti[text : 2 * text].astype(F32)).astype(BF).reshape(full)
            )
            for i in range(1, seq):
                other = lax.rem(s + i, seq)
                send(
                    tfin.at[other], rett.at[lane_block], s5.at[other], r5.at[lane_block], (other, g)
                ).start()

            rett[pl.ds(lane_block, 1)] = tfin[pl.ds(s, 1)]

        up_trade().wait_recv()
        up_out[pl.ds(c, 1)] = (
            (up_in2[pl.ds(0, 1), pl.ds(c, 1)] + up_in2[pl.ds(1, 1), pl.ds(0, 1)]) * unscale
        ).astype(BF).reshape(1, hrank, HEAD_SIZE)
        for i in range(1, peers):
            up_send(lax.rem(me + i, peers)).start()
        up_all[pl.ds(mine, 1), pl.ds(c, 1)] = up_out[pl.ds(c, 1)].reshape(1, 1, hrank, HEAD_SIZE)

    for t in range(seq):

        @pl.when(s != t)
        def _():
            send(xst.at[0], xcol.at[t], s6.at[0], r6.at[t], partner).wait_recv()
            send(low_out, low_in.at[t], s10.at[0], r10.at[t], partner).wait_recv()

    tiles = low_in[...]
    flat = tiles.reshape(seq * rows, HEAD_SIZE).T
    block = dot(flat, xcol[...].reshape(seq * rows, wide))[0:rank]
    step_group = jnp.sum(tiles[:, 0:16].astype(F32), axis=0)
    for other in range(head):
        red_out[other, 0:part] = block[other * part : (other + 1) * part]
        red_out[other, part : part + 16, 0:HEAD_SIZE] = step_group
        red_out[other, part : part + 16, HEAD_SIZE:wide] = jnp.zeros((16, wide - HEAD_SIZE), F32)

    def reduce_send(other):
        return send(red_out.at[other], red_in.at[g], s11.at[other], r11.at[g], (s, other))

    for i in range(1, head):
        reduce_send(lax.rem(g + i, head)).start()
    red_in[pl.ds(g, 1)] = red_out[pl.ds(g, 1)]
    for other in range(head):

        @pl.when(g != other)
        def _():
            send(red_out.at[0], red_in.at[other], s11.at[0], r11.at[other], partner).wait_recv()

    summed = jnp.sum(red_in[...], axis=0)
    gath[pl.ds(y, 1), pl.ds(c, 1), pl.ds(s, 1)] = (
        (summed[0:part] * unscale).astype(BF).reshape(1, 1, 1, part, wide)
    )

    def row_send(p):
        return send(gath.at[y, c, s], gath.at[y, c, s], s12.at[p], r12.at[me], peer(p))

    def core_send():
        return send(gath.at[:, c], gath.at[:, c], s12.at[peers], r12.at[peers], partner)

    def core_up_send():
        return send(up_all.at[:, c], up_all.at[:, c], s8.at[1], r8.at[1], partner)

    for i in range(1, peers):
        row_send(lax.rem(me + i, peers)).start()

    for j in range(group):

        @pl.when(s != first + c * group + j)
        def _():
            send(tfin.at[0], rett.at[j], s5.at[0], r5.at[j], partner).wait_recv()

        cols = slice(j * HEAD_SIZE, (j + 1) * HEAD_SIZE)
        dqt_ref[:, cols] = rett[j, 0]
        dkt_ref[:, cols] = rett[j, 1]
        dvt_ref[:, cols] = rett[j, 2]

    for h in range(heads):

        @pl.when(me != home_peer(h))
        def _():
            back_recv(0, h).wait_recv()
            back_recv(1, h).wait_recv()

        cols = slice(h * HEAD_SIZE, (h + 1) * HEAD_SIZE)
        dq_ref[:, cols] = ret[h, 0:rows]
        dk_ref[:, cols] = ret[h, rows : 2 * rows]

    slot_index = group_ref[time_ref[0]]
    lanes = summed[part : part + 16, 0:HEAD_SIZE]
    lane_at = lax.broadcasted_iota(jnp.int32, (16, HEAD_SIZE), 1)
    row_at = lax.broadcasted_iota(jnp.int32, (16, HEAD_SIZE), 0)
    chosen = jnp.logical_or(lane_at == rank, lane_at == rank + 1)
    head_sums = jnp.sum(jnp.where(chosen, lanes, 0.0), axis=1, keepdims=True)
    step_row = jnp.sum(jnp.where(lane_at == row_at, head_sums, 0.0), axis=0, keepdims=True)[:, 0:heads]
    step_row = step_row * (QMAX ** (-0.5) * unscale)
    slots = steps_ref.shape[0]
    slot_at = lax.broadcasted_iota(jnp.int32, (slots, heads), 0)
    steps_ref[...] = jnp.where(slot_at == slot_index, jnp.broadcast_to(step_row, (slots, heads)), 0.0)

    for h in range(heads):

        @pl.when(me != home_peer(h))
        def _():
            send(up_out.at[0], up_all.at[h, c], s9.at[0], r9.at[h], partner).wait_recv()

    core_up_send().start()

    for p in range(peers):

        @pl.when(me != p)
        def _():
            block_at = gath.at[p % planes, c, p // planes]
            send(block_at, block_at, s12.at[0], r12.at[p], partner).wait_recv()

    core_send().start()
    send(up_all.at[:, 1 - c], up_all.at[:, 1 - c], s8.at[1], r8.at[1], partner).wait_recv()
    for h in range(heads):
        cols = slice(h * HEAD_SIZE, (h + 1) * HEAD_SIZE)
        up_ref[:, cols] = up_all[h].reshape(rank, HEAD_SIZE).astype(F32)
    send(gath.at[:, 1 - c], gath.at[:, 1 - c], s12.at[peers], r12.at[peers], partner).wait_recv()
    for t in range(seq):
        down_ref[:, t * wide : (t + 1) * wide] = gath[:, :, t].reshape(rank, wide).astype(F32)

    for h in range(heads):

        @pl.when(me != home_peer(h))
        def _():
            first_send(h, 0).wait_send()
            first_send(h, 1).wait_send()
            low_send(h).wait_send()

    for i in range(1, seq):
        t = lax.rem(s + i, seq)
        column_send(t).wait_send()
        tile_send(t).wait_send()
    for i in range(1, head):
        reduce_send(lax.rem(g + i, head)).wait_send()
    for i in range(1, peers):
        row_send(lax.rem(me + i, peers)).wait_send()
    core_send().wait_send()
    core_up_send().wait_send()

    @pl.when(is_head)
    def _():
        send(recv.at[:, pl.ds(0, 2 * rows)], kv2, s2.at[0], r2.at[0], partner).wait_send()
        trade(0).wait_send()
        trade(1).wait_send()
        up_trade().wait_send()
        for i in range(1, peers):
            p = lax.rem(me + i, peers)
            back_query(p).wait_send()
            back_send(1, p).wait_send()
            back_send(2, p).wait_send()
            up_send(p).wait_send()

    @pl.when(takes_text)
    def _():
        text_trade().wait_send()

    @pl.when(holds_text)
    def _():
        for copy in text_copies():
            copy.wait_send()
        for i in range(1, seq):
            other = lax.rem(s + i, seq)
            send(
                tfin.at[other], rett.at[lane_block], s5.at[other], r5.at[lane_block], (other, g)
            ).wait_send()


def settle_kernel(count, *refs):
    sources, targets, done = refs[:count], refs[count : 2 * count], refs[2 * count]
    copies = [
        pltpu.make_async_copy(source, target, done.at[i])
        for i, (source, target) in enumerate(zip(sources, targets))
    ]
    for copy in copies:
        copy.start()
    for copy in copies:
        copy.wait()


def settle(arrays):
    count = len(arrays)
    anywhere = pl.BlockSpec(memory_space=pl.ANY)
    return pl.pallas_call(
        functools.partial(settle_kernel, count),
        out_shape=[jax.ShapeDtypeStruct(a.shape, a.dtype) for a in arrays],
        in_specs=[anywhere] * count,
        out_specs=[anywhere] * count,
        scratch_shapes=[pltpu.SemaphoreType.DMA((count,))],
        name="settle",
    )(*arrays)


def whole_heads(
    seq,
    head,
    image_input_rows,
    adapter_down_weight,
    adapter_up_weight,
    image_query_rows,
    image_key_rows,
    image_value_codes,
    value_fraction,
    value_step_sizes,
    timestep_group,
    timestep,
    image_output_grad,
    text_query_rows,
    text_key_rows,
    text_value_rows,
    text_output_grad,
):
    rows, width = image_query_rows.shape
    text, text_width = text_query_rows.shape
    heads, group = width // HEAD_SIZE, text_width // HEAD_SIZE
    peers = seq * head // 2
    image, share = peers * rows, text // seq
    keys = 2 * image + text
    rank, wide = adapter_up_weight.shape[0], image_input_rows.shape[1] // seq
    planes = head // 2
    vmem = pl.BlockSpec(memory_space=pltpu.VMEM)
    sems = pltpu.SemaphoreType.DMA
    hbm = pl.BlockSpec(memory_space=pl.ANY)
    smem = pl.BlockSpec(memory_space=pltpu.SMEM)
    results = pl.pallas_call(
        functools.partial(attention_kernel, seq, head),
        out_shape=[jax.ShapeDtypeStruct((rows, width), BF)] * 3
        + [jax.ShapeDtypeStruct((share, text_width), BF)] * 3
        + [
            jax.ShapeDtypeStruct(adapter_down_weight.shape[::-1], F32),
            jax.ShapeDtypeStruct(adapter_up_weight.shape, F32),
            jax.ShapeDtypeStruct(value_step_sizes.shape, F32),
        ],
        in_specs=[hbm] * 12 + [smem] * 3,
        out_specs=[vmem] * 9,
        scratch_shapes=[
            pltpu.VMEM((rows, width), BF),
            pltpu.VMEM((rows, width), BF),
            pltpu.VMEM((rows, width), jnp.int32),
            pltpu.VMEM((rows, width), BF),
            pltpu.VMEM(image_input_rows.shape, BF),
            pltpu.VMEM((rows, width), BF),
            pltpu.VMEM(adapter_up_weight.shape, BF),
            pltpu.VMEM(adapter_down_weight.shape[::-1], BF),
            pltpu.VMEM((heads, 4 * rows, HEAD_SIZE), BF),
            pltpu.VMEM((peers, 4 * rows, HEAD_SIZE), BF),
            pltpu.VMEM((peers, 2 * rows, HEAD_SIZE), BF),
            pltpu.VMEM((2, text, HEAD_SIZE), BF),
            pltpu.VMEM((2, text // 2, HEAD_SIZE), BF),
            pltpu.VMEM((keys, HEAD_SIZE), BF),
            pltpu.VMEM((HEAD_SIZE, keys), BF),
            pltpu.VMEM((keys, HEAD_SIZE), BF),
            pltpu.VMEM((image + text // 2, HEAD_SIZE), BF),
            pltpu.VMEM((image + text // 2, HEAD_SIZE), BF),
            pltpu.VMEM((image + text // 2, HEAD_SIZE), BF),
            pltpu.VMEM((keys, HEAD_SIZE), F32),
            pltpu.VMEM((keys, HEAD_SIZE), F32),
            pltpu.VMEM((2, image, HEAD_SIZE), BF),
            pltpu.VMEM((2, image, HEAD_SIZE), BF),
            pltpu.VMEM((2 * text + text // 2, HEAD_SIZE), BF),
            pltpu.VMEM((2 * text + text // 2, HEAD_SIZE), BF),
            pltpu.VMEM((peers, 3 * rows, HEAD_SIZE), BF),
            pltpu.VMEM((heads, 3 * rows, HEAD_SIZE), BF),
            pltpu.VMEM((seq, 3, share, HEAD_SIZE), BF),
            pltpu.VMEM((group, 3, share, HEAD_SIZE), BF),
            pltpu.VMEM((rows // 2, HEAD_SIZE), BF),
            pltpu.VMEM((peers, rows // 2, HEAD_SIZE), BF),
            pltpu.VMEM((seq, rows, wide), BF),
            pltpu.VMEM((seq, rows, wide), BF),
            pltpu.VMEM((2, rank // 2, HEAD_SIZE), BF),
            pltpu.VMEM((2, 2, rank // 2, HEAD_SIZE), F32),
            pltpu.VMEM((heads, 2, rank // 2, HEAD_SIZE), BF),
            pltpu.VMEM((rows, HEAD_SIZE), BF),
            pltpu.VMEM((seq, rows, HEAD_SIZE), BF),
            pltpu.VMEM((head, rank // head + 16, wide), F32),
            pltpu.VMEM((head, rank // head + 16, wide), F32),
            pltpu.VMEM((planes, 2, seq, rank // head, wide), BF),
            sems((12,)),
            sems((2, heads)),
            sems((2, peers)),
            sems((1,)),
            sems((1,)),
            sems((4,)),
            sems((4,)),
            sems((3,)),
            sems((3,)),
            sems((3, peers)),
            sems((3, heads)),
            sems((seq,)),
            sems((group,)),
            sems((seq,)),
            sems((seq,)),
            sems((heads,)),
            sems((peers,)),
            sems((2,)),
            sems((2,)),
            sems((peers,)),
            sems((heads,)),
            sems((seq,)),
            sems((seq,)),
            sems((head,)),
            sems((head,)),
            sems((peers + 1,)),
            sems((peers + 1,)),
        ],
        compiler_params=pltpu.CompilerParams(
            collective_id=0, has_side_effects=True, vmem_limit_bytes=56 * 1024 * 1024
        ),
        name="whole_heads",
    )(
        image_query_rows,
        image_key_rows,
        image_value_codes,
        image_output_grad,
        text_query_rows,
        text_key_rows,
        text_value_rows,
        text_output_grad,
        image_input_rows,
        value_fraction,
        adapter_up_weight,
        adapter_down_weight.T,
        value_step_sizes,
        timestep_group,
        timestep,
    )
    results = settle(results)
    return (*results[:6], results[6].T, *results[7:])


def pick(mesh):
    seq, head = mesh.shape["seq"], mesh.shape["head"]

    def chosen(*arguments):
        rows, width = arguments[3].shape
        text, text_width = arguments[11].shape
        pair = 2 * text_width // HEAD_SIZE
        fits = (
            head % 2 == 0
            and seq % 2 == 0
            and seq >= pair
            and rows % 32 == 0
            and 2 * arguments[2].shape[0] == HEAD_SIZE
            and width // HEAD_SIZE <= 16
            and (text // 2) % rows == 0
            and (seq * head // 2 * rows) % (text // 2) == 0
            and arguments[2].shape[0] % (16 * head) == 0
            and arguments[0].shape[1] % (seq * HEAD_SIZE) == 0
            and text % (seq * 16) == 0
            and (seq * head // 2 * rows) % (text // 2) == 0
            and (seq * head * rows + text) * HEAD_SIZE <= 1 << 18
        )
        if fits:
            return whole_heads(seq, head, *arguments)
        return on_device(*arguments)

    return chosen


def solution(mesh):
    placed = (
        P(("seq", "head"), None),
        P(),
        P(),
        P(("seq", "head"), None),
        P(("seq", "head"), None),
        P(("seq", "head"), None),
        P(("seq", "head"), None),
        P(),
        P(),
        P(),
        P(("seq", "head"), None),
        P(None, "head"),
        P(None, "head"),
        P(None, "head"),
        P(None, "head"),
    )
    return jax.shard_map(
        pick(mesh),
        mesh=mesh,
        in_specs=placed,
        out_specs=(
            P(("seq", "head"), None),
            P(("seq", "head"), None),
            P(("seq", "head"), None),
            P("seq", "head"),
            P("seq", "head"),
            P("seq", "head"),
            P(),
            P(),
            P(),
        ),
        check_vma=False,
    )
```

```python
import functools
import math

import jax
import jax.numpy as jnp
from jax import lax
from jax.experimental import pallas as pl
from jax.experimental.pallas import tpu as pltpu
from jax.sharding import PartitionSpec as P

HEAD_SIZE = 128
QMAX = 127


unscale = 0.0078125


def split_heads(rows):
    return rows.reshape(rows.shape[0], rows.shape[1] // HEAD_SIZE, HEAD_SIZE)


def join_heads(heads):
    return heads.reshape(heads.shape[0], heads.shape[1] * heads.shape[2])


def head_scores(queries, key_rows):
    return jnp.einsum(
        "qhd,khd->hqk", queries, key_rows, preferred_element_type=jnp.float32
    ) * HEAD_SIZE ** (-0.5)


def over_keys(step_fn, initial, key_rows, value_rows):
    block_rows = math.gcd(key_rows.shape[0], 2048)

    def over_one_turn(turn_index, carried):
        key_block = lax.dynamic_slice_in_dim(key_rows, turn_index * block_rows, block_rows, 0)
        value_block = lax.dynamic_slice_in_dim(value_rows, turn_index * block_rows, block_rows, 0)
        return step_fn(carried, key_block, value_block)

    return lax.fori_loop(0, key_rows.shape[0] // block_rows, over_one_turn, initial)


def key_terms(carried, queries, grads, log_rows, delta_rows, own_keys, own_values):
    key_grad, value_grad = carried
    probs = jnp.exp(head_scores(queries, own_keys) - log_rows.T[:, :, None])
    dprobs = jnp.einsum("qhd,khd->hqk", grads, own_values, preferred_element_type=jnp.float32)
    dscores = (probs * (dprobs - delta_rows.T[:, :, None])).astype(jnp.bfloat16)
    value_grad = value_grad + jnp.einsum(
        "hqk,qhd->khd", probs.astype(jnp.bfloat16), grads, preferred_element_type=jnp.float32
    )
    key_grad = key_grad + jnp.einsum(
        "hqk,qhd->khd", dscores, queries, preferred_element_type=jnp.float32
    ) * HEAD_SIZE ** (-0.5)
    return (key_grad, value_grad)


def on_device(
    image_input_rows,
    adapter_down_weight,
    adapter_up_weight,
    image_query_rows,
    image_key_rows,
    image_value_codes,
    value_fraction,
    value_step_sizes,
    timestep_group,
    timestep,
    image_output_grad,
    text_query_rows,
    text_key_rows,
    text_value_rows,
    text_output_grad,
):
    slot_index = jnp.sum(
        jnp.where(
            jnp.arange(timestep_group.shape[0], dtype=jnp.int32) == timestep[0], timestep_group, 0
        )
    )
    slot_rows = jnp.arange(value_step_sizes.shape[0], dtype=jnp.int32) == slot_index
    step_row = jnp.sum(jnp.where(slot_rows[:, None], value_step_sizes, 0.0), axis=0)
    code_values = image_value_codes.astype(jnp.float32)
    v_dequant = (code_values * jnp.repeat(step_row, HEAD_SIZE)[None, :]).astype(jnp.bfloat16)
    inside = jnp.abs(image_value_codes) < QMAX
    lsq_term = jnp.where(inside, -value_fraction.astype(jnp.float32), code_values)
    query_img, key_img, value_img, grad_img = (
        lax.all_to_all(image_query_rows, "head", split_axis=1, concat_axis=0, tiled=True),
        lax.all_to_all(image_key_rows, "head", split_axis=1, concat_axis=0, tiled=True),
        lax.all_to_all(v_dequant, "head", split_axis=1, concat_axis=0, tiled=True),
        lax.all_to_all(image_output_grad, "head", split_axis=1, concat_axis=0, tiled=True),
    )
    share_rows = text_query_rows.shape[0] // lax.axis_size("seq")
    first_row = lax.axis_index("seq") * share_rows

    def own_rows(table):
        return lax.dynamic_slice_in_dim(table, first_row, share_rows, 0)

    image_rows = query_img.shape[0]
    query_local = jnp.concatenate([query_img, own_rows(text_query_rows)], axis=0)
    grad_local = jnp.concatenate([grad_img, own_rows(text_output_grad)], axis=0)
    query_split = split_heads(query_local)
    grad_split = split_heads(grad_local)
    local_count = query_split.shape[0]
    head_count = query_split.shape[1]
    key_image, value_image = (
        lax.all_gather(key_img, "seq", axis=0, tiled=True),
        lax.all_gather(value_img, "seq", axis=0, tiled=True),
    )
    text_keys = split_heads(text_key_rows)
    text_values = split_heads(text_value_rows)
    key_sets = ((split_heads(key_image), split_heads(value_image)), (text_keys, text_values))

    def stat_turn(carried, key_block, value_block):
        row_max, running, weighted = carried
        scores = head_scores(query_split, key_block)
        dprobs = jnp.einsum(
            "qhd,khd->hqk", grad_split, value_block, preferred_element_type=jnp.float32
        )
        new_max = jnp.maximum(row_max, jnp.max(scores, axis=2, keepdims=True))
        factor = jnp.exp(row_max - new_max)
        expo = jnp.exp(scores - new_max)
        running = running * factor + jnp.sum(expo, axis=2, keepdims=True)
        weighted = weighted * factor + jnp.sum(expo * dprobs, axis=2, keepdims=True)
        return (new_max, running, weighted)

    row_stats = (
        jnp.full((head_count, local_count, 1), -jnp.inf, jnp.float32),
        jnp.zeros((head_count, local_count, 1), jnp.float32),
        jnp.zeros((head_count, local_count, 1), jnp.float32),
    )
    for key_rows, value_rows in key_sets:
        row_stats = over_keys(stat_turn, row_stats, key_rows, value_rows)
    log_sums = row_stats[0] + jnp.log(row_stats[1])
    deltas = row_stats[2] / row_stats[1]

    def query_turn(running, key_block, value_block):
        probs = jnp.exp(head_scores(query_split, key_block) - log_sums)
        dprobs = jnp.einsum(
            "qhd,khd->hqk", grad_split, value_block, preferred_element_type=jnp.float32
        )
        dscores = (probs * (dprobs - deltas)).astype(jnp.bfloat16)
        return running + jnp.einsum(
            "hqk,khd->qhd", dscores, key_block, preferred_element_type=jnp.float32
        ) * HEAD_SIZE ** (-0.5)

    query_grad = jnp.zeros((local_count, head_count, HEAD_SIZE), jnp.float32)
    for key_rows, value_rows in key_sets:
        query_grad = over_keys(query_turn, query_grad, key_rows, value_rows)
    query_grad = join_heads(query_grad).astype(jnp.bfloat16)
    log_rows = log_sums[:, :, 0].T
    delta_rows = deltas[:, :, 0].T
    own_keys = split_heads(key_img)
    own_values = split_heads(value_img)
    empty = jnp.zeros(own_keys.shape, jnp.float32)
    query_rows = lax.all_gather(query_local.astype(jnp.float32), "seq", axis=0, tiled=True).astype(
        jnp.bfloat16
    )
    grad_rows = lax.all_gather(grad_local.astype(jnp.float32), "seq", axis=0, tiled=True).astype(
        jnp.bfloat16
    )
    log_part = lax.all_gather(log_rows, "seq", axis=0, tiled=True)
    delta_part = lax.all_gather(delta_rows, "seq", axis=0, tiled=True)
    piece_rows = query_rows.shape[0]
    block_rows = piece_rows if piece_rows <= 2048 else math.gcd(piece_rows, 2048)

    def fold_one_turn(turn_index, running):

        def rows_of(table):
            return lax.dynamic_slice_in_dim(table, turn_index * block_rows, block_rows, 0)

        return key_terms(
            running,
            split_heads(rows_of(query_rows)),
            split_heads(rows_of(grad_rows)),
            rows_of(log_part),
            rows_of(delta_part),
            own_keys,
            own_values,
        )

    key_grad, value_grad = lax.fori_loop(0, piece_rows // block_rows, fold_one_turn, (empty, empty))
    key_grad = join_heads(key_grad).astype(jnp.bfloat16)
    value_grad = join_heads(value_grad).astype(jnp.bfloat16)
    text_empty = jnp.zeros(text_keys.shape, jnp.float32)
    text_key, text_value = key_terms(
        (text_empty, text_empty),
        query_split,
        grad_split,
        log_rows,
        delta_rows,
        text_keys,
        text_values,
    )
    text_key, text_value = (
        lax.psum_scatter(join_heads(text_key), "seq", scatter_dimension=0, tiled=True),
        lax.psum_scatter(join_heads(text_value), "seq", scatter_dimension=0, tiled=True),
    )
    dk_txt = text_key.astype(jnp.bfloat16)
    dv_txt = text_value.astype(jnp.bfloat16)
    dq_txt = query_grad[image_rows:]
    dq_heads = query_grad[:image_rows]
    dq_img, dk_img, dv_quant = (
        lax.all_to_all(dq_heads, "head", split_axis=0, concat_axis=1, tiled=True),
        lax.all_to_all(key_grad, "head", split_axis=0, concat_axis=1, tiled=True),
        lax.all_to_all(value_grad, "head", split_axis=0, concat_axis=1, tiled=True),
    )
    image_value_grad = jnp.where(inside, dv_quant, jnp.zeros_like(dv_quant))
    lowrank_gradient = jnp.einsum(
        "vg,zg->vz", image_value_grad, adapter_up_weight, preferred_element_type=jnp.float32
    ).astype(jnp.bfloat16)
    part_down = jnp.einsum(
        "td,tr->dr", image_input_rows, lowrank_gradient, preferred_element_type=jnp.float32
    )
    lowrank_input = jnp.dot(
        image_input_rows, adapter_down_weight, preferred_element_type=jnp.float32
    ).astype(jnp.bfloat16)
    part_up = jnp.einsum(
        "tr,tw->rw", lowrank_input, image_value_grad, preferred_element_type=jnp.float32
    )
    token_rows = dv_quant.shape[0]
    token_terms = (dv_quant.astype(jnp.float32) * lsq_term).reshape(
        token_rows, value_step_sizes.shape[1], HEAD_SIZE
    )
    total_down, total_up, step_sums = lax.psum(
        (part_down, part_up, jnp.sum(token_terms, axis=(0, 2))), ("seq", "head")
    )
    grad_steps = jnp.where(slot_rows[:, None], step_sums[None, :], 0.0) * (QMAX ** (-0.5) * unscale)
    return (
        dq_img,
        dk_img,
        image_value_grad,
        dq_txt,
        dk_txt,
        dv_txt,
        total_down * unscale,
        total_up * unscale,
        grad_steps,
    )


MESH = pl.DeviceIdType.MESH
BF = jnp.bfloat16
F32 = jnp.float32
NT = (((1,), (1,)), ((), ()))
NN = (((1,), (0,)), ((), ()))


def dot(left, right, dims=NN):
    return lax.dot_general(left, right, dims, preferred_element_type=F32)


def attention_kernel(
    seq,
    head,
    q_in,
    k_in,
    code_in,
    do_in,
    tq_in,
    tk_in,
    tv_in,
    tdo_in,
    x_in,
    frac_in,
    up_in,
    down_in,
    step_ref,
    group_ref,
    time_ref,
    dq_ref,
    dk_ref,
    dv_ref,
    dqt_ref,
    dkt_ref,
    dvt_ref,
    down_ref,
    up_ref,
    steps_ref,
    q_ref,
    k_ref,
    code_ref,
    do_ref,
    x_ref,
    frac_ref,
    upw_ref,
    downw_ref,
    stage,
    recv,
    kv2,
    tkv,
    tqd,
    kall,
    ktr,
    vall,
    qall,
    doall,
    dqall,
    dkacc,
    dvacc,
    xo,
    xi,
    to,
    ti,
    ost,
    ret,
    tfin,
    rett,
    xlow_out,
    xlow_in,
    xst,
    xcol,
    up_out,
    up_in2,
    up_all,
    low_out,
    low_in,
    red_out,
    red_in,
    sum_out,
    sum_in,
    gath,
    li,
    s1,
    r1,
    s2,
    r2,
    st,
    rt,
    s3,
    r3,
    s4,
    r4,
    s5,
    r5,
    s6,
    r6,
    s7,
    r7,
    s8,
    r8,
    s9,
    r9,
    s10,
    r10,
    s11,
    r11,
    s12,
    r12,
):
    rows = q_ref.shape[0]
    heads = q_ref.shape[1] // HEAD_SIZE
    text = tq_in.shape[0]
    half = text // 2
    planes = head // 2
    peers = seq * planes
    group = tq_in.shape[1] // HEAD_SIZE
    pair = 2 * group
    first = (seq - pair) // 2
    image = peers * rows
    share = text // seq
    scale = HEAD_SIZE ** (-0.5)
    rank = upw_ref.shape[0]
    wide = x_ref.shape[1] // seq
    part = rank // head
    hrank = rank // 2
    hrows = rows // 2

    s = lax.axis_index("seq")
    g = lax.axis_index("head")
    c = lax.rem(g, 2)
    y = g // 2
    me = s * planes + y
    partner = (s, g + 1 - 2 * c)
    slot = s - first
    is_head = jnp.logical_and(slot >= 0, slot < pair)
    mine = y * pair + slot
    holds_text = jnp.logical_and(is_head, slot // group == c)
    takes_text = jnp.logical_and(is_head, slot // group != c)
    lane_block = lax.rem(slot, group)

    def peer(p):
        return (p // planes, lax.rem(p, planes) * 2 + c)

    def home(h):
        return (first + lax.rem(h, pair), (h // pair) * 2 + c)

    def home_peer(h):
        return (first + lax.rem(h, pair)) * planes + h // pair

    def send(src, dst, ssem, rsem, to_id):
        return pltpu.make_async_remote_copy(
            src_ref=src, dst_ref=dst, send_sem=ssem, recv_sem=rsem, device_id=to_id, device_id_type=MESH
        )

    loads = [
        pltpu.make_async_copy(src, dst, li.at[i])
        for i, (src, dst) in enumerate(
            (
                (k_in, k_ref),
                (code_in, code_ref),
                (q_in, q_ref),
                (do_in, do_ref),
                (x_in, x_ref),
                (down_in, downw_ref),
                (up_in, upw_ref),
                (frac_in, frac_ref),
            )
        )
    ]
    for load in loads:
        load.start()

    barrier = pltpu.get_barrier_semaphore()
    for i in range(1, peers):
        pl.semaphore_signal(
            barrier, inc=1, device_id=peer(lax.rem(me + i, peers)), device_id_type=MESH
        )
    for other in range(planes):
        pl.semaphore_signal(
            barrier, inc=1, device_id=(s, other * 2 + 1 - c), device_id_type=MESH
        )

    for load in loads[:4]:
        load.wait()
    for h in range(heads):
        cols = slice(h * HEAD_SIZE, (h + 1) * HEAD_SIZE)
        stage[h, 0:rows] = k_ref[:, cols]
        stage[h, rows : 2 * rows] = code_ref[:, cols].astype(F32).astype(BF)
        stage[h, 2 * rows : 3 * rows] = q_ref[:, cols]
        stage[h, 3 * rows : 4 * rows] = do_ref[:, cols]

    pl.semaphore_wait(barrier, peers - 1 + planes)

    def first_send(h, k):
        at = pl.ds(k * 2 * rows, 2 * rows)
        return send(stage.at[h, at], recv.at[me, at], s1.at[k, h], r1.at[k, me], home(h))

    def first_recv(p, k):
        at = pl.ds(k * 2 * rows, 2 * rows)
        return send(stage.at[0, at], recv.at[p, at], s1.at[k, 0], r1.at[k, p], partner)

    for k in range(2):
        for i in range(heads):
            h = lax.rem(me + i, heads)

            @pl.when(me != home_peer(h))
            def _():
                first_send(h, k).start()

    def text_sources():
        cols = pl.ds(pl.multiple_of(lane_block * HEAD_SIZE, HEAD_SIZE), HEAD_SIZE)
        return cols, pl.ds(0, half), pl.ds(half, half)

    def text_copies():
        cols, _, low = text_sources()
        return (
            send(tk_in.at[:, cols], tkv.at[0], st.at[0], rt.at[0], partner),
            send(tv_in.at[:, cols], tkv.at[1], st.at[1], rt.at[1], partner),
            send(tq_in.at[low, cols], tqd.at[0], st.at[2], rt.at[2], partner),
            send(tdo_in.at[low, cols], tqd.at[1], st.at[3], rt.at[3], partner),
        )

    def text_loads():
        cols, high, _ = text_sources()
        return (
            pltpu.make_async_copy(tk_in.at[:, cols], tkv.at[0], li.at[8]),
            pltpu.make_async_copy(tv_in.at[:, cols], tkv.at[1], li.at[9]),
            pltpu.make_async_copy(tq_in.at[high, cols], tqd.at[0], li.at[10]),
            pltpu.make_async_copy(tdo_in.at[high, cols], tqd.at[1], li.at[11]),
        )

    @pl.when(holds_text)
    def _():
        for copy in text_copies() + text_loads():
            copy.start()

    for load in loads[4:6]:
        load.wait()
    for t in range(seq):
        xst[t] = x_ref[:, t * wide : (t + 1) * wide]

    def column_send(t):
        return send(xst.at[t], xcol.at[s], s6.at[t], r6.at[s], (t, g))

    xlow = dot(x_ref[...], downw_ref[...], NT)
    xlow_out[...] = jnp.concatenate([xlow[0:hrows], xlow[hrows:rows]], axis=1).astype(BF)

    def low_send(h):
        return send(xlow_out, xlow_in.at[me], s7.at[h], r7.at[me], home(h))

    for i in range(heads):
        h = lax.rem(me + i, heads)

        @pl.when(me != home_peer(h))
        def _():
            low_send(h).start()

    for load in loads[6:8]:
        load.wait()

    def up_send(p):
        return send(
            up_out.at[c], up_all.at[mine, c], s9.at[p], r9.at[mine], peer(p)
        )

    def column_sends():
        for i in range(1, seq):
            column_send(lax.rem(s + i, seq)).start()
        xcol[pl.ds(s, 1)] = xst[pl.ds(s, 1)]

    @pl.when(jnp.logical_not(is_head))
    def _():
        column_sends()

    def up_trade():
        return send(up_in2.at[0, 1 - c], up_in2.at[1, 0], s8.at[0], r8.at[0], partner)

    def text_trade():
        return send(to, ti, s3.at[2], r3.at[2], partner)

    def back_query(p):
        return send(
            dqall.at[pl.ds(pl.multiple_of(p * rows, rows), rows)], ret.at[mine, pl.ds(0, rows)],
            s4.at[0, p], r4.at[0, mine], peer(p)
        )

    def back_send(k, p):
        at = pl.ds(k * rows, rows)
        return send(ost.at[p, at], ret.at[mine, at], s4.at[k, p], r4.at[k, mine], peer(p))

    def back_recv(k, h):
        at = pl.ds(k * rows, rows)
        return send(ost.at[0, at], ret.at[h, at], s4.at[k, 0], r4.at[k, h], partner)

    def trade(k):
        return send(xo.at[k], xi.at[k], s3.at[k], r3.at[k], partner)

    @pl.when(is_head)
    def _():
        recv[pl.ds(me, 1)] = stage[pl.ds(mine, 1)]
        xlow_in[pl.ds(me, 1)] = xlow_out[...].reshape(1, hrows, HEAD_SIZE)
        for i in range(1, peers):
            p = lax.rem(me + i, peers)
            first_recv(p, 0).wait_recv()

        swap = send(recv.at[:, pl.ds(0, 2 * rows)], kv2, s2.at[0], r2.at[0], partner)
        swap.start()
        step = step_ref[group_ref[time_ref[0]], mine]

        def dequant(codes):
            return (codes.reshape(image, HEAD_SIZE).astype(F32) * step).astype(BF)

        kall[0:image] = recv[:, 0:rows].reshape(image, HEAD_SIZE)
        vall[0:image] = dequant(recv[:, rows : 2 * rows])
        for i in range(1, peers):
            p = lax.rem(me + i, peers)
            first_recv(p, 1).wait_recv()

        column_sends()
        qall[0:image] = recv[:, 2 * rows : 3 * rows].reshape(image, HEAD_SIZE)
        doall[0:image] = recv[:, 3 * rows : 4 * rows].reshape(image, HEAD_SIZE)

        @pl.when(takes_text)
        def _():
            for copy in text_copies():
                copy.wait_recv()

        @pl.when(holds_text)
        def _():
            for copy in text_loads():
                copy.wait()

        kall[2 * image : 2 * image + text] = tkv[0]
        vall[2 * image : 2 * image + text] = tkv[1]
        qall[image : image + half] = tqd[0]
        doall[image : image + half] = tqd[1]
        swap.wait_recv()
        kall[image : 2 * image] = kv2[:, 0:rows].reshape(image, HEAD_SIZE)
        vall[image : 2 * image] = dequant(kv2[:, rows : 2 * rows])
        ktr[...] = kall[...].T

        def query_block(index):
            at = slice(index * half, (index + 1) * half)
            queries, grads = qall[at], doall[at]
            scores = dot(kall[...], queries, NT)
            dprobs = dot(vall[...], grads, NT)
            top = jnp.max(scores, axis=0, keepdims=True) * (scale * math.log2(math.e))
            expo = jnp.exp2(scores * (scale * math.log2(math.e)) - top)
            probs = expo * (1.0 / jnp.sum(expo, axis=0, keepdims=True))
            value_part = dot(probs.astype(BF), grads)
            deltas = jnp.sum(probs * dprobs, axis=0, keepdims=True)
            dscores = (probs * (dprobs - deltas)).astype(BF)
            key_part = dot(dscores, queries)
            dvacc[...] = value_part if index == 0 else dvacc[...] + value_part
            dkacc[...] = key_part if index == 0 else dkacc[...] + key_part
            dqall[at] = (dot(ktr[...], dscores).T * scale).astype(BF)

        for index in range(image // half):
            query_block(index)
        for i in range(1, peers):
            back_query(lax.rem(me + i, peers)).start()
        query_block(image // half)
        xo[1] = dvacc[image : 2 * image].astype(BF)
        trade(1).start()
        xo[0] = (dkacc[image : 2 * image] * scale).astype(BF)
        trade(0).start()
        trade(1).wait_recv()
        ost[:, 2 * rows : 3 * rows] = (
            (dvacc[0:image] + xi[1].astype(F32)).astype(BF).reshape(peers, rows, HEAD_SIZE)
        )
        for i in range(1, peers):
            back_send(2, lax.rem(me + i, peers)).start()
        trade(0).wait_recv()
        ost[:, rows : 2 * rows] = (
            (dkacc[0:image] * scale + xi[0].astype(F32)).astype(BF).reshape(peers, rows, HEAD_SIZE)
        )
        for i in range(1, peers):
            back_send(1, lax.rem(me + i, peers)).start()
        ret[pl.ds(mine, 1), rows : 3 * rows] = ost[pl.ds(me, 1), rows : 3 * rows]
        ret[pl.ds(mine, 1), 0:rows] = dqall[pl.ds(pl.multiple_of(me * rows, rows), rows)].reshape(
            1, rows, HEAD_SIZE
        )

        @pl.when(takes_text)
        def _():
            to[0:text] = (dkacc[2 * image : 2 * image + text] * scale).astype(BF)
            to[text : 2 * text] = dvacc[2 * image : 2 * image + text].astype(BF)
            to[2 * text : 2 * text + half] = dqall[image : image + half]
            text_trade().start()

        for i in range(1, peers):
            p = lax.rem(me + i, peers)
            send(xlow_out, xlow_in.at[p], s7.at[0], r7.at[p], partner).wait_recv()

        codes = recv[:, rows : 2 * rows]
        kept = jnp.where(jnp.abs(codes.astype(F32)) < QMAX, ost[:, 2 * rows : 3 * rows].astype(F32), 0.0)
        kept = kept.astype(BF)
        low_rows = xlow_in[...].reshape(peers * hrows, HEAD_SIZE).T
        early = dot(low_rows, kept[:, 0:hrows].reshape(peers * hrows, HEAD_SIZE))
        late = dot(low_rows, kept[:, hrows:rows].reshape(peers * hrows, HEAD_SIZE))
        part_up = (early[0:rank] + late[rank : 2 * rank]).reshape(2, hrank, HEAD_SIZE)
        up_in2[0] = part_up
        up_trade().start()

    for h in range(heads):

        @pl.when(me != home_peer(h))
        def _():
            back_recv(2, h).wait_recv()

    sums = []
    for h in range(heads):
        cols = slice(h * HEAD_SIZE, (h + 1) * HEAD_SIZE)
        codes = code_ref[:, cols]
        inside = jnp.abs(codes) < QMAX
        value_grad = ret[h, 2 * rows : 3 * rows].astype(F32)
        kept = jnp.where(inside, value_grad, 0.0).astype(BF)
        lsq_term = jnp.where(inside, -frac_ref[:, cols].astype(F32), codes.astype(F32))
        sums.append(jnp.sum(value_grad * lsq_term, axis=0, keepdims=True))
        dv_ref[:, cols] = kept

    low = dot(dv_ref[...], upw_ref[...], NT)
    sums.append(jnp.zeros((rows - heads, HEAD_SIZE), F32))
    step_terms = jnp.sum(jnp.concatenate(sums, axis=0), axis=1, keepdims=True)
    step_high = step_terms.astype(BF).astype(F32)
    lane_at = lax.broadcasted_iota(jnp.int32, (rows, rank), 1)
    beside = jnp.where(lane_at == 0, step_high, jnp.where(lane_at == 1, step_terms - step_high, 0.0))
    low_out[...] = jnp.concatenate([low, beside], axis=1).astype(BF)

    def tile_send(t):
        return send(low_out, low_in.at[s], s10.at[t], r10.at[s], (t, g))

    for i in range(1, seq):
        tile_send(lax.rem(s + i, seq)).start()
    low_in[pl.ds(s, 1)] = low_out[...].reshape(1, rows, HEAD_SIZE)

    @pl.when(is_head)
    def _():
        @pl.when(holds_text)
        def _():
            text_trade().wait_recv()
            full = (seq, share, HEAD_SIZE)
            tfin[0 : seq // 2, 0] = dqall[image : image + half].reshape(seq // 2, share, HEAD_SIZE)
            tfin[seq // 2 : seq, 0] = ti[2 * text : 2 * text + half].reshape(seq // 2, share, HEAD_SIZE)
            tfin[:, 1] = (
                (dkacc[2 * image : 2 * image + text] * scale + ti[0:text].astype(F32)).astype(BF).reshape(full)
            )
            tfin[:, 2] = (
                (dvacc[2 * image : 2 * image + text] + ti[text : 2 * text].astype(F32)).astype(BF).reshape(full)
            )
            for i in range(1, seq):
                other = lax.rem(s + i, seq)
                send(
                    tfin.at[other], rett.at[lane_block], s5.at[other], r5.at[lane_block], (other, g)
                ).start()

            rett[pl.ds(lane_block, 1)] = tfin[pl.ds(s, 1)]

        up_trade().wait_recv()
        up_out[pl.ds(c, 1)] = (
            (up_in2[pl.ds(0, 1), pl.ds(c, 1)] + up_in2[pl.ds(1, 1), pl.ds(0, 1)]) * unscale
        ).astype(BF).reshape(1, hrank, HEAD_SIZE)
        for i in range(1, peers):
            up_send(lax.rem(me + i, peers)).start()
        up_all[pl.ds(mine, 1), pl.ds(c, 1)] = up_out[pl.ds(c, 1)].reshape(1, 1, hrank, HEAD_SIZE)

    for i in range(1, seq):
        t = lax.rem(s + i, seq)
        send(xst.at[0], xcol.at[t], s6.at[0], r6.at[t], partner).wait_recv()
        send(low_out, low_in.at[t], s10.at[0], r10.at[t], partner).wait_recv()

    tiles = low_in[...]
    flat = tiles.reshape(seq * rows, HEAD_SIZE).T
    block = dot(flat, xcol[...].reshape(seq * rows, wide))[0:rank]
    step_group = jnp.sum(tiles[:, 0:16].astype(F32), axis=0)
    red_out[...] = block.astype(BF).reshape(head, part, wide)
    sum_out[...] = step_group

    def reduce_send(other):
        return send(red_out.at[other], red_in.at[g], s11.at[0, other], r11.at[0, g], (s, other))

    def sum_send(other):
        return send(sum_out, sum_in.at[g], s11.at[1, other], r11.at[1, g], (s, other))

    for i in range(1, head):
        reduce_send(lax.rem(g + i, head)).start()
    for i in range(1, head):
        sum_send(lax.rem(g + i, head)).start()
    red_in[pl.ds(g, 1)] = red_out[pl.ds(g, 1)]
    sum_in[pl.ds(g, 1)] = step_group.reshape(1, 16, HEAD_SIZE)
    for i in range(1, head):
        other = lax.rem(g + i, head)
        send(red_out.at[0], red_in.at[other], s11.at[0, 0], r11.at[0, other], partner).wait_recv()

    summed = jnp.sum(red_in[...].astype(F32), axis=0) * unscale
    gath[pl.ds(y, 1), pl.ds(c, 1), pl.ds(s, 1)] = summed.astype(BF).reshape(1, 1, 1, part, wide)

    def row_send(p):
        return send(gath.at[y, c, s], gath.at[y, c, s], s12.at[p], r12.at[me], peer(p))

    def core_send():
        return send(gath.at[:, c], gath.at[:, c], s12.at[peers], r12.at[peers], partner)

    def core_up_send():
        return send(up_all.at[:, c], up_all.at[:, c], s8.at[1], r8.at[1], partner)

    for i in range(1, peers):
        row_send(lax.rem(me + i, peers)).start()

    for j in range(group):

        @pl.when(s != first + c * group + j)
        def _():
            send(tfin.at[0], rett.at[j], s5.at[0], r5.at[j], partner).wait_recv()

        cols = slice(j * HEAD_SIZE, (j + 1) * HEAD_SIZE)
        dqt_ref[:, cols] = rett[j, 0]
        dkt_ref[:, cols] = rett[j, 1]
        dvt_ref[:, cols] = rett[j, 2]

    for h in range(heads):

        @pl.when(me != home_peer(h))
        def _():
            back_recv(0, h).wait_recv()
            back_recv(1, h).wait_recv()

    for h in range(heads):
        cols = slice(h * HEAD_SIZE, (h + 1) * HEAD_SIZE)
        dq_ref[:, cols] = ret[h, 0:rows]
        dk_ref[:, cols] = ret[h, rows : 2 * rows]

    slot_index = group_ref[time_ref[0]]
    for i in range(1, head):
        other = lax.rem(g + i, head)
        send(sum_out, sum_in.at[other], s11.at[1, 0], r11.at[1, other], partner).wait_recv()

    lanes = jnp.sum(sum_in[...], axis=0)
    lane_at = lax.broadcasted_iota(jnp.int32, (16, HEAD_SIZE), 1)
    row_at = lax.broadcasted_iota(jnp.int32, (16, HEAD_SIZE), 0)
    chosen = jnp.logical_or(lane_at == rank, lane_at == rank + 1)
    head_sums = jnp.sum(jnp.where(chosen, lanes, 0.0), axis=1, keepdims=True)
    step_row = jnp.sum(jnp.where(lane_at == row_at, head_sums, 0.0), axis=0, keepdims=True)[:, 0:heads]
    step_row = step_row * (QMAX ** (-0.5) * unscale)
    slots = steps_ref.shape[0]
    slot_at = lax.broadcasted_iota(jnp.int32, (slots, heads), 0)
    steps_ref[...] = jnp.where(slot_at == slot_index, jnp.broadcast_to(step_row, (slots, heads)), 0.0)

    for h in range(heads):

        @pl.when(me != home_peer(h))
        def _():
            send(up_out.at[0], up_all.at[h, c], s9.at[0], r9.at[h], partner).wait_recv()

    core_up_send().start()

    for i in range(1, peers):
        p = lax.rem(me + i, peers)
        block_at = gath.at[lax.rem(p, planes), c, p // planes]
        send(block_at, block_at, s12.at[0], r12.at[p], partner).wait_recv()

    core_send().start()
    send(up_all.at[:, 1 - c], up_all.at[:, 1 - c], s8.at[1], r8.at[1], partner).wait_recv()
    for h in range(heads):
        cols = slice(h * HEAD_SIZE, (h + 1) * HEAD_SIZE)
        up_ref[:, cols] = up_all[h].reshape(rank, HEAD_SIZE).astype(F32)
    send(gath.at[:, 1 - c], gath.at[:, 1 - c], s12.at[peers], r12.at[peers], partner).wait_recv()
    for t in range(seq):
        down_ref[:, t * wide : (t + 1) * wide] = gath[:, :, t].reshape(rank, wide).astype(F32)

    for h in range(heads):

        @pl.when(me != home_peer(h))
        def _():
            first_send(h, 0).wait_send()
            first_send(h, 1).wait_send()
            low_send(h).wait_send()

    for i in range(1, seq):
        t = lax.rem(s + i, seq)
        column_send(t).wait_send()
        tile_send(t).wait_send()
    for i in range(1, head):
        reduce_send(lax.rem(g + i, head)).wait_send()
        sum_send(lax.rem(g + i, head)).wait_send()
    for i in range(1, peers):
        row_send(lax.rem(me + i, peers)).wait_send()
    core_send().wait_send()
    core_up_send().wait_send()

    @pl.when(is_head)
    def _():
        send(recv.at[:, pl.ds(0, 2 * rows)], kv2, s2.at[0], r2.at[0], partner).wait_send()
        trade(0).wait_send()
        trade(1).wait_send()
        up_trade().wait_send()
        for i in range(1, peers):
            p = lax.rem(me + i, peers)
            back_query(p).wait_send()
            back_send(1, p).wait_send()
            back_send(2, p).wait_send()
            up_send(p).wait_send()

    @pl.when(takes_text)
    def _():
        text_trade().wait_send()

    @pl.when(holds_text)
    def _():
        for copy in text_copies():
            copy.wait_send()
        for i in range(1, seq):
            other = lax.rem(s + i, seq)
            send(
                tfin.at[other], rett.at[lane_block], s5.at[other], r5.at[lane_block], (other, g)
            ).wait_send()


def settle_kernel(count, *refs):
    sources, targets, held = refs[:count], refs[count : 2 * count], refs[2 * count : 3 * count]
    came, went = refs[3 * count :]
    loads = [pltpu.make_async_copy(a, b, came.at[i]) for i, (a, b) in enumerate(zip(sources, held))]
    stores = [pltpu.make_async_copy(a, b, went.at[i]) for i, (a, b) in enumerate(zip(held, targets))]
    for load in loads:
        load.start()
    for load, store in zip(loads, stores):
        load.wait()
        store.start()
    for store in stores:
        store.wait()


def settle(arrays):
    count = len(arrays)
    anywhere = pl.BlockSpec(memory_space=pl.ANY)
    return pl.pallas_call(
        functools.partial(settle_kernel, count),
        out_shape=[jax.ShapeDtypeStruct(a.shape, a.dtype) for a in arrays],
        in_specs=[anywhere] * count,
        out_specs=[anywhere] * count,
        scratch_shapes=[pltpu.VMEM(a.shape, a.dtype) for a in arrays]
        + [pltpu.SemaphoreType.DMA((count,))] * 2,
        compiler_params=pltpu.CompilerParams(vmem_limit_bytes=56 * 1024 * 1024),
        name="settle",
    )(*arrays)


def whole_heads(
    seq,
    head,
    image_input_rows,
    adapter_down_weight,
    adapter_up_weight,
    image_query_rows,
    image_key_rows,
    image_value_codes,
    value_fraction,
    value_step_sizes,
    timestep_group,
    timestep,
    image_output_grad,
    text_query_rows,
    text_key_rows,
    text_value_rows,
    text_output_grad,
):
    rows, width = image_query_rows.shape
    text, text_width = text_query_rows.shape
    heads, group = width // HEAD_SIZE, text_width // HEAD_SIZE
    peers = seq * head // 2
    image, share = peers * rows, text // seq
    keys = 2 * image + text
    rank, wide = adapter_up_weight.shape[0], image_input_rows.shape[1] // seq
    planes = head // 2
    vmem = pl.BlockSpec(memory_space=pltpu.VMEM)
    sems = pltpu.SemaphoreType.DMA
    hbm = pl.BlockSpec(memory_space=pl.ANY)
    smem = pl.BlockSpec(memory_space=pltpu.SMEM)
    results = pl.pallas_call(
        functools.partial(attention_kernel, seq, head),
        out_shape=[jax.ShapeDtypeStruct((rows, width), BF)] * 3
        + [jax.ShapeDtypeStruct((share, text_width), BF)] * 3
        + [
            jax.ShapeDtypeStruct(adapter_down_weight.shape[::-1], F32),
            jax.ShapeDtypeStruct(adapter_up_weight.shape, F32),
            jax.ShapeDtypeStruct(value_step_sizes.shape, F32),
        ],
        in_specs=[hbm] * 12 + [smem] * 3,
        out_specs=[vmem] * 9,
        scratch_shapes=[
            pltpu.VMEM((rows, width), BF),
            pltpu.VMEM((rows, width), BF),
            pltpu.VMEM((rows, width), jnp.int32),
            pltpu.VMEM((rows, width), BF),
            pltpu.VMEM(image_input_rows.shape, BF),
            pltpu.VMEM((rows, width), BF),
            pltpu.VMEM(adapter_up_weight.shape, BF),
            pltpu.VMEM(adapter_down_weight.shape[::-1], BF),
            pltpu.VMEM((heads, 4 * rows, HEAD_SIZE), BF),
            pltpu.VMEM((peers, 4 * rows, HEAD_SIZE), BF),
            pltpu.VMEM((peers, 2 * rows, HEAD_SIZE), BF),
            pltpu.VMEM((2, text, HEAD_SIZE), BF),
            pltpu.VMEM((2, text // 2, HEAD_SIZE), BF),
            pltpu.VMEM((keys, HEAD_SIZE), BF),
            pltpu.VMEM((HEAD_SIZE, keys), BF),
            pltpu.VMEM((keys, HEAD_SIZE), BF),
            pltpu.VMEM((image + text // 2, HEAD_SIZE), BF),
            pltpu.VMEM((image + text // 2, HEAD_SIZE), BF),
            pltpu.VMEM((image + text // 2, HEAD_SIZE), BF),
            pltpu.VMEM((keys, HEAD_SIZE), F32),
            pltpu.VMEM((keys, HEAD_SIZE), F32),
            pltpu.VMEM((2, image, HEAD_SIZE), BF),
            pltpu.VMEM((2, image, HEAD_SIZE), BF),
            pltpu.VMEM((2 * text + text // 2, HEAD_SIZE), BF),
            pltpu.VMEM((2 * text + text // 2, HEAD_SIZE), BF),
            pltpu.VMEM((peers, 3 * rows, HEAD_SIZE), BF),
            pltpu.VMEM((heads, 3 * rows, HEAD_SIZE), BF),
            pltpu.VMEM((seq, 3, share, HEAD_SIZE), BF),
            pltpu.VMEM((group, 3, share, HEAD_SIZE), BF),
            pltpu.VMEM((rows // 2, HEAD_SIZE), BF),
            pltpu.VMEM((peers, rows // 2, HEAD_SIZE), BF),
            pltpu.VMEM((seq, rows, wide), BF),
            pltpu.VMEM((seq, rows, wide), BF),
            pltpu.VMEM((2, rank // 2, HEAD_SIZE), BF),
            pltpu.VMEM((2, 2, rank // 2, HEAD_SIZE), F32),
            pltpu.VMEM((heads, 2, rank // 2, HEAD_SIZE), BF),
            pltpu.VMEM((rows, HEAD_SIZE), BF),
            pltpu.VMEM((seq, rows, HEAD_SIZE), BF),
            pltpu.VMEM((head, rank // head, wide), BF),
            pltpu.VMEM((head, rank // head, wide), BF),
            pltpu.VMEM((16, HEAD_SIZE), F32),
            pltpu.VMEM((head, 16, HEAD_SIZE), F32),
            pltpu.VMEM((planes, 2, seq, rank // head, wide), BF),
            sems((12,)),
            sems((2, heads)),
            sems((2, peers)),
            sems((1,)),
            sems((1,)),
            sems((4,)),
            sems((4,)),
            sems((3,)),
            sems((3,)),
            sems((3, peers)),
            sems((3, heads)),
            sems((seq,)),
            sems((group,)),
            sems((seq,)),
            sems((seq,)),
            sems((heads,)),
            sems((peers,)),
            sems((2,)),
            sems((2,)),
            sems((peers,)),
            sems((heads,)),
            sems((seq,)),
            sems((seq,)),
            sems((2, head)),
            sems((2, head)),
            sems((peers + 1,)),
            sems((peers + 1,)),
        ],
        compiler_params=pltpu.CompilerParams(
            collective_id=0, has_side_effects=True, vmem_limit_bytes=56 * 1024 * 1024
        ),
        name="whole_heads",
    )(
        image_query_rows,
        image_key_rows,
        image_value_codes,
        image_output_grad,
        text_query_rows,
        text_key_rows,
        text_value_rows,
        text_output_grad,
        image_input_rows,
        value_fraction,
        adapter_up_weight,
        adapter_down_weight.T,
        value_step_sizes,
        timestep_group,
        timestep,
    )
    results = settle(results)
    return (*results[:6], results[6].T, *results[7:])


def pick(mesh):
    seq, head = mesh.shape["seq"], mesh.shape["head"]

    def chosen(*arguments):
        rows, width = arguments[3].shape
        text, text_width = arguments[11].shape
        pair = 2 * text_width // HEAD_SIZE
        fits = (
            head % 2 == 0
            and seq % 2 == 0
            and seq >= pair
            and rows % 32 == 0
            and 2 * arguments[2].shape[0] == HEAD_SIZE
            and width // HEAD_SIZE <= 16
            and (text // 2) % rows == 0
            and (seq * head // 2 * rows) % (text // 2) == 0
            and arguments[2].shape[0] % (16 * head) == 0
            and arguments[0].shape[1] % (seq * HEAD_SIZE) == 0
            and text % (seq * 16) == 0
            and (seq * head // 2 * rows) % (text // 2) == 0
            and (seq * head * rows + text) * HEAD_SIZE <= 1 << 18
        )
        if fits:
            return whole_heads(seq, head, *arguments)
        return on_device(*arguments)

    return chosen


def solution(mesh):
    placed = (
        P(("seq", "head"), None),
        P(),
        P(),
        P(("seq", "head"), None),
        P(("seq", "head"), None),
        P(("seq", "head"), None),
        P(("seq", "head"), None),
        P(),
        P(),
        P(),
        P(("seq", "head"), None),
        P(None, "head"),
        P(None, "head"),
        P(None, "head"),
        P(None, "head"),
    )
    return jax.shard_map(
        pick(mesh),
        mesh=mesh,
        in_specs=placed,
        out_specs=(
            P(("seq", "head"), None),
            P(("seq", "head"), None),
            P(("seq", "head"), None),
            P("seq", "head"),
            P("seq", "head"),
            P("seq", "head"),
            P(),
            P(),
            P(),
        ),
        check_vma=False,
    )
```

```python
import functools
import math

import jax
import jax.numpy as jnp
from jax import lax
from jax.experimental import pallas as pl
from jax.experimental.pallas import tpu as pltpu
from jax.sharding import PartitionSpec as P

HEAD_SIZE = 128
QMAX = 127


unscale = 0.0078125


def split_heads(rows):
    return rows.reshape(rows.shape[0], rows.shape[1] // HEAD_SIZE, HEAD_SIZE)


def join_heads(heads):
    return heads.reshape(heads.shape[0], heads.shape[1] * heads.shape[2])


def head_scores(queries, key_rows):
    return jnp.einsum(
        "qhd,khd->hqk", queries, key_rows, preferred_element_type=jnp.float32
    ) * HEAD_SIZE ** (-0.5)


def over_keys(step_fn, initial, key_rows, value_rows):
    block_rows = math.gcd(key_rows.shape[0], 2048)

    def over_one_turn(turn_index, carried):
        key_block = lax.dynamic_slice_in_dim(key_rows, turn_index * block_rows, block_rows, 0)
        value_block = lax.dynamic_slice_in_dim(value_rows, turn_index * block_rows, block_rows, 0)
        return step_fn(carried, key_block, value_block)

    return lax.fori_loop(0, key_rows.shape[0] // block_rows, over_one_turn, initial)


def key_terms(carried, queries, grads, log_rows, delta_rows, own_keys, own_values):
    key_grad, value_grad = carried
    probs = jnp.exp(head_scores(queries, own_keys) - log_rows.T[:, :, None])
    dprobs = jnp.einsum("qhd,khd->hqk", grads, own_values, preferred_element_type=jnp.float32)
    dscores = (probs * (dprobs - delta_rows.T[:, :, None])).astype(jnp.bfloat16)
    value_grad = value_grad + jnp.einsum(
        "hqk,qhd->khd", probs.astype(jnp.bfloat16), grads, preferred_element_type=jnp.float32
    )
    key_grad = key_grad + jnp.einsum(
        "hqk,qhd->khd", dscores, queries, preferred_element_type=jnp.float32
    ) * HEAD_SIZE ** (-0.5)
    return (key_grad, value_grad)


def on_device(
    image_input_rows,
    adapter_down_weight,
    adapter_up_weight,
    image_query_rows,
    image_key_rows,
    image_value_codes,
    value_fraction,
    value_step_sizes,
    timestep_group,
    timestep,
    image_output_grad,
    text_query_rows,
    text_key_rows,
    text_value_rows,
    text_output_grad,
):
    slot_index = jnp.sum(
        jnp.where(
            jnp.arange(timestep_group.shape[0], dtype=jnp.int32) == timestep[0], timestep_group, 0
        )
    )
    slot_rows = jnp.arange(value_step_sizes.shape[0], dtype=jnp.int32) == slot_index
    step_row = jnp.sum(jnp.where(slot_rows[:, None], value_step_sizes, 0.0), axis=0)
    code_values = image_value_codes.astype(jnp.float32)
    v_dequant = (code_values * jnp.repeat(step_row, HEAD_SIZE)[None, :]).astype(jnp.bfloat16)
    inside = jnp.abs(image_value_codes) < QMAX
    lsq_term = jnp.where(inside, -value_fraction.astype(jnp.float32), code_values)
    query_img, key_img, value_img, grad_img = (
        lax.all_to_all(image_query_rows, "head", split_axis=1, concat_axis=0, tiled=True),
        lax.all_to_all(image_key_rows, "head", split_axis=1, concat_axis=0, tiled=True),
        lax.all_to_all(v_dequant, "head", split_axis=1, concat_axis=0, tiled=True),
        lax.all_to_all(image_output_grad, "head", split_axis=1, concat_axis=0, tiled=True),
    )
    share_rows = text_query_rows.shape[0] // lax.axis_size("seq")
    first_row = lax.axis_index("seq") * share_rows

    def own_rows(table):
        return lax.dynamic_slice_in_dim(table, first_row, share_rows, 0)

    image_rows = query_img.shape[0]
    query_local = jnp.concatenate([query_img, own_rows(text_query_rows)], axis=0)
    grad_local = jnp.concatenate([grad_img, own_rows(text_output_grad)], axis=0)
    query_split = split_heads(query_local)
    grad_split = split_heads(grad_local)
    local_count = query_split.shape[0]
    head_count = query_split.shape[1]
    key_image, value_image = (
        lax.all_gather(key_img, "seq", axis=0, tiled=True),
        lax.all_gather(value_img, "seq", axis=0, tiled=True),
    )
    text_keys = split_heads(text_key_rows)
    text_values = split_heads(text_value_rows)
    key_sets = ((split_heads(key_image), split_heads(value_image)), (text_keys, text_values))

    def stat_turn(carried, key_block, value_block):
        row_max, running, weighted = carried
        scores = head_scores(query_split, key_block)
        dprobs = jnp.einsum(
            "qhd,khd->hqk", grad_split, value_block, preferred_element_type=jnp.float32
        )
        new_max = jnp.maximum(row_max, jnp.max(scores, axis=2, keepdims=True))
        factor = jnp.exp(row_max - new_max)
        expo = jnp.exp(scores - new_max)
        running = running * factor + jnp.sum(expo, axis=2, keepdims=True)
        weighted = weighted * factor + jnp.sum(expo * dprobs, axis=2, keepdims=True)
        return (new_max, running, weighted)

    row_stats = (
        jnp.full((head_count, local_count, 1), -jnp.inf, jnp.float32),
        jnp.zeros((head_count, local_count, 1), jnp.float32),
        jnp.zeros((head_count, local_count, 1), jnp.float32),
    )
    for key_rows, value_rows in key_sets:
        row_stats = over_keys(stat_turn, row_stats, key_rows, value_rows)
    log_sums = row_stats[0] + jnp.log(row_stats[1])
    deltas = row_stats[2] / row_stats[1]

    def query_turn(running, key_block, value_block):
        probs = jnp.exp(head_scores(query_split, key_block) - log_sums)
        dprobs = jnp.einsum(
            "qhd,khd->hqk", grad_split, value_block, preferred_element_type=jnp.float32
        )
        dscores = (probs * (dprobs - deltas)).astype(jnp.bfloat16)
        return running + jnp.einsum(
            "hqk,khd->qhd", dscores, key_block, preferred_element_type=jnp.float32
        ) * HEAD_SIZE ** (-0.5)

    query_grad = jnp.zeros((local_count, head_count, HEAD_SIZE), jnp.float32)
    for key_rows, value_rows in key_sets:
        query_grad = over_keys(query_turn, query_grad, key_rows, value_rows)
    query_grad = join_heads(query_grad).astype(jnp.bfloat16)
    log_rows = log_sums[:, :, 0].T
    delta_rows = deltas[:, :, 0].T
    own_keys = split_heads(key_img)
    own_values = split_heads(value_img)
    empty = jnp.zeros(own_keys.shape, jnp.float32)
    query_rows = lax.all_gather(query_local.astype(jnp.float32), "seq", axis=0, tiled=True).astype(
        jnp.bfloat16
    )
    grad_rows = lax.all_gather(grad_local.astype(jnp.float32), "seq", axis=0, tiled=True).astype(
        jnp.bfloat16
    )
    log_part = lax.all_gather(log_rows, "seq", axis=0, tiled=True)
    delta_part = lax.all_gather(delta_rows, "seq", axis=0, tiled=True)
    piece_rows = query_rows.shape[0]
    block_rows = piece_rows if piece_rows <= 2048 else math.gcd(piece_rows, 2048)

    def fold_one_turn(turn_index, running):

        def rows_of(table):
            return lax.dynamic_slice_in_dim(table, turn_index * block_rows, block_rows, 0)

        return key_terms(
            running,
            split_heads(rows_of(query_rows)),
            split_heads(rows_of(grad_rows)),
            rows_of(log_part),
            rows_of(delta_part),
            own_keys,
            own_values,
        )

    key_grad, value_grad = lax.fori_loop(0, piece_rows // block_rows, fold_one_turn, (empty, empty))
    key_grad = join_heads(key_grad).astype(jnp.bfloat16)
    value_grad = join_heads(value_grad).astype(jnp.bfloat16)
    text_empty = jnp.zeros(text_keys.shape, jnp.float32)
    text_key, text_value = key_terms(
        (text_empty, text_empty),
        query_split,
        grad_split,
        log_rows,
        delta_rows,
        text_keys,
        text_values,
    )
    text_key, text_value = (
        lax.psum_scatter(join_heads(text_key), "seq", scatter_dimension=0, tiled=True),
        lax.psum_scatter(join_heads(text_value), "seq", scatter_dimension=0, tiled=True),
    )
    dk_txt = text_key.astype(jnp.bfloat16)
    dv_txt = text_value.astype(jnp.bfloat16)
    dq_txt = query_grad[image_rows:]
    dq_heads = query_grad[:image_rows]
    dq_img, dk_img, dv_quant = (
        lax.all_to_all(dq_heads, "head", split_axis=0, concat_axis=1, tiled=True),
        lax.all_to_all(key_grad, "head", split_axis=0, concat_axis=1, tiled=True),
        lax.all_to_all(value_grad, "head", split_axis=0, concat_axis=1, tiled=True),
    )
    image_value_grad = jnp.where(inside, dv_quant, jnp.zeros_like(dv_quant))
    lowrank_gradient = jnp.einsum(
        "vg,zg->vz", image_value_grad, adapter_up_weight, preferred_element_type=jnp.float32
    ).astype(jnp.bfloat16)
    part_down = jnp.einsum(
        "td,tr->dr", image_input_rows, lowrank_gradient, preferred_element_type=jnp.float32
    )
    lowrank_input = jnp.dot(
        image_input_rows, adapter_down_weight, preferred_element_type=jnp.float32
    ).astype(jnp.bfloat16)
    part_up = jnp.einsum(
        "tr,tw->rw", lowrank_input, image_value_grad, preferred_element_type=jnp.float32
    )
    token_rows = dv_quant.shape[0]
    token_terms = (dv_quant.astype(jnp.float32) * lsq_term).reshape(
        token_rows, value_step_sizes.shape[1], HEAD_SIZE
    )
    total_down, total_up, step_sums = lax.psum(
        (part_down, part_up, jnp.sum(token_terms, axis=(0, 2))), ("seq", "head")
    )
    grad_steps = jnp.where(slot_rows[:, None], step_sums[None, :], 0.0) * (QMAX ** (-0.5) * unscale)
    return (
        dq_img,
        dk_img,
        image_value_grad,
        dq_txt,
        dk_txt,
        dv_txt,
        total_down * unscale,
        total_up * unscale,
        grad_steps,
    )


MESH = pl.DeviceIdType.MESH
BF = jnp.bfloat16
F32 = jnp.float32
NT = (((1,), (1,)), ((), ()))
NN = (((1,), (0,)), ((), ()))


def dot(left, right, dims=NN):
    return lax.dot_general(left, right, dims, preferred_element_type=F32)


def attention_kernel(
    seq,
    head,
    q_in,
    k_in,
    code_in,
    do_in,
    tq_in,
    tk_in,
    tv_in,
    tdo_in,
    x_in,
    frac_in,
    up_in,
    down_in,
    step_ref,
    group_ref,
    time_ref,
    dq_ref,
    dk_ref,
    dv_ref,
    dqt_ref,
    dkt_ref,
    dvt_ref,
    down_ref,
    up_ref,
    steps_ref,
    q_ref,
    k_ref,
    code_ref,
    do_ref,
    x_ref,
    frac_ref,
    upw_ref,
    downw_ref,
    stage,
    recv,
    kv2,
    tkv,
    tqd,
    kall,
    ktr,
    vall,
    qall,
    doall,
    dqall,
    dkacc,
    dvacc,
    xo,
    xi,
    to,
    ti,
    ost,
    ret,
    tfin,
    rett,
    xlow_out,
    xlow_in,
    xst,
    xcol,
    up_out,
    up_in2,
    up_all,
    low_out,
    low_in,
    red_out,
    red_in,
    sum_out,
    sum_in,
    gath,
    li,
    s1,
    r1,
    s2,
    r2,
    st,
    rt,
    s3,
    r3,
    s4,
    r4,
    s5,
    r5,
    s6,
    r6,
    s7,
    r7,
    s8,
    r8,
    s9,
    r9,
    s10,
    r10,
    s11,
    r11,
    s12,
    r12,
):
    rows = q_ref.shape[0]
    heads = q_ref.shape[1] // HEAD_SIZE
    text = tq_in.shape[0]
    half = text // 2
    planes = head // 2
    peers = seq * planes
    group = tq_in.shape[1] // HEAD_SIZE
    pair = 2 * group
    first = (seq - pair) // 2
    image = peers * rows
    share = text // seq
    scale = HEAD_SIZE ** (-0.5)
    rank = upw_ref.shape[0]
    wide = x_ref.shape[1] // seq
    part = rank // head
    hrank = rank // 2
    hrows = rows // 2

    s = lax.axis_index("seq")
    g = lax.axis_index("head")
    c = lax.rem(g, 2)
    y = g // 2
    me = s * planes + y
    partner = (s, g + 1 - 2 * c)
    slot = s - first
    is_head = jnp.logical_and(slot >= 0, slot < pair)
    mine = y * pair + slot
    holds_text = jnp.logical_and(is_head, slot // group == c)
    takes_text = jnp.logical_and(is_head, slot // group != c)
    lane_block = lax.rem(slot, group)

    def peer(p):
        return (p // planes, lax.rem(p, planes) * 2 + c)

    def home(h):
        return (first + lax.rem(h, pair), (h // pair) * 2 + c)

    def home_peer(h):
        return (first + lax.rem(h, pair)) * planes + h // pair

    def send(src, dst, ssem, rsem, to_id):
        return pltpu.make_async_remote_copy(
            src_ref=src, dst_ref=dst, send_sem=ssem, recv_sem=rsem, device_id=to_id, device_id_type=MESH
        )

    loads = [
        pltpu.make_async_copy(src, dst, li.at[i])
        for i, (src, dst) in enumerate(
            (
                (k_in, k_ref),
                (code_in, code_ref),
                (q_in, q_ref),
                (do_in, do_ref),
                (x_in, x_ref),
                (down_in, downw_ref),
                (up_in, upw_ref),
                (frac_in, frac_ref),
            )
        )
    ]
    for load in loads:
        load.start()

    barrier = pltpu.get_barrier_semaphore()
    for i in range(1, peers):
        pl.semaphore_signal(
            barrier, inc=1, device_id=peer(lax.rem(me + i, peers)), device_id_type=MESH
        )
    for other in range(planes):
        pl.semaphore_signal(
            barrier, inc=1, device_id=(s, other * 2 + 1 - c), device_id_type=MESH
        )

    for load in loads[:4]:
        load.wait()
    for h in range(heads):
        cols = slice(h * HEAD_SIZE, (h + 1) * HEAD_SIZE)
        stage[h, 0:rows] = k_ref[:, cols]
        stage[h, rows : 2 * rows] = code_ref[:, cols].astype(F32).astype(BF)
        stage[h, 2 * rows : 3 * rows] = q_ref[:, cols]
        stage[h, 3 * rows : 4 * rows] = do_ref[:, cols]

    pl.semaphore_wait(barrier, peers - 1 + planes)

    def first_send(h, k):
        at = pl.ds(k * 2 * rows, 2 * rows)
        return send(stage.at[h, at], recv.at[me, at], s1.at[k, h], r1.at[k, me], home(h))

    def first_recv(p, k):
        at = pl.ds(k * 2 * rows, 2 * rows)
        return send(stage.at[0, at], recv.at[p, at], s1.at[k, 0], r1.at[k, p], partner)

    for k in range(2):
        for i in range(heads):
            h = lax.rem(me + i, heads)

            @pl.when(me != home_peer(h))
            def _():
                first_send(h, k).start()

    def text_sources():
        cols = pl.ds(pl.multiple_of(lane_block * HEAD_SIZE, HEAD_SIZE), HEAD_SIZE)
        return cols, pl.ds(0, half), pl.ds(half, half)

    def text_copies():
        cols, _, low = text_sources()
        return (
            send(tk_in.at[:, cols], tkv.at[0], st.at[0], rt.at[0], partner),
            send(tv_in.at[:, cols], tkv.at[1], st.at[1], rt.at[1], partner),
            send(tq_in.at[low, cols], tqd.at[0], st.at[2], rt.at[2], partner),
            send(tdo_in.at[low, cols], tqd.at[1], st.at[3], rt.at[3], partner),
        )

    def text_loads():
        cols, high, _ = text_sources()
        return (
            pltpu.make_async_copy(tk_in.at[:, cols], tkv.at[0], li.at[8]),
            pltpu.make_async_copy(tv_in.at[:, cols], tkv.at[1], li.at[9]),
            pltpu.make_async_copy(tq_in.at[high, cols], tqd.at[0], li.at[10]),
            pltpu.make_async_copy(tdo_in.at[high, cols], tqd.at[1], li.at[11]),
        )

    @pl.when(holds_text)
    def _():
        for copy in text_copies() + text_loads():
            copy.start()

    for load in loads[4:6]:
        load.wait()
    for t in range(seq):
        xst[t] = x_ref[:, t * wide : (t + 1) * wide]

    def column_send(t):
        return send(xst.at[t], xcol.at[s], s6.at[t], r6.at[s], (t, g))

    xlow = dot(x_ref[...], downw_ref[...], NT)
    xlow_out[...] = jnp.concatenate([xlow[0:hrows], xlow[hrows:rows]], axis=1).astype(BF)

    def low_send(h):
        return send(xlow_out, xlow_in.at[me], s7.at[h], r7.at[me], home(h))

    for i in range(heads):
        h = lax.rem(me + i, heads)

        @pl.when(me != home_peer(h))
        def _():
            low_send(h).start()

    for load in loads[6:8]:
        load.wait()

    def up_send(p):
        return send(
            up_out.at[c], up_all.at[mine, c], s9.at[p], r9.at[mine], peer(p)
        )

    def column_sends():
        for i in range(1, seq):
            column_send(lax.rem(s + i, seq)).start()
        xcol[pl.ds(s, 1)] = xst[pl.ds(s, 1)]

    @pl.when(jnp.logical_not(is_head))
    def _():
        column_sends()

    def up_trade():
        return send(up_in2.at[0, 1 - c], up_in2.at[1, 0], s8.at[0], r8.at[0], partner)

    def text_trade():
        return send(to, ti, s3.at[2], r3.at[2], partner)

    def back_query(p):
        return send(
            dqall.at[pl.ds(pl.multiple_of(p * rows, rows), rows)], ret.at[mine, pl.ds(0, rows)],
            s4.at[0, p], r4.at[0, mine], peer(p)
        )

    def back_send(k, p):
        at = pl.ds(k * rows, rows)
        return send(ost.at[p, at], ret.at[mine, at], s4.at[k, p], r4.at[k, mine], peer(p))

    def back_recv(k, h):
        at = pl.ds(k * rows, rows)
        return send(ost.at[0, at], ret.at[h, at], s4.at[k, 0], r4.at[k, h], partner)

    def trade(k):
        return send(xo.at[k], xi.at[k], s3.at[k], r3.at[k], partner)

    @pl.when(is_head)
    def _():
        recv[pl.ds(me, 1)] = stage[pl.ds(mine, 1)]
        xlow_in[pl.ds(me, 1)] = xlow_out[...].reshape(1, hrows, HEAD_SIZE)
        for i in range(1, peers):
            p = lax.rem(me + i, peers)
            first_recv(p, 0).wait_recv()

        swap = send(recv.at[:, pl.ds(0, 2 * rows)], kv2, s2.at[0], r2.at[0], partner)
        swap.start()
        step = step_ref[group_ref[time_ref[0]], mine]

        def dequant(codes):
            return (codes.reshape(image, HEAD_SIZE).astype(F32) * step).astype(BF)

        kall[0:image] = recv[:, 0:rows].reshape(image, HEAD_SIZE)
        vall[0:image] = dequant(recv[:, rows : 2 * rows])
        for i in range(1, peers):
            p = lax.rem(me + i, peers)
            first_recv(p, 1).wait_recv()

        column_sends()
        qall[0:image] = recv[:, 2 * rows : 3 * rows].reshape(image, HEAD_SIZE)
        doall[0:image] = recv[:, 3 * rows : 4 * rows].reshape(image, HEAD_SIZE)

        @pl.when(takes_text)
        def _():
            for copy in text_copies():
                copy.wait_recv()

        @pl.when(holds_text)
        def _():
            for copy in text_loads():
                copy.wait()

        kall[2 * image : 2 * image + text] = tkv[0]
        vall[2 * image : 2 * image + text] = tkv[1]
        qall[image : image + half] = tqd[0]
        doall[image : image + half] = tqd[1]
        swap.wait_recv()
        kall[image : 2 * image] = kv2[:, 0:rows].reshape(image, HEAD_SIZE)
        vall[image : 2 * image] = dequant(kv2[:, rows : 2 * rows])
        ktr[...] = kall[...].T

        def weights(index):
            at = slice(index * half, (index + 1) * half)
            queries, grads = qall[at], doall[at]
            scores = dot(kall[...], queries, NT)
            dprobs = dot(vall[...], grads, NT)
            top = jnp.max(scores, axis=0, keepdims=True) * (scale * math.log2(math.e))
            expo = jnp.exp2(scores * (scale * math.log2(math.e)) - top)
            probs = expo * (1.0 / jnp.sum(expo, axis=0, keepdims=True))
            value_part = dot(probs.astype(BF), grads)
            dvacc[...] = value_part if index == 0 else dvacc[...] + value_part
            return probs, dprobs

        def score_grads(probs, dprobs):
            deltas = jnp.sum(probs * dprobs, axis=0, keepdims=True)
            return (probs * (dprobs - deltas)).astype(BF)

        def key_query(index, dscores):
            at = slice(index * half, (index + 1) * half)
            key_part = dot(dscores, qall[at])
            dkacc[...] = key_part if index == 0 else dkacc[...] + key_part
            dqall[at] = (dot(ktr[...], dscores).T * scale).astype(BF)

        last = image // half
        for index in range(last):
            key_query(index, score_grads(*weights(index)))
        for i in range(1, peers):
            back_query(lax.rem(me + i, peers)).start()
        last_weights = weights(last)
        xo[1] = dvacc[image : 2 * image].astype(BF)
        trade(1).start()
        last_grads = score_grads(*last_weights)
        trade(1).wait_recv()
        ost[:, 2 * rows : 3 * rows] = (
            (dvacc[0:image] + xi[1].astype(F32)).astype(BF).reshape(peers, rows, HEAD_SIZE)
        )
        for i in range(1, peers):
            back_send(2, lax.rem(me + i, peers)).start()
        ret[pl.ds(mine, 1), 2 * rows : 3 * rows] = ost[pl.ds(me, 1), 2 * rows : 3 * rows]
        key_query(last, last_grads)
        xo[0] = (dkacc[image : 2 * image] * scale).astype(BF)
        trade(0).start()

        @pl.when(takes_text)
        def _():
            to[0:text] = (dkacc[2 * image : 2 * image + text] * scale).astype(BF)
            to[text : 2 * text] = dvacc[2 * image : 2 * image + text].astype(BF)
            to[2 * text : 2 * text + half] = dqall[image : image + half]
            text_trade().start()

        for i in range(1, peers):
            p = lax.rem(me + i, peers)
            send(xlow_out, xlow_in.at[p], s7.at[0], r7.at[p], partner).wait_recv()

        codes = recv[:, rows : 2 * rows]
        kept = jnp.where(jnp.abs(codes.astype(F32)) < QMAX, ost[:, 2 * rows : 3 * rows].astype(F32), 0.0)
        kept = kept.astype(BF)
        low_rows = xlow_in[...].reshape(peers * hrows, HEAD_SIZE).T
        early = dot(low_rows, kept[:, 0:hrows].reshape(peers * hrows, HEAD_SIZE))
        late = dot(low_rows, kept[:, hrows:rows].reshape(peers * hrows, HEAD_SIZE))
        part_up = (early[0:rank] + late[rank : 2 * rank]).reshape(2, hrank, HEAD_SIZE)
        up_in2[0] = part_up
        up_trade().start()

    for h in range(heads):

        @pl.when(me != home_peer(h))
        def _():
            back_recv(2, h).wait_recv()

    sums = []
    for h in range(heads):
        cols = slice(h * HEAD_SIZE, (h + 1) * HEAD_SIZE)
        codes = code_ref[:, cols]
        inside = jnp.abs(codes) < QMAX
        value_grad = ret[h, 2 * rows : 3 * rows].astype(F32)
        kept = jnp.where(inside, value_grad, 0.0).astype(BF)
        lsq_term = jnp.where(inside, -frac_ref[:, cols].astype(F32), codes.astype(F32))
        sums.append(jnp.sum(value_grad * lsq_term, axis=0, keepdims=True))
        dv_ref[:, cols] = kept

    low = dot(dv_ref[...], upw_ref[...], NT)
    sums.append(jnp.zeros((rows - heads, HEAD_SIZE), F32))
    step_terms = jnp.sum(jnp.concatenate(sums, axis=0), axis=1, keepdims=True)
    step_high = step_terms.astype(BF).astype(F32)
    lane_at = lax.broadcasted_iota(jnp.int32, (rows, rank), 1)
    beside = jnp.where(lane_at == 0, step_high, jnp.where(lane_at == 1, step_terms - step_high, 0.0))
    low_out[...] = jnp.concatenate([low, beside], axis=1).astype(BF)

    def tile_send(t):
        return send(low_out, low_in.at[s], s10.at[t], r10.at[s], (t, g))

    for i in range(1, seq):
        tile_send(lax.rem(s + i, seq)).start()
    low_in[pl.ds(s, 1)] = low_out[...].reshape(1, rows, HEAD_SIZE)

    @pl.when(is_head)
    def _():
        trade(0).wait_recv()
        ost[:, rows : 2 * rows] = (
            (dkacc[0:image] * scale + xi[0].astype(F32)).astype(BF).reshape(peers, rows, HEAD_SIZE)
        )
        for i in range(1, peers):
            back_send(1, lax.rem(me + i, peers)).start()
        ret[pl.ds(mine, 1), rows : 2 * rows] = ost[pl.ds(me, 1), rows : 2 * rows]
        ret[pl.ds(mine, 1), 0:rows] = dqall[pl.ds(pl.multiple_of(me * rows, rows), rows)].reshape(
            1, rows, HEAD_SIZE
        )

    for i in range(1, seq):
        t = lax.rem(s + i, seq)
        send(xst.at[0], xcol.at[t], s6.at[0], r6.at[t], partner).wait_recv()
        send(low_out, low_in.at[t], s10.at[0], r10.at[t], partner).wait_recv()

    tiles = low_in[...]
    flat = tiles.reshape(seq * rows, HEAD_SIZE).T
    block = dot(flat, xcol[...].reshape(seq * rows, wide))[0:rank]
    step_group = jnp.sum(tiles[:, 0:16].astype(F32), axis=0)
    red_out[...] = block.astype(BF).reshape(head, part, wide)
    sum_out[...] = step_group

    def reduce_send(other):
        return send(red_out.at[other], red_in.at[g], s11.at[0, other], r11.at[0, g], (s, other))

    def sum_send(other):
        return send(sum_out, sum_in.at[g], s11.at[1, other], r11.at[1, g], (s, other))

    for i in range(1, head):
        reduce_send(lax.rem(g + i, head)).start()
    for i in range(1, head):
        sum_send(lax.rem(g + i, head)).start()
    red_in[pl.ds(g, 1)] = red_out[pl.ds(g, 1)]
    sum_in[pl.ds(g, 1)] = step_group.reshape(1, 16, HEAD_SIZE)

    @pl.when(is_head)
    def _():
        @pl.when(holds_text)
        def _():
            text_trade().wait_recv()
            full = (seq, share, HEAD_SIZE)
            tfin[0 : seq // 2, 0] = dqall[image : image + half].reshape(seq // 2, share, HEAD_SIZE)
            tfin[seq // 2 : seq, 0] = ti[2 * text : 2 * text + half].reshape(seq // 2, share, HEAD_SIZE)
            tfin[:, 1] = (
                (dkacc[2 * image : 2 * image + text] * scale + ti[0:text].astype(F32)).astype(BF).reshape(full)
            )
            tfin[:, 2] = (
                (dvacc[2 * image : 2 * image + text] + ti[text : 2 * text].astype(F32)).astype(BF).reshape(full)
            )
            for i in range(1, seq):
                other = lax.rem(s + i, seq)
                send(
                    tfin.at[other], rett.at[lane_block], s5.at[other], r5.at[lane_block], (other, g)
                ).start()

            rett[pl.ds(lane_block, 1)] = tfin[pl.ds(s, 1)]

        up_trade().wait_recv()
        up_out[pl.ds(c, 1)] = (
            (up_in2[pl.ds(0, 1), pl.ds(c, 1)] + up_in2[pl.ds(1, 1), pl.ds(0, 1)]) * unscale
        ).astype(BF).reshape(1, hrank, HEAD_SIZE)
        for i in range(1, peers):
            up_send(lax.rem(me + i, peers)).start()
        up_all[pl.ds(mine, 1), pl.ds(c, 1)] = up_out[pl.ds(c, 1)].reshape(1, 1, hrank, HEAD_SIZE)

    for i in range(1, head):
        other = lax.rem(g + i, head)
        send(red_out.at[0], red_in.at[other], s11.at[0, 0], r11.at[0, other], partner).wait_recv()

    summed = jnp.sum(red_in[...].astype(F32), axis=0) * unscale
    gath[pl.ds(y, 1), pl.ds(c, 1), pl.ds(s, 1)] = summed.astype(BF).reshape(1, 1, 1, part, wide)

    def row_send(p):
        return send(gath.at[y, c, s], gath.at[y, c, s], s12.at[p], r12.at[me], peer(p))

    def core_send():
        return send(gath.at[:, c], gath.at[:, c], s12.at[peers], r12.at[peers], partner)

    def core_up_send():
        return send(up_all.at[:, c], up_all.at[:, c], s8.at[1], r8.at[1], partner)

    for i in range(1, peers):
        row_send(lax.rem(me + i, peers)).start()

    for j in range(group):

        @pl.when(s != first + c * group + j)
        def _():
            send(tfin.at[0], rett.at[j], s5.at[0], r5.at[j], partner).wait_recv()

        cols = slice(j * HEAD_SIZE, (j + 1) * HEAD_SIZE)
        dqt_ref[:, cols] = rett[j, 0]
        dkt_ref[:, cols] = rett[j, 1]
        dvt_ref[:, cols] = rett[j, 2]

    for h in range(heads):

        @pl.when(me != home_peer(h))
        def _():
            back_recv(0, h).wait_recv()
            back_recv(1, h).wait_recv()

    for h in range(heads):
        cols = slice(h * HEAD_SIZE, (h + 1) * HEAD_SIZE)
        dq_ref[:, cols] = ret[h, 0:rows]
        dk_ref[:, cols] = ret[h, rows : 2 * rows]

    slot_index = group_ref[time_ref[0]]
    for i in range(1, head):
        other = lax.rem(g + i, head)
        send(sum_out, sum_in.at[other], s11.at[1, 0], r11.at[1, other], partner).wait_recv()

    lanes = jnp.sum(sum_in[...], axis=0)
    lane_at = lax.broadcasted_iota(jnp.int32, (16, HEAD_SIZE), 1)
    row_at = lax.broadcasted_iota(jnp.int32, (16, HEAD_SIZE), 0)
    chosen = jnp.logical_or(lane_at == rank, lane_at == rank + 1)
    head_sums = jnp.sum(jnp.where(chosen, lanes, 0.0), axis=1, keepdims=True)
    step_row = jnp.sum(jnp.where(lane_at == row_at, head_sums, 0.0), axis=0, keepdims=True)[:, 0:heads]
    step_row = step_row * (QMAX ** (-0.5) * unscale)
    slots = steps_ref.shape[0]
    slot_at = lax.broadcasted_iota(jnp.int32, (slots, heads), 0)
    steps_ref[...] = jnp.where(slot_at == slot_index, jnp.broadcast_to(step_row, (slots, heads)), 0.0)

    for h in range(heads):

        @pl.when(me != home_peer(h))
        def _():
            send(up_out.at[0], up_all.at[h, c], s9.at[0], r9.at[h], partner).wait_recv()

    core_up_send().start()

    for i in range(1, peers):
        p = lax.rem(me + i, peers)
        block_at = gath.at[lax.rem(p, planes), c, p // planes]
        send(block_at, block_at, s12.at[0], r12.at[p], partner).wait_recv()

    core_send().start()
    send(up_all.at[:, 1 - c], up_all.at[:, 1 - c], s8.at[1], r8.at[1], partner).wait_recv()
    for h in range(heads):
        cols = slice(h * HEAD_SIZE, (h + 1) * HEAD_SIZE)
        up_ref[:, cols] = up_all[h].reshape(rank, HEAD_SIZE).astype(F32)
    send(gath.at[:, 1 - c], gath.at[:, 1 - c], s12.at[peers], r12.at[peers], partner).wait_recv()
    for t in range(seq):
        down_ref[:, t * wide : (t + 1) * wide] = gath[:, :, t].reshape(rank, wide).astype(F32)

    for h in range(heads):

        @pl.when(me != home_peer(h))
        def _():
            first_send(h, 0).wait_send()
            first_send(h, 1).wait_send()
            low_send(h).wait_send()

    for i in range(1, seq):
        t = lax.rem(s + i, seq)
        column_send(t).wait_send()
        tile_send(t).wait_send()
    for i in range(1, head):
        reduce_send(lax.rem(g + i, head)).wait_send()
        sum_send(lax.rem(g + i, head)).wait_send()
    for i in range(1, peers):
        row_send(lax.rem(me + i, peers)).wait_send()
    core_send().wait_send()
    core_up_send().wait_send()

    @pl.when(is_head)
    def _():
        send(recv.at[:, pl.ds(0, 2 * rows)], kv2, s2.at[0], r2.at[0], partner).wait_send()
        trade(0).wait_send()
        trade(1).wait_send()
        up_trade().wait_send()
        for i in range(1, peers):
            p = lax.rem(me + i, peers)
            back_query(p).wait_send()
            back_send(1, p).wait_send()
            back_send(2, p).wait_send()
            up_send(p).wait_send()

    @pl.when(takes_text)
    def _():
        text_trade().wait_send()

    @pl.when(holds_text)
    def _():
        for copy in text_copies():
            copy.wait_send()
        for i in range(1, seq):
            other = lax.rem(s + i, seq)
            send(
                tfin.at[other], rett.at[lane_block], s5.at[other], r5.at[lane_block], (other, g)
            ).wait_send()


def settle_kernel(count, *refs):
    sources, targets, held = refs[:count], refs[count : 2 * count], refs[2 * count : 3 * count]
    came, went = refs[3 * count :]
    loads = [pltpu.make_async_copy(a, b, came.at[i]) for i, (a, b) in enumerate(zip(sources, held))]
    stores = [pltpu.make_async_copy(a, b, went.at[i]) for i, (a, b) in enumerate(zip(held, targets))]
    for load in loads:
        load.start()
    for load, store in zip(loads, stores):
        load.wait()
        store.start()
    for store in stores:
        store.wait()


def settle(arrays):
    count = len(arrays)
    anywhere = pl.BlockSpec(memory_space=pl.ANY)
    return pl.pallas_call(
        functools.partial(settle_kernel, count),
        out_shape=[jax.ShapeDtypeStruct(a.shape, a.dtype) for a in arrays],
        in_specs=[anywhere] * count,
        out_specs=[anywhere] * count,
        scratch_shapes=[pltpu.VMEM(a.shape, a.dtype) for a in arrays]
        + [pltpu.SemaphoreType.DMA((count,))] * 2,
        compiler_params=pltpu.CompilerParams(vmem_limit_bytes=56 * 1024 * 1024),
        name="settle",
    )(*arrays)


def whole_heads(
    seq,
    head,
    image_input_rows,
    adapter_down_weight,
    adapter_up_weight,
    image_query_rows,
    image_key_rows,
    image_value_codes,
    value_fraction,
    value_step_sizes,
    timestep_group,
    timestep,
    image_output_grad,
    text_query_rows,
    text_key_rows,
    text_value_rows,
    text_output_grad,
):
    rows, width = image_query_rows.shape
    text, text_width = text_query_rows.shape
    heads, group = width // HEAD_SIZE, text_width // HEAD_SIZE
    peers = seq * head // 2
    image, share = peers * rows, text // seq
    keys = 2 * image + text
    rank, wide = adapter_up_weight.shape[0], image_input_rows.shape[1] // seq
    planes = head // 2
    vmem = pl.BlockSpec(memory_space=pltpu.VMEM)
    sems = pltpu.SemaphoreType.DMA
    hbm = pl.BlockSpec(memory_space=pl.ANY)
    smem = pl.BlockSpec(memory_space=pltpu.SMEM)
    results = pl.pallas_call(
        functools.partial(attention_kernel, seq, head),
        out_shape=[jax.ShapeDtypeStruct((rows, width), BF)] * 3
        + [jax.ShapeDtypeStruct((share, text_width), BF)] * 3
        + [
            jax.ShapeDtypeStruct(adapter_down_weight.shape[::-1], F32),
            jax.ShapeDtypeStruct(adapter_up_weight.shape, F32),
            jax.ShapeDtypeStruct(value_step_sizes.shape, F32),
        ],
        in_specs=[hbm] * 12 + [smem] * 3,
        out_specs=[vmem] * 9,
        scratch_shapes=[
            pltpu.VMEM((rows, width), BF),
            pltpu.VMEM((rows, width), BF),
            pltpu.VMEM((rows, width), jnp.int32),
            pltpu.VMEM((rows, width), BF),
            pltpu.VMEM(image_input_rows.shape, BF),
            pltpu.VMEM((rows, width), BF),
            pltpu.VMEM(adapter_up_weight.shape, BF),
            pltpu.VMEM(adapter_down_weight.shape[::-1], BF),
            pltpu.VMEM((heads, 4 * rows, HEAD_SIZE), BF),
            pltpu.VMEM((peers, 4 * rows, HEAD_SIZE), BF),
            pltpu.VMEM((peers, 2 * rows, HEAD_SIZE), BF),
            pltpu.VMEM((2, text, HEAD_SIZE), BF),
            pltpu.VMEM((2, text // 2, HEAD_SIZE), BF),
            pltpu.VMEM((keys, HEAD_SIZE), BF),
            pltpu.VMEM((HEAD_SIZE, keys), BF),
            pltpu.VMEM((keys, HEAD_SIZE), BF),
            pltpu.VMEM((image + text // 2, HEAD_SIZE), BF),
            pltpu.VMEM((image + text // 2, HEAD_SIZE), BF),
            pltpu.VMEM((image + text // 2, HEAD_SIZE), BF),
            pltpu.VMEM((keys, HEAD_SIZE), F32),
            pltpu.VMEM((keys, HEAD_SIZE), F32),
            pltpu.VMEM((2, image, HEAD_SIZE), BF),
            pltpu.VMEM((2, image, HEAD_SIZE), BF),
            pltpu.VMEM((2 * text + text // 2, HEAD_SIZE), BF),
            pltpu.VMEM((2 * text + text // 2, HEAD_SIZE), BF),
            pltpu.VMEM((peers, 3 * rows, HEAD_SIZE), BF),
            pltpu.VMEM((heads, 3 * rows, HEAD_SIZE), BF),
            pltpu.VMEM((seq, 3, share, HEAD_SIZE), BF),
            pltpu.VMEM((group, 3, share, HEAD_SIZE), BF),
            pltpu.VMEM((rows // 2, HEAD_SIZE), BF),
            pltpu.VMEM((peers, rows // 2, HEAD_SIZE), BF),
            pltpu.VMEM((seq, rows, wide), BF),
            pltpu.VMEM((seq, rows, wide), BF),
            pltpu.VMEM((2, rank // 2, HEAD_SIZE), BF),
            pltpu.VMEM((2, 2, rank // 2, HEAD_SIZE), F32),
            pltpu.VMEM((heads, 2, rank // 2, HEAD_SIZE), BF),
            pltpu.VMEM((rows, HEAD_SIZE), BF),
            pltpu.VMEM((seq, rows, HEAD_SIZE), BF),
            pltpu.VMEM((head, rank // head, wide), BF),
            pltpu.VMEM((head, rank // head, wide), BF),
            pltpu.VMEM((16, HEAD_SIZE), F32),
            pltpu.VMEM((head, 16, HEAD_SIZE), F32),
            pltpu.VMEM((planes, 2, seq, rank // head, wide), BF),
            sems((12,)),
            sems((2, heads)),
            sems((2, peers)),
            sems((1,)),
            sems((1,)),
            sems((4,)),
            sems((4,)),
            sems((3,)),
            sems((3,)),
            sems((3, peers)),
            sems((3, heads)),
            sems((seq,)),
            sems((group,)),
            sems((seq,)),
            sems((seq,)),
            sems((heads,)),
            sems((peers,)),
            sems((2,)),
            sems((2,)),
            sems((peers,)),
            sems((heads,)),
            sems((seq,)),
            sems((seq,)),
            sems((2, head)),
            sems((2, head)),
            sems((peers + 1,)),
            sems((peers + 1,)),
        ],
        compiler_params=pltpu.CompilerParams(
            collective_id=0, has_side_effects=True, vmem_limit_bytes=56 * 1024 * 1024
        ),
        name="whole_heads",
    )(
        image_query_rows,
        image_key_rows,
        image_value_codes,
        image_output_grad,
        text_query_rows,
        text_key_rows,
        text_value_rows,
        text_output_grad,
        image_input_rows,
        value_fraction,
        adapter_up_weight,
        adapter_down_weight.T,
        value_step_sizes,
        timestep_group,
        timestep,
    )
    results = settle(results)
    return (*results[:6], results[6].T, *results[7:])


def pick(mesh):
    seq, head = mesh.shape["seq"], mesh.shape["head"]

    def chosen(*arguments):
        rows, width = arguments[3].shape
        text, text_width = arguments[11].shape
        pair = 2 * text_width // HEAD_SIZE
        fits = (
            head % 2 == 0
            and seq % 2 == 0
            and seq >= pair
            and rows % 32 == 0
            and 2 * arguments[2].shape[0] == HEAD_SIZE
            and width // HEAD_SIZE <= 16
            and (text // 2) % rows == 0
            and (seq * head // 2 * rows) % (text // 2) == 0
            and arguments[2].shape[0] % (16 * head) == 0
            and arguments[0].shape[1] % (seq * HEAD_SIZE) == 0
            and text % (seq * 16) == 0
            and (seq * head // 2 * rows) % (text // 2) == 0
            and (seq * head * rows + text) * HEAD_SIZE <= 1 << 18
        )
        if fits:
            return whole_heads(seq, head, *arguments)
        return on_device(*arguments)

    return chosen


def solution(mesh):
    placed = (
        P(("seq", "head"), None),
        P(),
        P(),
        P(("seq", "head"), None),
        P(("seq", "head"), None),
        P(("seq", "head"), None),
        P(("seq", "head"), None),
        P(),
        P(),
        P(),
        P(("seq", "head"), None),
        P(None, "head"),
        P(None, "head"),
        P(None, "head"),
        P(None, "head"),
    )
    return jax.shard_map(
        pick(mesh),
        mesh=mesh,
        in_specs=placed,
        out_specs=(
            P(("seq", "head"), None),
            P(("seq", "head"), None),
            P(("seq", "head"), None),
            P("seq", "head"),
            P("seq", "head"),
            P("seq", "head"),
            P(),
            P(),
            P(),
        ),
        check_vma=False,
    )
```

```python
import functools
import math

import jax
import jax.numpy as jnp
from jax import lax
from jax.experimental import pallas as pl
from jax.experimental.pallas import tpu as pltpu
from jax.sharding import PartitionSpec as P

HEAD_SIZE = 128
QMAX = 127


unscale = 0.0078125


def split_heads(rows):
    return rows.reshape(rows.shape[0], rows.shape[1] // HEAD_SIZE, HEAD_SIZE)


def join_heads(heads):
    return heads.reshape(heads.shape[0], heads.shape[1] * heads.shape[2])


def head_scores(queries, key_rows):
    return jnp.einsum(
        "qhd,khd->hqk", queries, key_rows, preferred_element_type=jnp.float32
    ) * HEAD_SIZE ** (-0.5)


def over_keys(step_fn, initial, key_rows, value_rows):
    block_rows = math.gcd(key_rows.shape[0], 2048)

    def over_one_turn(turn_index, carried):
        key_block = lax.dynamic_slice_in_dim(key_rows, turn_index * block_rows, block_rows, 0)
        value_block = lax.dynamic_slice_in_dim(value_rows, turn_index * block_rows, block_rows, 0)
        return step_fn(carried, key_block, value_block)

    return lax.fori_loop(0, key_rows.shape[0] // block_rows, over_one_turn, initial)


def key_terms(carried, queries, grads, log_rows, delta_rows, own_keys, own_values):
    key_grad, value_grad = carried
    probs = jnp.exp(head_scores(queries, own_keys) - log_rows.T[:, :, None])
    dprobs = jnp.einsum("qhd,khd->hqk", grads, own_values, preferred_element_type=jnp.float32)
    dscores = (probs * (dprobs - delta_rows.T[:, :, None])).astype(jnp.bfloat16)
    value_grad = value_grad + jnp.einsum(
        "hqk,qhd->khd", probs.astype(jnp.bfloat16), grads, preferred_element_type=jnp.float32
    )
    key_grad = key_grad + jnp.einsum(
        "hqk,qhd->khd", dscores, queries, preferred_element_type=jnp.float32
    ) * HEAD_SIZE ** (-0.5)
    return (key_grad, value_grad)


def on_device(
    image_input_rows,
    adapter_down_weight,
    adapter_up_weight,
    image_query_rows,
    image_key_rows,
    image_value_codes,
    value_fraction,
    value_step_sizes,
    timestep_group,
    timestep,
    image_output_grad,
    text_query_rows,
    text_key_rows,
    text_value_rows,
    text_output_grad,
):
    slot_index = jnp.sum(
        jnp.where(
            jnp.arange(timestep_group.shape[0], dtype=jnp.int32) == timestep[0], timestep_group, 0
        )
    )
    slot_rows = jnp.arange(value_step_sizes.shape[0], dtype=jnp.int32) == slot_index
    step_row = jnp.sum(jnp.where(slot_rows[:, None], value_step_sizes, 0.0), axis=0)
    code_values = image_value_codes.astype(jnp.float32)
    v_dequant = (code_values * jnp.repeat(step_row, HEAD_SIZE)[None, :]).astype(jnp.bfloat16)
    inside = jnp.abs(image_value_codes) < QMAX
    lsq_term = jnp.where(inside, -value_fraction.astype(jnp.float32), code_values)
    query_img, key_img, value_img, grad_img = (
        lax.all_to_all(image_query_rows, "head", split_axis=1, concat_axis=0, tiled=True),
        lax.all_to_all(image_key_rows, "head", split_axis=1, concat_axis=0, tiled=True),
        lax.all_to_all(v_dequant, "head", split_axis=1, concat_axis=0, tiled=True),
        lax.all_to_all(image_output_grad, "head", split_axis=1, concat_axis=0, tiled=True),
    )
    share_rows = text_query_rows.shape[0] // lax.axis_size("seq")
    first_row = lax.axis_index("seq") * share_rows

    def own_rows(table):
        return lax.dynamic_slice_in_dim(table, first_row, share_rows, 0)

    image_rows = query_img.shape[0]
    query_local = jnp.concatenate([query_img, own_rows(text_query_rows)], axis=0)
    grad_local = jnp.concatenate([grad_img, own_rows(text_output_grad)], axis=0)
    query_split = split_heads(query_local)
    grad_split = split_heads(grad_local)
    local_count = query_split.shape[0]
    head_count = query_split.shape[1]
    key_image, value_image = (
        lax.all_gather(key_img, "seq", axis=0, tiled=True),
        lax.all_gather(value_img, "seq", axis=0, tiled=True),
    )
    text_keys = split_heads(text_key_rows)
    text_values = split_heads(text_value_rows)
    key_sets = ((split_heads(key_image), split_heads(value_image)), (text_keys, text_values))

    def stat_turn(carried, key_block, value_block):
        row_max, running, weighted = carried
        scores = head_scores(query_split, key_block)
        dprobs = jnp.einsum(
            "qhd,khd->hqk", grad_split, value_block, preferred_element_type=jnp.float32
        )
        new_max = jnp.maximum(row_max, jnp.max(scores, axis=2, keepdims=True))
        factor = jnp.exp(row_max - new_max)
        expo = jnp.exp(scores - new_max)
        running = running * factor + jnp.sum(expo, axis=2, keepdims=True)
        weighted = weighted * factor + jnp.sum(expo * dprobs, axis=2, keepdims=True)
        return (new_max, running, weighted)

    row_stats = (
        jnp.full((head_count, local_count, 1), -jnp.inf, jnp.float32),
        jnp.zeros((head_count, local_count, 1), jnp.float32),
        jnp.zeros((head_count, local_count, 1), jnp.float32),
    )
    for key_rows, value_rows in key_sets:
        row_stats = over_keys(stat_turn, row_stats, key_rows, value_rows)
    log_sums = row_stats[0] + jnp.log(row_stats[1])
    deltas = row_stats[2] / row_stats[1]

    def query_turn(running, key_block, value_block):
        probs = jnp.exp(head_scores(query_split, key_block) - log_sums)
        dprobs = jnp.einsum(
            "qhd,khd->hqk", grad_split, value_block, preferred_element_type=jnp.float32
        )
        dscores = (probs * (dprobs - deltas)).astype(jnp.bfloat16)
        return running + jnp.einsum(
            "hqk,khd->qhd", dscores, key_block, preferred_element_type=jnp.float32
        ) * HEAD_SIZE ** (-0.5)

    query_grad = jnp.zeros((local_count, head_count, HEAD_SIZE), jnp.float32)
    for key_rows, value_rows in key_sets:
        query_grad = over_keys(query_turn, query_grad, key_rows, value_rows)
    query_grad = join_heads(query_grad).astype(jnp.bfloat16)
    log_rows = log_sums[:, :, 0].T
    delta_rows = deltas[:, :, 0].T
    own_keys = split_heads(key_img)
    own_values = split_heads(value_img)
    empty = jnp.zeros(own_keys.shape, jnp.float32)
    query_rows = lax.all_gather(query_local.astype(jnp.float32), "seq", axis=0, tiled=True).astype(
        jnp.bfloat16
    )
    grad_rows = lax.all_gather(grad_local.astype(jnp.float32), "seq", axis=0, tiled=True).astype(
        jnp.bfloat16
    )
    log_part = lax.all_gather(log_rows, "seq", axis=0, tiled=True)
    delta_part = lax.all_gather(delta_rows, "seq", axis=0, tiled=True)
    piece_rows = query_rows.shape[0]
    block_rows = piece_rows if piece_rows <= 2048 else math.gcd(piece_rows, 2048)

    def fold_one_turn(turn_index, running):

        def rows_of(table):
            return lax.dynamic_slice_in_dim(table, turn_index * block_rows, block_rows, 0)

        return key_terms(
            running,
            split_heads(rows_of(query_rows)),
            split_heads(rows_of(grad_rows)),
            rows_of(log_part),
            rows_of(delta_part),
            own_keys,
            own_values,
        )

    key_grad, value_grad = lax.fori_loop(0, piece_rows // block_rows, fold_one_turn, (empty, empty))
    key_grad = join_heads(key_grad).astype(jnp.bfloat16)
    value_grad = join_heads(value_grad).astype(jnp.bfloat16)
    text_empty = jnp.zeros(text_keys.shape, jnp.float32)
    text_key, text_value = key_terms(
        (text_empty, text_empty),
        query_split,
        grad_split,
        log_rows,
        delta_rows,
        text_keys,
        text_values,
    )
    text_key, text_value = (
        lax.psum_scatter(join_heads(text_key), "seq", scatter_dimension=0, tiled=True),
        lax.psum_scatter(join_heads(text_value), "seq", scatter_dimension=0, tiled=True),
    )
    dk_txt = text_key.astype(jnp.bfloat16)
    dv_txt = text_value.astype(jnp.bfloat16)
    dq_txt = query_grad[image_rows:]
    dq_heads = query_grad[:image_rows]
    dq_img, dk_img, dv_quant = (
        lax.all_to_all(dq_heads, "head", split_axis=0, concat_axis=1, tiled=True),
        lax.all_to_all(key_grad, "head", split_axis=0, concat_axis=1, tiled=True),
        lax.all_to_all(value_grad, "head", split_axis=0, concat_axis=1, tiled=True),
    )
    image_value_grad = jnp.where(inside, dv_quant, jnp.zeros_like(dv_quant))
    lowrank_gradient = jnp.einsum(
        "vg,zg->vz", image_value_grad, adapter_up_weight, preferred_element_type=jnp.float32
    ).astype(jnp.bfloat16)
    part_down = jnp.einsum(
        "td,tr->dr", image_input_rows, lowrank_gradient, preferred_element_type=jnp.float32
    )
    lowrank_input = jnp.dot(
        image_input_rows, adapter_down_weight, preferred_element_type=jnp.float32
    ).astype(jnp.bfloat16)
    part_up = jnp.einsum(
        "tr,tw->rw", lowrank_input, image_value_grad, preferred_element_type=jnp.float32
    )
    token_rows = dv_quant.shape[0]
    token_terms = (dv_quant.astype(jnp.float32) * lsq_term).reshape(
        token_rows, value_step_sizes.shape[1], HEAD_SIZE
    )
    total_down, total_up, step_sums = lax.psum(
        (part_down, part_up, jnp.sum(token_terms, axis=(0, 2))), ("seq", "head")
    )
    grad_steps = jnp.where(slot_rows[:, None], step_sums[None, :], 0.0) * (QMAX ** (-0.5) * unscale)
    return (
        dq_img,
        dk_img,
        image_value_grad,
        dq_txt,
        dk_txt,
        dv_txt,
        total_down * unscale,
        total_up * unscale,
        grad_steps,
    )


MESH = pl.DeviceIdType.MESH
BF = jnp.bfloat16
F32 = jnp.float32
NT = (((1,), (1,)), ((), ()))
NN = (((1,), (0,)), ((), ()))


def dot(left, right, dims=NN):
    return lax.dot_general(left, right, dims, preferred_element_type=F32)


def attention_kernel(
    seq,
    head,
    q_in,
    k_in,
    code_in,
    do_in,
    tq_in,
    tk_in,
    tv_in,
    tdo_in,
    x_in,
    frac_in,
    up_in,
    down_in,
    step_ref,
    group_ref,
    time_ref,
    dq_ref,
    dk_ref,
    dv_ref,
    dqt_ref,
    dkt_ref,
    dvt_ref,
    down_ref,
    up_ref,
    steps_ref,
    q_ref,
    k_ref,
    code_ref,
    do_ref,
    x_ref,
    frac_ref,
    upw_ref,
    downw_ref,
    stage,
    recv,
    kv2,
    tkv,
    tqd,
    kall,
    ktr,
    vall,
    qall,
    doall,
    dqall,
    dkacc,
    dvacc,
    xo,
    xi,
    to,
    ti,
    ost,
    ret,
    tfin,
    rett,
    xlow_out,
    xlow_in,
    xst,
    xcol,
    up_out,
    up_in2,
    up_all,
    low_out,
    low_in,
    red_out,
    red_in,
    sum_out,
    sum_in,
    gath,
    li,
    s1,
    r1,
    s2,
    r2,
    st,
    rt,
    s3,
    r3,
    s4,
    r4,
    s5,
    r5,
    s6,
    r6,
    s7,
    r7,
    s8,
    r8,
    s9,
    r9,
    s10,
    r10,
    s11,
    r11,
    s12,
    r12,
):
    rows = q_ref.shape[0]
    heads = q_ref.shape[1] // HEAD_SIZE
    text = tq_in.shape[0]
    half = text // 2
    planes = head // 2
    peers = seq * planes
    group = tq_in.shape[1] // HEAD_SIZE
    pair = 2 * group
    first = (seq - pair) // 2
    image = peers * rows
    share = text // seq
    scale = HEAD_SIZE ** (-0.5)
    rank = upw_ref.shape[0]
    wide = x_ref.shape[1] // seq
    part = rank // head
    hrank = rank // 2
    hrows = rows // 2

    s = lax.axis_index("seq")
    g = lax.axis_index("head")
    c = lax.rem(g, 2)
    y = g // 2
    me = s * planes + y
    partner = (s, g + 1 - 2 * c)
    slot = s - first
    is_head = jnp.logical_and(slot >= 0, slot < pair)
    mine = y * pair + slot
    holds_text = jnp.logical_and(is_head, slot // group == c)
    takes_text = jnp.logical_and(is_head, slot // group != c)
    lane_block = lax.rem(slot, group)

    def peer(p):
        return (p // planes, lax.rem(p, planes) * 2 + c)

    def home(h):
        return (first + lax.rem(h, pair), (h // pair) * 2 + c)

    def home_peer(h):
        return (first + lax.rem(h, pair)) * planes + h // pair

    def send(src, dst, ssem, rsem, to_id):
        return pltpu.make_async_remote_copy(
            src_ref=src, dst_ref=dst, send_sem=ssem, recv_sem=rsem, device_id=to_id, device_id_type=MESH
        )

    loads = [
        pltpu.make_async_copy(src, dst, li.at[i])
        for i, (src, dst) in enumerate(
            (
                (k_in, k_ref),
                (code_in, code_ref),
                (q_in, q_ref),
                (do_in, do_ref),
                (x_in, x_ref),
                (down_in, downw_ref),
                (up_in, upw_ref),
                (frac_in, frac_ref),
            )
        )
    ]
    for load in loads:
        load.start()

    barrier = pltpu.get_barrier_semaphore()
    for i in range(1, peers):
        pl.semaphore_signal(
            barrier, inc=1, device_id=peer(lax.rem(me + i, peers)), device_id_type=MESH
        )
    for other in range(planes):
        pl.semaphore_signal(
            barrier, inc=1, device_id=(s, other * 2 + 1 - c), device_id_type=MESH
        )

    for load in loads[:4]:
        load.wait()
    for h in range(heads):
        cols = slice(h * HEAD_SIZE, (h + 1) * HEAD_SIZE)
        stage[h, 0:rows] = k_ref[:, cols]
        stage[h, rows : 2 * rows] = code_ref[:, cols].astype(F32).astype(BF)
        stage[h, 2 * rows : 3 * rows] = q_ref[:, cols]
        stage[h, 3 * rows : 4 * rows] = do_ref[:, cols]

    pl.semaphore_wait(barrier, peers - 1 + planes)

    def first_send(h, k):
        at = pl.ds(k * 2 * rows, 2 * rows)
        return send(stage.at[h, at], recv.at[me, at], s1.at[k, h], r1.at[k, me], home(h))

    def first_recv(p, k):
        at = pl.ds(k * 2 * rows, 2 * rows)
        return send(stage.at[0, at], recv.at[p, at], s1.at[k, 0], r1.at[k, p], partner)

    for k in range(2):
        for i in range(heads):
            h = lax.rem(me + i, heads)

            @pl.when(me != home_peer(h))
            def _():
                first_send(h, k).start()

    def text_sources():
        cols = pl.ds(pl.multiple_of(lane_block * HEAD_SIZE, HEAD_SIZE), HEAD_SIZE)
        return cols, pl.ds(0, half), pl.ds(half, half)

    def text_copies():
        cols, _, low = text_sources()
        return (
            send(tk_in.at[:, cols], tkv.at[0], st.at[0], rt.at[0], partner),
            send(tv_in.at[:, cols], tkv.at[1], st.at[1], rt.at[1], partner),
            send(tq_in.at[low, cols], tqd.at[0], st.at[2], rt.at[2], partner),
            send(tdo_in.at[low, cols], tqd.at[1], st.at[3], rt.at[3], partner),
        )

    def text_loads():
        cols, high, _ = text_sources()
        return (
            pltpu.make_async_copy(tk_in.at[:, cols], tkv.at[0], li.at[8]),
            pltpu.make_async_copy(tv_in.at[:, cols], tkv.at[1], li.at[9]),
            pltpu.make_async_copy(tq_in.at[high, cols], tqd.at[0], li.at[10]),
            pltpu.make_async_copy(tdo_in.at[high, cols], tqd.at[1], li.at[11]),
        )

    @pl.when(holds_text)
    def _():
        for copy in text_copies() + text_loads():
            copy.start()

    for load in loads[4:6]:
        load.wait()
    for t in range(seq):
        xst[t] = x_ref[:, t * wide : (t + 1) * wide]

    def column_send(t):
        return send(xst.at[t], xcol.at[s], s6.at[t], r6.at[s], (t, g))

    xlow = dot(x_ref[...], downw_ref[...], NT)
    xlow_out[...] = jnp.concatenate([xlow[0:hrows], xlow[hrows:rows]], axis=1).astype(BF)

    def low_send(h):
        return send(xlow_out, xlow_in.at[me], s7.at[h], r7.at[me], home(h))

    for i in range(heads):
        h = lax.rem(me + i, heads)

        @pl.when(me != home_peer(h))
        def _():
            low_send(h).start()

    for load in loads[6:8]:
        load.wait()

    def up_send(p):
        return send(
            up_out.at[c], up_all.at[mine, c], s9.at[p], r9.at[mine], peer(p)
        )

    def column_sends():
        for i in range(1, seq):
            column_send(lax.rem(s + i, seq)).start()
        xcol[pl.ds(s, 1)] = xst[pl.ds(s, 1)]

    @pl.when(jnp.logical_not(is_head))
    def _():
        column_sends()

    def up_trade():
        return send(up_in2.at[0, 1 - c], up_in2.at[1, 0], s8.at[0], r8.at[0], partner)

    def text_trade():
        return send(to, ti, s3.at[2], r3.at[2], partner)

    def back_query(p):
        return send(
            dqall.at[pl.ds(pl.multiple_of(p * rows, rows), rows)], ret.at[mine, pl.ds(0, rows)],
            s4.at[0, p], r4.at[0, mine], peer(p)
        )

    def back_send(k, p):
        at = pl.ds(k * rows, rows)
        return send(ost.at[p, at], ret.at[mine, at], s4.at[k, p], r4.at[k, mine], peer(p))

    def back_recv(k, h):
        at = pl.ds(k * rows, rows)
        return send(ost.at[0, at], ret.at[h, at], s4.at[k, 0], r4.at[k, h], partner)

    def trade(k):
        return send(xo.at[k], xi.at[k], s3.at[k], r3.at[k], partner)

    @pl.when(is_head)
    def _():
        recv[pl.ds(me, 1)] = stage[pl.ds(mine, 1)]
        xlow_in[pl.ds(me, 1)] = xlow_out[...].reshape(1, hrows, HEAD_SIZE)
        for i in range(1, peers):
            p = lax.rem(me + i, peers)
            first_recv(p, 0).wait_recv()

        swap = send(recv.at[:, pl.ds(0, 2 * rows)], kv2, s2.at[0], r2.at[0], partner)
        swap.start()
        step = step_ref[group_ref[time_ref[0]], mine]

        def dequant(codes):
            return (codes.reshape(image, HEAD_SIZE).astype(F32) * step).astype(BF)

        kall[0:image] = recv[:, 0:rows].reshape(image, HEAD_SIZE)
        vall[0:image] = dequant(recv[:, rows : 2 * rows])
        for i in range(1, peers):
            p = lax.rem(me + i, peers)
            first_recv(p, 1).wait_recv()

        column_sends()
        qall[0:image] = recv[:, 2 * rows : 3 * rows].reshape(image, HEAD_SIZE)
        doall[0:image] = recv[:, 3 * rows : 4 * rows].reshape(image, HEAD_SIZE)

        @pl.when(takes_text)
        def _():
            for copy in text_copies():
                copy.wait_recv()

        @pl.when(holds_text)
        def _():
            for copy in text_loads():
                copy.wait()

        kall[2 * image : 2 * image + text] = tkv[0]
        vall[2 * image : 2 * image + text] = tkv[1]
        qall[image : image + half] = tqd[0]
        doall[image : image + half] = tqd[1]
        swap.wait_recv()
        kall[image : 2 * image] = kv2[:, 0:rows].reshape(image, HEAD_SIZE)
        vall[image : 2 * image] = dequant(kv2[:, rows : 2 * rows])
        ktr[...] = kall[...].T

        def weights(index):
            at = slice(index * half, (index + 1) * half)
            queries, grads = qall[at], doall[at]
            scores = dot(kall[...], queries, NT)
            dprobs = dot(vall[...], grads, NT)
            top = jnp.max(scores, axis=0, keepdims=True) * (scale * math.log2(math.e))
            expo = jnp.exp2(scores * (scale * math.log2(math.e)) - top)
            probs = expo * (1.0 / jnp.sum(expo, axis=0, keepdims=True))
            value_part = dot(probs.astype(BF), grads)
            dvacc[...] = value_part if index == 0 else dvacc[...] + value_part
            return probs, dprobs

        def score_grads(probs, dprobs):
            deltas = jnp.sum(probs * dprobs, axis=0, keepdims=True)
            return (probs * (dprobs - deltas)).astype(BF)

        def key_query(index, dscores):
            at = slice(index * half, (index + 1) * half)
            key_part = dot(dscores, qall[at])
            dkacc[...] = key_part if index == 0 else dkacc[...] + key_part
            dqall[at] = (dot(ktr[...], dscores).T * scale).astype(BF)

        last = image // half
        for index in range(last):
            key_query(index, score_grads(*weights(index)))
        for i in range(1, peers):
            back_query(lax.rem(me + i, peers)).start()
        last_weights = weights(last)
        xo[1] = dvacc[image : 2 * image].astype(BF)
        trade(1).start()
        last_grads = score_grads(*last_weights)
        trade(1).wait_recv()
        ost[:, 2 * rows : 3 * rows] = (
            (dvacc[0:image] + xi[1].astype(F32)).astype(BF).reshape(peers, rows, HEAD_SIZE)
        )
        for i in range(1, peers):
            back_send(2, lax.rem(me + i, peers)).start()
        ret[pl.ds(mine, 1), 2 * rows : 3 * rows] = ost[pl.ds(me, 1), 2 * rows : 3 * rows]
        key_query(last, last_grads)
        xo[0] = (dkacc[image : 2 * image] * scale).astype(BF)
        trade(0).start()

        @pl.when(takes_text)
        def _():
            to[0:text] = (dkacc[2 * image : 2 * image + text] * scale).astype(BF)
            to[text : 2 * text] = dvacc[2 * image : 2 * image + text].astype(BF)
            to[2 * text : 2 * text + half] = dqall[image : image + half]
            text_trade().start()

        trade(0).wait_recv()
        ost[:, rows : 2 * rows] = (
            (dkacc[0:image] * scale + xi[0].astype(F32)).astype(BF).reshape(peers, rows, HEAD_SIZE)
        )
        for i in range(1, peers):
            back_send(1, lax.rem(me + i, peers)).start()
        ret[pl.ds(mine, 1), rows : 2 * rows] = ost[pl.ds(me, 1), rows : 2 * rows]
        ret[pl.ds(mine, 1), 0:rows] = dqall[pl.ds(pl.multiple_of(me * rows, rows), rows)].reshape(
            1, rows, HEAD_SIZE
        )

        for i in range(1, peers):
            p = lax.rem(me + i, peers)
            send(xlow_out, xlow_in.at[p], s7.at[0], r7.at[p], partner).wait_recv()

        codes = recv[:, rows : 2 * rows]
        kept = jnp.where(jnp.abs(codes.astype(F32)) < QMAX, ost[:, 2 * rows : 3 * rows].astype(F32), 0.0)
        kept = kept.astype(BF)
        low_rows = xlow_in[...].reshape(peers * hrows, HEAD_SIZE).T
        early = dot(low_rows, kept[:, 0:hrows].reshape(peers * hrows, HEAD_SIZE))
        late = dot(low_rows, kept[:, hrows:rows].reshape(peers * hrows, HEAD_SIZE))
        part_up = (early[0:rank] + late[rank : 2 * rank]).reshape(2, hrank, HEAD_SIZE)
        up_in2[0] = part_up
        up_trade().start()

    for h in range(heads):

        @pl.when(me != home_peer(h))
        def _():
            back_recv(2, h).wait_recv()

    sums = []
    for h in range(heads):
        cols = slice(h * HEAD_SIZE, (h + 1) * HEAD_SIZE)
        codes = code_ref[:, cols]
        inside = jnp.abs(codes) < QMAX
        value_grad = ret[h, 2 * rows : 3 * rows].astype(F32)
        kept = jnp.where(inside, value_grad, 0.0).astype(BF)
        lsq_term = jnp.where(inside, -frac_ref[:, cols].astype(F32), codes.astype(F32))
        sums.append(jnp.sum(value_grad * lsq_term, axis=0, keepdims=True))
        dv_ref[:, cols] = kept

    low = dot(dv_ref[...], upw_ref[...], NT)
    sums.append(jnp.zeros((rows - heads, HEAD_SIZE), F32))
    step_terms = jnp.sum(jnp.concatenate(sums, axis=0), axis=1, keepdims=True)
    step_high = step_terms.astype(BF).astype(F32)
    lane_at = lax.broadcasted_iota(jnp.int32, (rows, rank), 1)
    beside = jnp.where(lane_at == 0, step_high, jnp.where(lane_at == 1, step_terms - step_high, 0.0))
    low_out[...] = jnp.concatenate([low, beside], axis=1).astype(BF)

    def tile_send(t):
        return send(low_out, low_in.at[s], s10.at[t], r10.at[s], (t, g))

    for i in range(1, seq):
        tile_send(lax.rem(s + i, seq)).start()
    low_in[pl.ds(s, 1)] = low_out[...].reshape(1, rows, HEAD_SIZE)

    @pl.when(is_head)
    def _():
        @pl.when(holds_text)
        def _():
            text_trade().wait_recv()
            full = (seq, share, HEAD_SIZE)
            tfin[0 : seq // 2, 0] = dqall[image : image + half].reshape(seq // 2, share, HEAD_SIZE)
            tfin[seq // 2 : seq, 0] = ti[2 * text : 2 * text + half].reshape(seq // 2, share, HEAD_SIZE)
            tfin[:, 1] = (
                (dkacc[2 * image : 2 * image + text] * scale + ti[0:text].astype(F32)).astype(BF).reshape(full)
            )
            tfin[:, 2] = (
                (dvacc[2 * image : 2 * image + text] + ti[text : 2 * text].astype(F32)).astype(BF).reshape(full)
            )
            for i in range(1, seq):
                other = lax.rem(s + i, seq)
                send(
                    tfin.at[other], rett.at[lane_block], s5.at[other], r5.at[lane_block], (other, g)
                ).start()

            rett[pl.ds(lane_block, 1)] = tfin[pl.ds(s, 1)]

        up_trade().wait_recv()
        up_out[pl.ds(c, 1)] = (
            (up_in2[pl.ds(0, 1), pl.ds(c, 1)] + up_in2[pl.ds(1, 1), pl.ds(0, 1)]) * unscale
        ).astype(BF).reshape(1, hrank, HEAD_SIZE)
        for i in range(1, peers):
            up_send(lax.rem(me + i, peers)).start()
        up_all[pl.ds(mine, 1), pl.ds(c, 1)] = up_out[pl.ds(c, 1)].reshape(1, 1, hrank, HEAD_SIZE)

    for i in range(1, seq):
        t = lax.rem(s + i, seq)
        send(xst.at[0], xcol.at[t], s6.at[0], r6.at[t], partner).wait_recv()
        send(low_out, low_in.at[t], s10.at[0], r10.at[t], partner).wait_recv()

    tiles = low_in[...]
    flat = tiles.reshape(seq * rows, HEAD_SIZE).T
    block = dot(flat, xcol[...].reshape(seq * rows, wide))[0:rank]
    step_group = jnp.sum(tiles[:, 0:16].astype(F32), axis=0)
    red_out[...] = block.astype(BF).reshape(head, part, wide)
    sum_out[...] = step_group

    def reduce_send(other):
        return send(red_out.at[other], red_in.at[g], s11.at[0, other], r11.at[0, g], (s, other))

    def sum_send(other):
        return send(sum_out, sum_in.at[g], s11.at[1, other], r11.at[1, g], (s, other))

    for i in range(1, head):
        reduce_send(lax.rem(g + i, head)).start()
    for i in range(1, head):
        sum_send(lax.rem(g + i, head)).start()
    red_in[pl.ds(g, 1)] = red_out[pl.ds(g, 1)]
    sum_in[pl.ds(g, 1)] = step_group.reshape(1, 16, HEAD_SIZE)

    for i in range(1, head):
        other = lax.rem(g + i, head)
        send(red_out.at[0], red_in.at[other], s11.at[0, 0], r11.at[0, other], partner).wait_recv()

    summed = jnp.sum(red_in[...].astype(F32), axis=0) * unscale
    gath[pl.ds(y, 1), pl.ds(c, 1), pl.ds(s, 1)] = summed.astype(BF).reshape(1, 1, 1, part, wide)

    def row_send(p):
        return send(gath.at[y, c, s], gath.at[y, c, s], s12.at[p], r12.at[me], peer(p))

    def core_send():
        return send(gath.at[:, c], gath.at[:, c], s12.at[peers], r12.at[peers], partner)

    def core_up_send():
        return send(up_all.at[:, c], up_all.at[:, c], s8.at[1], r8.at[1], partner)

    for i in range(1, peers):
        row_send(lax.rem(me + i, peers)).start()

    for j in range(group):

        @pl.when(s != first + c * group + j)
        def _():
            send(tfin.at[0], rett.at[j], s5.at[0], r5.at[j], partner).wait_recv()

        cols = slice(j * HEAD_SIZE, (j + 1) * HEAD_SIZE)
        dqt_ref[:, cols] = rett[j, 0]
        dkt_ref[:, cols] = rett[j, 1]
        dvt_ref[:, cols] = rett[j, 2]

    for h in range(heads):

        @pl.when(me != home_peer(h))
        def _():
            back_recv(0, h).wait_recv()
            back_recv(1, h).wait_recv()

    for h in range(heads):
        cols = slice(h * HEAD_SIZE, (h + 1) * HEAD_SIZE)
        dq_ref[:, cols] = ret[h, 0:rows]
        dk_ref[:, cols] = ret[h, rows : 2 * rows]

    slot_index = group_ref[time_ref[0]]
    for i in range(1, head):
        other = lax.rem(g + i, head)
        send(sum_out, sum_in.at[other], s11.at[1, 0], r11.at[1, other], partner).wait_recv()

    lanes = jnp.sum(sum_in[...], axis=0)
    lane_at = lax.broadcasted_iota(jnp.int32, (16, HEAD_SIZE), 1)
    row_at = lax.broadcasted_iota(jnp.int32, (16, HEAD_SIZE), 0)
    chosen = jnp.logical_or(lane_at == rank, lane_at == rank + 1)
    head_sums = jnp.sum(jnp.where(chosen, lanes, 0.0), axis=1, keepdims=True)
    step_row = jnp.sum(jnp.where(lane_at == row_at, head_sums, 0.0), axis=0, keepdims=True)[:, 0:heads]
    step_row = step_row * (QMAX ** (-0.5) * unscale)
    slots = steps_ref.shape[0]
    slot_at = lax.broadcasted_iota(jnp.int32, (slots, heads), 0)
    steps_ref[...] = jnp.where(slot_at == slot_index, jnp.broadcast_to(step_row, (slots, heads)), 0.0)

    for h in range(heads):

        @pl.when(me != home_peer(h))
        def _():
            send(up_out.at[0], up_all.at[h, c], s9.at[0], r9.at[h], partner).wait_recv()

    core_up_send().start()

    for i in range(1, peers):
        p = lax.rem(me + i, peers)
        block_at = gath.at[lax.rem(p, planes), c, p // planes]
        send(block_at, block_at, s12.at[0], r12.at[p], partner).wait_recv()

    core_send().start()
    send(up_all.at[:, 1 - c], up_all.at[:, 1 - c], s8.at[1], r8.at[1], partner).wait_recv()
    for h in range(heads):
        cols = slice(h * HEAD_SIZE, (h + 1) * HEAD_SIZE)
        up_ref[:, cols] = up_all[h].reshape(rank, HEAD_SIZE).astype(F32)
    send(gath.at[:, 1 - c], gath.at[:, 1 - c], s12.at[peers], r12.at[peers], partner).wait_recv()
    for t in range(seq):
        down_ref[:, t * wide : (t + 1) * wide] = gath[:, :, t].reshape(rank, wide).astype(F32)

    for h in range(heads):

        @pl.when(me != home_peer(h))
        def _():
            first_send(h, 0).wait_send()
            first_send(h, 1).wait_send()
            low_send(h).wait_send()

    for i in range(1, seq):
        t = lax.rem(s + i, seq)
        column_send(t).wait_send()
        tile_send(t).wait_send()
    for i in range(1, head):
        reduce_send(lax.rem(g + i, head)).wait_send()
        sum_send(lax.rem(g + i, head)).wait_send()
    for i in range(1, peers):
        row_send(lax.rem(me + i, peers)).wait_send()
    core_send().wait_send()
    core_up_send().wait_send()

    @pl.when(is_head)
    def _():
        send(recv.at[:, pl.ds(0, 2 * rows)], kv2, s2.at[0], r2.at[0], partner).wait_send()
        trade(0).wait_send()
        trade(1).wait_send()
        up_trade().wait_send()
        for i in range(1, peers):
            p = lax.rem(me + i, peers)
            back_query(p).wait_send()
            back_send(1, p).wait_send()
            back_send(2, p).wait_send()
            up_send(p).wait_send()

    @pl.when(takes_text)
    def _():
        text_trade().wait_send()

    @pl.when(holds_text)
    def _():
        for copy in text_copies():
            copy.wait_send()
        for i in range(1, seq):
            other = lax.rem(s + i, seq)
            send(
                tfin.at[other], rett.at[lane_block], s5.at[other], r5.at[lane_block], (other, g)
            ).wait_send()


def settle_kernel(count, *refs):
    sources, targets, held = refs[:count], refs[count : 2 * count], refs[2 * count : 3 * count]
    came, went = refs[3 * count :]
    loads = [pltpu.make_async_copy(a, b, came.at[i]) for i, (a, b) in enumerate(zip(sources, held))]
    stores = [pltpu.make_async_copy(a, b, went.at[i]) for i, (a, b) in enumerate(zip(held, targets))]
    for load in loads:
        load.start()
    for load, store in zip(loads, stores):
        load.wait()
        store.start()
    for store in stores:
        store.wait()


def settle(arrays):
    count = len(arrays)
    anywhere = pl.BlockSpec(memory_space=pl.ANY)
    return pl.pallas_call(
        functools.partial(settle_kernel, count),
        out_shape=[jax.ShapeDtypeStruct(a.shape, a.dtype) for a in arrays],
        in_specs=[anywhere] * count,
        out_specs=[anywhere] * count,
        scratch_shapes=[pltpu.VMEM(a.shape, a.dtype) for a in arrays]
        + [pltpu.SemaphoreType.DMA((count,))] * 2,
        compiler_params=pltpu.CompilerParams(vmem_limit_bytes=56 * 1024 * 1024),
        name="settle",
    )(*arrays)


def whole_heads(
    seq,
    head,
    image_input_rows,
    adapter_down_weight,
    adapter_up_weight,
    image_query_rows,
    image_key_rows,
    image_value_codes,
    value_fraction,
    value_step_sizes,
    timestep_group,
    timestep,
    image_output_grad,
    text_query_rows,
    text_key_rows,
    text_value_rows,
    text_output_grad,
):
    rows, width = image_query_rows.shape
    text, text_width = text_query_rows.shape
    heads, group = width // HEAD_SIZE, text_width // HEAD_SIZE
    peers = seq * head // 2
    image, share = peers * rows, text // seq
    keys = 2 * image + text
    rank, wide = adapter_up_weight.shape[0], image_input_rows.shape[1] // seq
    planes = head // 2
    vmem = pl.BlockSpec(memory_space=pltpu.VMEM)
    sems = pltpu.SemaphoreType.DMA
    hbm = pl.BlockSpec(memory_space=pl.ANY)
    smem = pl.BlockSpec(memory_space=pltpu.SMEM)
    results = pl.pallas_call(
        functools.partial(attention_kernel, seq, head),
        out_shape=[jax.ShapeDtypeStruct((rows, width), BF)] * 3
        + [jax.ShapeDtypeStruct((share, text_width), BF)] * 3
        + [
            jax.ShapeDtypeStruct(adapter_down_weight.shape[::-1], F32),
            jax.ShapeDtypeStruct(adapter_up_weight.shape, F32),
            jax.ShapeDtypeStruct(value_step_sizes.shape, F32),
        ],
        in_specs=[hbm] * 12 + [smem] * 3,
        out_specs=[vmem] * 9,
        scratch_shapes=[
            pltpu.VMEM((rows, width), BF),
            pltpu.VMEM((rows, width), BF),
            pltpu.VMEM((rows, width), jnp.int32),
            pltpu.VMEM((rows, width), BF),
            pltpu.VMEM(image_input_rows.shape, BF),
            pltpu.VMEM((rows, width), BF),
            pltpu.VMEM(adapter_up_weight.shape, BF),
            pltpu.VMEM(adapter_down_weight.shape[::-1], BF),
            pltpu.VMEM((heads, 4 * rows, HEAD_SIZE), BF),
            pltpu.VMEM((peers, 4 * rows, HEAD_SIZE), BF),
            pltpu.VMEM((peers, 2 * rows, HEAD_SIZE), BF),
            pltpu.VMEM((2, text, HEAD_SIZE), BF),
            pltpu.VMEM((2, text // 2, HEAD_SIZE), BF),
            pltpu.VMEM((keys, HEAD_SIZE), BF),
            pltpu.VMEM((HEAD_SIZE, keys), BF),
            pltpu.VMEM((keys, HEAD_SIZE), BF),
            pltpu.VMEM((image + text // 2, HEAD_SIZE), BF),
            pltpu.VMEM((image + text // 2, HEAD_SIZE), BF),
            pltpu.VMEM((image + text // 2, HEAD_SIZE), BF),
            pltpu.VMEM((keys, HEAD_SIZE), F32),
            pltpu.VMEM((keys, HEAD_SIZE), F32),
            pltpu.VMEM((2, image, HEAD_SIZE), BF),
            pltpu.VMEM((2, image, HEAD_SIZE), BF),
            pltpu.VMEM((2 * text + text // 2, HEAD_SIZE), BF),
            pltpu.VMEM((2 * text + text // 2, HEAD_SIZE), BF),
            pltpu.VMEM((peers, 3 * rows, HEAD_SIZE), BF),
            pltpu.VMEM((heads, 3 * rows, HEAD_SIZE), BF),
            pltpu.VMEM((seq, 3, share, HEAD_SIZE), BF),
            pltpu.VMEM((group, 3, share, HEAD_SIZE), BF),
            pltpu.VMEM((rows // 2, HEAD_SIZE), BF),
            pltpu.VMEM((peers, rows // 2, HEAD_SIZE), BF),
            pltpu.VMEM((seq, rows, wide), BF),
            pltpu.VMEM((seq, rows, wide), BF),
            pltpu.VMEM((2, rank // 2, HEAD_SIZE), BF),
            pltpu.VMEM((2, 2, rank // 2, HEAD_SIZE), F32),
            pltpu.VMEM((heads, 2, rank // 2, HEAD_SIZE), BF),
            pltpu.VMEM((rows, HEAD_SIZE), BF),
            pltpu.VMEM((seq, rows, HEAD_SIZE), BF),
            pltpu.VMEM((head, rank // head, wide), BF),
            pltpu.VMEM((head, rank // head, wide), BF),
            pltpu.VMEM((16, HEAD_SIZE), F32),
            pltpu.VMEM((head, 16, HEAD_SIZE), F32),
            pltpu.VMEM((planes, 2, seq, rank // head, wide), BF),
            sems((12,)),
            sems((2, heads)),
            sems((2, peers)),
            sems((1,)),
            sems((1,)),
            sems((4,)),
            sems((4,)),
            sems((3,)),
            sems((3,)),
            sems((3, peers)),
            sems((3, heads)),
            sems((seq,)),
            sems((group,)),
            sems((seq,)),
            sems((seq,)),
            sems((heads,)),
            sems((peers,)),
            sems((2,)),
            sems((2,)),
            sems((peers,)),
            sems((heads,)),
            sems((seq,)),
            sems((seq,)),
            sems((2, head)),
            sems((2, head)),
            sems((peers + 1,)),
            sems((peers + 1,)),
        ],
        compiler_params=pltpu.CompilerParams(
            collective_id=0, has_side_effects=True, vmem_limit_bytes=56 * 1024 * 1024
        ),
        name="whole_heads",
    )(
        image_query_rows,
        image_key_rows,
        image_value_codes,
        image_output_grad,
        text_query_rows,
        text_key_rows,
        text_value_rows,
        text_output_grad,
        image_input_rows,
        value_fraction,
        adapter_up_weight,
        adapter_down_weight.T,
        value_step_sizes,
        timestep_group,
        timestep,
    )
    results = settle(results)
    return (*results[:6], results[6].T, *results[7:])


def pick(mesh):
    seq, head = mesh.shape["seq"], mesh.shape["head"]

    def chosen(*arguments):
        rows, width = arguments[3].shape
        text, text_width = arguments[11].shape
        pair = 2 * text_width // HEAD_SIZE
        fits = (
            head % 2 == 0
            and seq % 2 == 0
            and seq >= pair
            and rows % 32 == 0
            and 2 * arguments[2].shape[0] == HEAD_SIZE
            and width // HEAD_SIZE <= 16
            and (text // 2) % rows == 0
            and (seq * head // 2 * rows) % (text // 2) == 0
            and arguments[2].shape[0] % (16 * head) == 0
            and arguments[0].shape[1] % (seq * HEAD_SIZE) == 0
            and text % (seq * 16) == 0
            and (seq * head // 2 * rows) % (text // 2) == 0
            and (seq * head * rows + text) * HEAD_SIZE <= 1 << 18
        )
        if fits:
            return whole_heads(seq, head, *arguments)
        return on_device(*arguments)

    return chosen


def solution(mesh):
    placed = (
        P(("seq", "head"), None),
        P(),
        P(),
        P(("seq", "head"), None),
        P(("seq", "head"), None),
        P(("seq", "head"), None),
        P(("seq", "head"), None),
        P(),
        P(),
        P(),
        P(("seq", "head"), None),
        P(None, "head"),
        P(None, "head"),
        P(None, "head"),
        P(None, "head"),
    )
    return jax.shard_map(
        pick(mesh),
        mesh=mesh,
        in_specs=placed,
        out_specs=(
            P(("seq", "head"), None),
            P(("seq", "head"), None),
            P(("seq", "head"), None),
            P("seq", "head"),
            P("seq", "head"),
            P("seq", "head"),
            P(),
            P(),
            P(),
        ),
        check_vma=False,
    )
```
